32 devices in a mesh: gx: 4 (over y, x), gy: 4 (over z), gz: 2 (over core).
Axes of the slice: x: 2, y: 2, z: 4, core: 2. Of those that a mesh axis runs over, the one named last changes fastest.
Arguments:
- positions: float32 [8, 8, 2, 192], P('gx', 'gy', 'gz'), may hold values from 0 to 1
- species: int32 [8, 8, 2, 64], P('gx', 'gy', 'gz'), may hold values from 0 to 88
- counts: int32 [8, 8, 2], P('gx', 'gy', 'gz'), may hold values from 1 to 64, as said below
- embed: bfloat16 [89, 128], replicated, may hold values from -6 to 6
- filters: bfloat16 [128, 512], replicated, may hold values from -0.5 to 0.5
- w_up: bfloat16 [128, 128], replicated, may hold values from -0.5 to 0.5
- w_energy: float32 [128], replicated, may hold values from -0.5 to 0.5
Outputs:
- energies: float32 [8, 8, 2, 64], P('gx', 'gy', 'gz')
- forces: float32 [8, 8, 2, 192], P('gx', 'gy', 'gz')
The draws below stay inside these ranges and needn't reach their ends.
Inputs may be any that keep to these rules, and one draw needn't show every extreme that they name: `counts`: at most 64 atoms a cell; some cell holds exactly 64 and some exactly 1.
All inputs are finite; a program needn't handle non-finite values.
Results may differ from the reference program's by a relative error of at most 0.0038.
Values may be sent and summed in bfloat16 or wider, within the bound.
No kernel may reach another device: no remote copies, remote signals or barrier semaphores. Data moves between devices by JAX's collectives and lax.ppermute only.
A program may use at most 64 MiB of HBM per device.

```python
import jax
import jax.numpy as jnp
from jax import lax

CH = 128
RAD = 4
NSPEC = 89
SLOTS = 64
BX = 8
BY = 8
BZ = 2


def draw_counts(key, part):
    counts = jax.random.randint(key, (BX, BY, BZ), 1, SLOTS + 1)
    counts = counts.at[0, 0, 0].set(SLOTS)
    counts = counts.at[0, 0, 1].set(1)
    return counts.astype(jnp.int32)


def plant(values, rng, least, largest):
    spot = [jax.random.randint(jax.random.fold_in(rng, axis), (), 0, length) for axis, length in enumerate(values.shape)]
    longest = values.shape.index(max(values.shape))
    neighbour = spot[:longest] + [(spot[longest] + 1) % values.shape[longest]] + spot[longest + 1:]
    return values.at[tuple(spot)].set(least).at[tuple(neighbour)].set(largest)


def shard_levels(rng, dims, cuts, least, top_value):
    gain, own = 1.0, jax.random.fold_in(rng, 6)
    for position, shards_of in cuts:
        draws = jnp.exp(jax.random.uniform(jax.random.fold_in(own, position), (shards_of,), jnp.float32, least / len(cuts), top_value / len(cuts)))
        gain = gain * jnp.repeat(draws, dims[position] // shards_of).reshape([-1 if axis == position else 1 for axis in range(len(dims))])
    return gain


def gaussian(key, shape, scale, bound, kind=jnp.bfloat16):
    values = scale * jax.random.normal(key, shape, jnp.float32)
    return jnp.clip(values, min=-bound, max=bound).astype(kind)


def setup_inputs(seed: int = 0) -> dict:
    key_list = jax.random.split(jax.random.key(seed), 8)
    positions = jnp.clip(1.0 * jax.random.uniform(key_list[0], (BX, BY, BZ, 3 * SLOTS), jnp.float32) ** shard_levels(key_list[0], (BX, BY, BZ, 3 * SLOTS), ((0, 4), (1, 4), (2, 2)), -0.2, 0.2), 0.0, 1.0)
    species = plant(jax.random.randint(key_list[1], (BX, BY, BZ, SLOTS), 0, NSPEC), jax.random.fold_in(key_list[1], 1), 0, NSPEC - 1).astype(jnp.int32)
    counts = draw_counts(jax.random.fold_in(key_list[7], 71), 0)
    embed = gaussian(key_list[3], (NSPEC, CH), 1.0, 6.0)
    filters = gaussian(key_list[4], (CH, RAD * CH), CH ** -0.5, 0.5)
    w_up = gaussian(key_list[5], (CH, CH), CH ** -0.5, 0.5)
    w_energy = gaussian(key_list[6], (CH,), CH ** -0.5, 0.5, jnp.float32)
    return dict(positions=positions, species=species, counts=counts, embed=embed, filters=filters, w_up=w_up, w_energy=w_energy)


MSG_SCALE = 0.1


def rounded(values):
    return lax.optimization_barrier(values.astype(jnp.bfloat16)).astype(jnp.float32)


def radial(dist_sq, radial_count):
    decay_rates = 0.5 * 3.0 ** jnp.arange(radial_count).astype(jnp.float32)
    falloff = jnp.maximum(1.0 - dist_sq, 0.0)[..., None]
    decaying = jnp.exp(-decay_rates * dist_sq[..., None])
    return decaying * falloff * falloff, -decaying * (decay_rates * falloff * falloff + 2.0 * falloff)


def geometry(anchor_pos, target_pos, offset):
    slot_count = anchor_pos.shape[-1] // 3
    leading = anchor_pos.shape[:-1]
    anchor = anchor_pos.reshape(leading + (3, slot_count))
    target = target_pos.reshape(leading + (3, slot_count))
    shift_vec = jnp.array(offset, jnp.float32).reshape((3, 1, 1))
    displace = target[..., :, None, :] - anchor[..., :, :, None] + shift_vec
    return displace, jnp.sum(displace * displace, axis=-3)


def window(padded, offset, cell_shape):
    return padded[1 + offset[0]:1 + offset[0] + cell_shape[0], 1 + offset[1]:1 + offset[1] + cell_shape[1], 1 + offset[2]:1 + offset[2] + cell_shape[2]]


def all_offsets():
    return [(first, second, third) for first in (-1, 0, 1) for second in (-1, 0, 1) for third in (-1, 0, 1)]


def slab_messages(pos_slab, feat_slab, cell_shape, slot_count, radial_count, feature_width):
    anchor_pos = window(pos_slab, (0, 0, 0), cell_shape)
    diagonal = jnp.eye(slot_count, dtype=jnp.float32)[..., None]
    message = jnp.zeros(cell_shape + (slot_count, feature_width), jnp.float32)
    for offset in all_offsets():
        target_pos = window(pos_slab, offset, cell_shape)
        target_feat = window(feat_slab, offset, cell_shape).reshape(cell_shape + (slot_count * radial_count, feature_width))
        displace, dist_sq = geometry(anchor_pos, target_pos, offset)
        radial_vals = radial(dist_sq, radial_count)[0]
        if offset == (0, 0, 0):
            radial_vals = radial_vals * (1.0 - diagonal)
        weights = rounded(radial_vals.reshape(cell_shape + (slot_count, slot_count * radial_count)))
        message = message + jnp.einsum("abcip,abcpd->abcid", weights, target_feat.astype(jnp.float32))
    return MSG_SCALE * message


def slab_forces(pos_slab, feat_slab, adj_slab, cell_shape, slot_count, radial_count, feature_width):
    anchor_pos = window(pos_slab, (0, 0, 0), cell_shape)
    anchor_adj = window(adj_slab, (0, 0, 0), cell_shape).astype(jnp.float32)
    anchor_feat = window(feat_slab, (0, 0, 0), cell_shape).reshape(cell_shape + (slot_count * radial_count, feature_width)).astype(jnp.float32)
    forces = jnp.zeros(cell_shape + (3, slot_count), jnp.float32)
    for offset in all_offsets():
        target_pos = window(pos_slab, offset, cell_shape)
        target_feat = window(feat_slab, offset, cell_shape).reshape(cell_shape + (slot_count * radial_count, feature_width)).astype(jnp.float32)
        target_adj = window(adj_slab, offset, cell_shape).astype(jnp.float32)
        displace, dist_sq = geometry(anchor_pos, target_pos, offset)
        radial_slope = radial(dist_sq, radial_count)[1]
        outward = jnp.einsum("abcid,abcpd->abcip", anchor_adj, target_feat).reshape(cell_shape + (slot_count, slot_count, radial_count))
        inward = jnp.einsum("abcjd,abcpd->abcjp", target_adj, anchor_feat).reshape(cell_shape + (slot_count, slot_count, radial_count))
        inward = jnp.swapaxes(inward, -3, -2)
        pair_weight = MSG_SCALE * jnp.sum(radial_slope * (outward + inward), axis=-1)
        forces = forces + 2.0 * jnp.sum(displace * pair_weight[..., None, :, :], axis=-1)
    return forces


def periodic(values):
    return jnp.pad(values, ((1, 1), (1, 1), (1, 1)) + ((0, 0),) * (values.ndim - 3), mode="wrap")


def reference(positions, species, counts, embed, filters, w_up, w_energy):
    slot_count = species.shape[-1]
    feature_width = embed.shape[1]
    radial_count = filters.shape[1] // feature_width
    occupied = (jnp.arange(slot_count, dtype=jnp.int32) < counts[..., None]).astype(jnp.float32)
    embedded = (embed[species].astype(jnp.float32) * occupied[..., None]).astype(jnp.bfloat16)

    def project_plane(plane):
        return jnp.einsum("bcsd,de->bcse", plane.astype(jnp.float32), filters.astype(jnp.float32)).astype(jnp.bfloat16)

    projected = lax.map(project_plane, embedded)
    pos_pad = periodic(positions)
    feat_pad = periodic(projected)
    plane_shape = (1,) + positions.shape[1:3]

    def messages_at(row):
        pos_slab = lax.dynamic_slice_in_dim(pos_pad, row, 3, 0)
        feat_slab = lax.dynamic_slice_in_dim(feat_pad, row, 3, 0)
        return slab_messages(pos_slab, feat_slab, plane_shape, slot_count, radial_count, feature_width)[0]

    rows = jnp.arange(positions.shape[0], dtype=jnp.int32)
    message = lax.map(messages_at, rows)
    sigmoid_msg = jax.nn.sigmoid(message)
    activated = rounded(message * sigmoid_msg)
    hidden = embedded.astype(jnp.float32) + jnp.einsum("xyzsd,de->xyzse", activated, w_up.astype(jnp.float32))
    energies = occupied * jnp.sum(hidden * w_energy, axis=-1)
    readout = jnp.sum(w_up.astype(jnp.float32) * w_energy[None, :], axis=1)
    adjoint = (occupied[..., None] * sigmoid_msg * (1.0 + message * (1.0 - sigmoid_msg)) * readout).astype(jnp.bfloat16)
    adj_pad = periodic(adjoint)

    def forces_at(row):
        pos_slab = lax.dynamic_slice_in_dim(pos_pad, row, 3, 0)
        feat_slab = lax.dynamic_slice_in_dim(feat_pad, row, 3, 0)
        adj_slab = lax.dynamic_slice_in_dim(adj_pad, row, 3, 0)
        return slab_forces(pos_slab, feat_slab, adj_slab, plane_shape, slot_count, radial_count, feature_width)[0]

    forces = lax.map(forces_at, rows)
    forces = (forces * occupied[..., None, :]).reshape(positions.shape)
    return energies, forces
```

```python
import functools

import jax
import jax.numpy as jnp
from jax import lax
from jax.experimental import pallas as pl
from jax.experimental.pallas import tpu as pltpu
from jax.sharding import PartitionSpec as P

MSG_SCALE = 0.1
HALO = 2
LANES = 128
NT = (((1,), (1,)), ((), ()))
NN = (((1,), (0,)), ((), ()))


def exchange(block, axis, dim, width):
    count = lax.axis_size(axis)
    first = lax.slice_in_dim(block, 0, width, axis=dim)
    last = lax.slice_in_dim(block, block.shape[dim] - width, None, axis=dim)
    if count % 2 == 0:
        odd = lax.axis_index(axis) % 2 == 1
        whole = block.shape[dim] == width
        up = block if whole else jnp.where(odd, last, first)
        down = block if whole else jnp.where(odd, first, last)
        far = [(i, (i + 1) % count if i % 2 else (i - 1) % count) for i in range(count)]
        near = [(i, i - 1 if i % 2 else i + 1) for i in range(count)]
        from_far = lax.ppermute(up, axis, far)
        from_near = lax.ppermute(down, axis, near)
        low = jnp.where(odd, from_near, from_far)
        high = jnp.where(odd, from_far, from_near)
    else:
        forward = [(i, (i + 1) % count) for i in range(count)]
        low = lax.ppermute(last, axis, forward)
        high = lax.ppermute(first, axis, [(b, a) for a, b in forward])
    return jnp.concatenate([low, block, high], axis=dim)


def dot(a, b, dims, precision=None):
    return lax.dot_general(a, b, dims, precision=precision, preferred_element_type=jnp.float32)


def split(values):
    high = values.astype(jnp.bfloat16)
    return high, (values - high.astype(jnp.float32)).astype(jnp.bfloat16)


def kernel(
    cells, merged, rad,
    region, zrow_ref, embed, filters, w_up, w_energy,
    energies, own, other,
    emb_pad, table, onehot, stage, anchors, adj_table, act,
):
    nax, nay = cells[0] + 2, cells[1] + 2
    groups = region.shape[2] // 4
    slots = energies.shape[-1]
    nspec, width = embed.shape
    spec = emb_pad.shape[0]
    neighbours = [(dx, dy) for dx in (-1, 0, 1) for dy in (-1, 0, 1)]
    bf = jnp.bfloat16

    emb_pad[...] = jnp.zeros_like(emb_pad)
    emb_pad[0:nspec, :] = embed[...].astype(jnp.float32)
    emb = emb_pad[...]
    rows = dot(emb.astype(bf), filters[...], NN).astype(bf)
    for k in range(rad):
        table[k * spec:(k + 1) * spec, :] = rows[:, k * width:(k + 1) * width]
    energy_row = jnp.broadcast_to(w_energy[...], (8, width))
    readout = dot(energy_row, w_up[...].astype(jnp.float32), NT, lax.Precision.HIGHEST)
    emb_energy = dot(energy_row, emb, NT, lax.Precision.HIGHEST)

    ids = lax.broadcasted_iota(jnp.int32, (spec, LANES), 0).astype(jnp.float32)
    for x in range(region.shape[0]):
        for y in range(region.shape[1]):
            for g in range(groups):
                marked = region[x, y, g * 4 + 3:g * 4 + 4, :]
                onehot[(x * region.shape[1] + y) * groups + g] = (marked == ids).astype(bf)

    for q in range(4):
        for x in range(nax):
            stage[q, x * nay:(x + 1) * nay, :] = region[1 + x, 1:1 + nay, q, :]
        columns = stage[q].T
        for a in range(nax * nay):
            anchors[a, q] = jnp.broadcast_to(columns[0:slots, a:a + 1], (slots, LANES))

    def target(x, y, g, shift):
        row = region[x, y, g * 4:g * 4 + 3, :]
        return row[0:1] + shift[0], row[1:2] + shift[1], row[2:3]

    def z_image(dz, g):
        shift = zrow_ref[g:g + 1, :]
        if merged:
            return jnp.where(dz > 0.0, dz - shift, dz + shift)
        return dz + shift

    def onehot_at(x, y, g):
        return onehot[(x * region.shape[1] + y) * groups + g]

    step = 16
    chunks = [slice(r, r + step) for r in range(0, slots, step)]
    diagonal = lax.broadcasted_iota(jnp.int32, (slots, LANES), 0) == lax.broadcasted_iota(
        jnp.int32, (slots, LANES), 1
    )

    def message_at(a, carry):
        ax, ay = a // nay, a % nay
        parts = []
        for dx, dy in neighbours:
            for g in range(groups):
                tx, ty, tz = target(ax + 1 + dx, ay + 1 + dy, g, (dx, dy))
                weights = [[] for _ in range(rad)]
                for c in chunks:
                    ex = tx - anchors[a, 0, c, :]
                    ey = ty - anchors[a, 1, c, :]
                    dz = tz - anchors[a, 2, c, :]
                    if merged:
                        ez = jnp.abs(dz) - zrow_ref[g:g + 1, :]
                    else:
                        ez = dz + zrow_ref[g:g + 1, :]
                    s = ex * ex + ey * ey + ez * ez
                    f = jnp.maximum(1.0 - s, 0.0)
                    e = jnp.exp(-0.5 * s)
                    w = e * (f * f)
                    if dx == 0 and dy == 0 and g == 0:
                        w = jnp.where(diagonal[c], 0.0, w)
                    e = e * e
                    for k in range(rad):
                        if k == 1:
                            w = w * e
                        elif k > 1:
                            e = e * e * e
                            w = w * e
                        weights[k].append(w.astype(bf))
                parts.append(jnp.concatenate([jnp.concatenate(w, axis=0) for w in weights], axis=0))
        hots = [
            onehot_at(ax + 1 + dx, ay + 1 + dy, g) for dx, dy in neighbours for g in range(groups)
        ]
        sums = dot(jnp.concatenate(parts, axis=1), jnp.concatenate(hots, axis=1), NT)
        by_filter = jnp.concatenate([sums[k * slots:(k + 1) * slots] for k in range(rad)], axis=1)
        halves = dot(jnp.concatenate(split(by_filter), axis=0), table[...], NN)
        message = MSG_SCALE * (halves[0:slots] + halves[slots:])
        sigmoid = 1.0 / (1.0 + jnp.exp(-message))
        act[a] = (message * sigmoid).astype(bf)
        slope = sigmoid * (1.0 + message * (1.0 - sigmoid)) * readout[0:1]
        adjoint = jnp.where(anchors[a, 3] >= 0.0, slope, 0.0).astype(bf)
        high, low = split(dot(adjoint, table[...], NT))
        for k in range(rad):
            at = slice(k * slots, (k + 1) * slots)
            adj_table[a, at, 0:spec] = high[:, k * spec:(k + 1) * spec]
            adj_table[a, at, spec:] = low[:, k * spec:(k + 1) * spec]
        return carry

    lax.fori_loop(0, nax * nay, message_at, 0)

    def pairs(a, x, y, g, shift, gains, c):
        tx, ty, tz = target(x, y, g, shift)
        ex = tx - anchors[a, 0, c, :]
        ey = ty - anchors[a, 1, c, :]
        ez = z_image(tz - anchors[a, 2, c, :], g)
        s = ex * ex + ey * ey + ez * ez
        f = jnp.maximum(1.0 - s, 0.0)
        e = jnp.exp(-0.5 * s)
        total = None
        for k in range(rad):
            if k == 1:
                e = e * e * e
            elif k > 1:
                e = e * e * e
            gain = gains[k * slots + c.start:k * slots + c.stop, :]
            term = (e * gain) * (0.5 * 3.0 ** k * f + 2.0)
            total = term if total is None else total + term
        return total * f, (ex, ey, ez)

    scale = -2.0 * MSG_SCALE

    def both(hot):
        return jnp.concatenate([hot, hot], axis=0)

    def forces_at(o, carry):
        ox, oy = o // cells[1], o % cells[1]
        a = (ox + 1) * nay + oy + 1
        sums = [[None] * len(chunks) for _ in range(3)]
        for dx, dy in neighbours:
            for g in range(groups):
                x, y = ox + 2 + dx, oy + 2 + dy
                gains = dot(adj_table[a], both(onehot_at(x, y, g)), NN)
                for n, c in enumerate(chunks):
                    p, displace = pairs(a, x, y, g, (dx, dy), gains, c)
                    for q in range(3):
                        term = p * displace[q]
                        sums[q][n] = term if sums[q][n] is None else sums[q][n] + term
        ones = jnp.ones((8, LANES), jnp.float32)
        mine = [dot(ones, jnp.concatenate(sums[q], axis=0), NT, lax.Precision.HIGHEST)[0:1] for q in range(3)]
        back = []
        for g in range(groups):
            sums = [None] * 3
            for dx, dy in neighbours:
                b = (ox + 1 - dx) * nay + oy + 1 - dy
                gains = dot(adj_table[b], both(onehot_at(ox + 2, oy + 2, g)), NN)
                for c in chunks:
                    p, displace = pairs(b, ox + 2, oy + 2, g, (dx, dy), gains, c)
                    for q in range(3):
                        term = p * displace[q]
                        sums[q] = term if sums[q] is None else sums[q] + term
            back.append([jnp.sum(v, axis=0, keepdims=True) for v in sums])
        row = []
        for q in range(3):
            row.append(scale * (mine[q] - back[0][q][:, 0:slots]))
        own[pl.ds(o, 1), :] = jnp.concatenate(row, axis=1)
        for g in range(groups):
            halves = [(1, slots)] if g == 0 else [(0, 0)]
            for _, start in halves:
                other[g, pl.ds(o, 1), :] = jnp.concatenate(
                    [-scale * back[g][q][:, start:start + slots] for q in range(3)], axis=1
                )
        hot = onehot_at(ox + 2, oy + 2, 0).astype(jnp.float32)
        energy = dot(emb_energy, hot, NN, lax.Precision.HIGHEST)[0:1, 0:slots]
        energy += dot(readout, act[a].astype(jnp.float32), NT, lax.Precision.HIGHEST)[0:1]
        marked = region[ox + 2, oy + 2, 3:4, 0:slots]
        energies[pl.ds(o, 1), :] = jnp.where(marked >= 0.0, energy, 0.0)
        return carry

    lax.fori_loop(0, cells[0] * cells[1], forces_at, 0)


def on_device(positions, species, counts, embed, filters, w_up, w_energy):
    bx, by, bz = positions.shape[:3]
    slots = species.shape[-1]
    width = embed.shape[1]
    rad = filters.shape[1] // width
    spec = -(-embed.shape[0] // LANES) * LANES
    depth = lax.axis_size("gz")
    merged = depth * bz == 2
    occupied = jnp.arange(slots, dtype=jnp.int32) < counts[..., None]
    marked = jnp.where(occupied, species, -1).astype(jnp.float32)
    block = jnp.concatenate(
        [positions.reshape(bx, by, 3, slots), marked.reshape(bx, by, 1, slots)], axis=2
    )
    upward = [(i, (i + 1) % depth) for i in range(depth)]
    downward = [(b, a) for a, b in upward]
    low = lax.ppermute(block, "gz", upward)
    zero = jnp.zeros((slots,), jnp.float32)
    if merged:
        block = jnp.concatenate([block, low], axis=3)
        zrow = jnp.concatenate([zero, zero + 1.0])[None]
    else:
        high = lax.ppermute(block, "gz", downward)
        empty = jnp.full_like(block, -1.0)
        block = jnp.concatenate(
            [jnp.concatenate([block, low], axis=3), jnp.concatenate([high, empty], axis=3)], axis=2
        )
        zrow = jnp.stack([jnp.concatenate([zero, zero - 1.0]), jnp.concatenate([zero + 1.0, zero])])
    groups = block.shape[2] // 4
    block = exchange(block, "gx", 0, HALO)
    region = exchange(block, "gy", 1, HALO)

    anchors = (bx + 2) * (by + 2)
    cells = bx * by
    columns = region.shape[0] * region.shape[1] * groups
    energies, own, other = pl.pallas_call(
        functools.partial(kernel, (bx, by), merged, rad),
        out_shape=(
            jax.ShapeDtypeStruct((cells, slots), jnp.float32),
            jax.ShapeDtypeStruct((cells, 3 * slots), jnp.float32),
            jax.ShapeDtypeStruct((groups, cells, 3 * slots), jnp.float32),
        ),
        in_specs=[pl.BlockSpec(memory_space=pltpu.VMEM)] * 6,
        out_specs=[pl.BlockSpec(memory_space=pltpu.VMEM)] * 3,
        scratch_shapes=[
            pltpu.VMEM((spec, width), jnp.float32),
            pltpu.VMEM((rad * spec, width), jnp.bfloat16),
            pltpu.VMEM((columns, spec, LANES), jnp.bfloat16),
            pltpu.VMEM((4, LANES, LANES), jnp.float32),
            pltpu.VMEM((anchors, 4, slots, LANES), jnp.float32),
            pltpu.VMEM((anchors, rad * slots, 2 * spec), jnp.bfloat16),
            pltpu.VMEM((anchors, slots, width), jnp.bfloat16),
        ],
        compiler_params=pltpu.CompilerParams(vmem_limit_bytes=48 * 1024 * 1024),
    )(region, zrow, embed, filters, w_up, w_energy.reshape(1, width))

    forces = own + lax.ppermute(other[0], "gz", downward)
    if not merged:
        forces = forces + lax.ppermute(other[1], "gz", upward)
    return energies.reshape(species.shape), forces.reshape(positions.shape)


def solution(mesh):
    in_specs = (
        P("gx", "gy", "gz", None),
        P("gx", "gy", "gz", None),
        P("gx", "gy", "gz"),
        P(),
        P(),
        P(),
        P(),
    )
    out_specs = (P("gx", "gy", "gz", None), P("gx", "gy", "gz", None))
    return jax.shard_map(
        on_device, mesh=mesh, in_specs=in_specs, out_specs=out_specs, check_vma=False
    )
```

```python
import functools

import jax
import jax.numpy as jnp
from jax import lax
from jax.experimental import pallas as pl
from jax.experimental.pallas import tpu as pltpu
from jax.sharding import PartitionSpec as P

MSG_SCALE = 0.1
HALO = 2
LANES = 128
NT = (((1,), (1,)), ((), ()))
NN = (((1,), (0,)), ((), ()))


def exchange(block, axis, dim, width):
    count = lax.axis_size(axis)
    first = lax.slice_in_dim(block, 0, width, axis=dim)
    last = lax.slice_in_dim(block, block.shape[dim] - width, None, axis=dim)
    if count % 2 == 0:
        odd = lax.axis_index(axis) % 2 == 1
        whole = block.shape[dim] == width
        up = block if whole else jnp.where(odd, last, first)
        down = block if whole else jnp.where(odd, first, last)
        far = [(i, (i + 1) % count if i % 2 else (i - 1) % count) for i in range(count)]
        near = [(i, i - 1 if i % 2 else i + 1) for i in range(count)]
        from_far = lax.ppermute(up, axis, far)
        from_near = lax.ppermute(down, axis, near)
        low = jnp.where(odd, from_near, from_far)
        high = jnp.where(odd, from_far, from_near)
    else:
        forward = [(i, (i + 1) % count) for i in range(count)]
        low = lax.ppermute(last, axis, forward)
        high = lax.ppermute(first, axis, [(b, a) for a, b in forward])
    return jnp.concatenate([low, block, high], axis=dim)


def dot(a, b, dims, precision=None):
    return lax.dot_general(a, b, dims, precision=precision, preferred_element_type=jnp.float32)


def split(values):
    high = values.astype(jnp.bfloat16)
    return high, (values - high.astype(jnp.float32)).astype(jnp.bfloat16)


def thirds(rows):
    high = rows.astype(jnp.bfloat16)
    middle, low = split(rows - high.astype(jnp.float32))
    at = lax.broadcasted_iota(jnp.int32, rows.shape, 0)
    parts = [part.astype(jnp.float32) for part in (high, middle, low)]
    kept = jnp.where(at == 0, parts[0], jnp.where(at == 1, parts[1], jnp.where(at == 2, parts[2], 0.0)))
    return kept.astype(jnp.bfloat16)


def kernel(
    cells, merged, rad,
    region, zrow_ref, embed, filters, w_up, w_energy,
    energies, own, other,
    emb_pad, table, onehot, stage, anchors, adj_table, mixed, act, weights_a, weights_b, kept, back, mine,
):
    nax, nay = cells[0] + 2, cells[1] + 2
    groups = region.shape[2] // 4
    slots = energies.shape[-1]
    nspec, width = embed.shape
    spec = emb_pad.shape[0]
    neighbours = [(dx, dy) for dx in (-1, 0, 1) for dy in (-1, 0, 1)]
    bf = jnp.bfloat16

    emb_pad[...] = jnp.zeros_like(emb_pad)
    emb_pad[0:nspec, :] = embed[...].astype(jnp.float32)
    emb = emb_pad[...]
    rows = dot(emb.astype(bf), filters[...], NN).astype(bf)
    for k in range(rad):
        table[k * spec:(k + 1) * spec, :] = rows[:, k * width:(k + 1) * width]
    energy_row = jnp.broadcast_to(w_energy[...], (8, width))
    readout = dot(energy_row, w_up[...].astype(jnp.float32), NT, lax.Precision.HIGHEST)
    emb_energy = dot(energy_row, emb, NT, lax.Precision.HIGHEST)

    ids = lax.broadcasted_iota(jnp.int32, (spec, LANES), 0).astype(jnp.float32)
    for x in range(region.shape[0]):
        for y in range(region.shape[1]):
            for g in range(groups):
                marked = region[x, y, g * 4 + 3:g * 4 + 4, :]
                onehot[(x * region.shape[1] + y) * groups + g] = (marked == ids).astype(bf)

    for q in range(4):
        for x in range(nax):
            stage[q, x * nay:(x + 1) * nay, :] = region[1 + x, 1:1 + nay, q, :]
        columns = stage[q].T
        for a in range(nax * nay):
            anchors[a, q] = jnp.broadcast_to(columns[0:slots, a:a + 1], (slots, LANES))

    def target(x, y, g, shift):
        row = region[x, y, g * 4:g * 4 + 3, :]
        return row[0:1] + shift[0], row[1:2] + shift[1], row[2:3]

    def z_image(dz, g):
        shift = zrow_ref[g:g + 1, :]
        if merged:
            return jnp.where(dz > 0.0, dz - shift, dz + shift)
        return dz + shift

    def onehot_at(x, y, g):
        return onehot[(x * region.shape[1] + y) * groups + g]

    step = 16
    chunks = [slice(r, r + step) for r in range(0, slots, step)]
    diagonal = lax.broadcasted_iota(jnp.int32, (slots, LANES), 0) == lax.broadcasted_iota(
        jnp.int32, (slots, LANES), 1
    )

    offsets = [(dx, dy, g) for dx, dy in neighbours for g in range(groups)]

    def weigh(a, buffer, n):
        ax, ay = a // nay, a % nay
        dx, dy, g = offsets[n]
        tx, ty, tz = target(ax + 1 + dx, ay + 1 + dy, g, (dx, dy))
        lanes = slice(n * LANES, (n + 1) * LANES)
        for c in chunks:
            ex = tx - anchors[a, 0, c, :]
            ey = ty - anchors[a, 1, c, :]
            dz = tz - anchors[a, 2, c, :]
            if merged:
                ez = jnp.abs(dz) - zrow_ref[g:g + 1, :]
            else:
                ez = dz + zrow_ref[g:g + 1, :]
            s = ex * ex + ey * ey + ez * ez
            f = jnp.maximum(1.0 - s, 0.0)
            e = jnp.exp(-0.5 * s)
            kept[a, n, 0, c, :] = f
            kept[a, n, 1, c, :] = e
            w = e * (f * f)
            if dx == 0 and dy == 0 and g == 0:
                w = jnp.where(diagonal[c], 0.0, w)
            e = e * e
            for k in range(rad):
                if k == 1:
                    w = w * e
                elif k > 1:
                    e = e * e * e
                    w = w * e
                buffer[k * slots + c.start:k * slots + c.stop, lanes] = w.astype(bf)

    def gather(a, buffer, n, total):
        ax, ay = a // nay, a % nay
        some = offsets[n:n + 2]
        hots = [onehot_at(ax + 1 + dx, ay + 1 + dy, g) for dx, dy, g in some]
        term = dot(buffer[:, n * LANES:(n + len(some)) * LANES], jnp.concatenate(hots, axis=1), NT)
        return term if total is None else total + term

    def keep(a, sums):
        for k in range(rad):
            high, low = split(sums[k * slots:(k + 1) * slots])
            mixed[a, 0:slots, k * spec:(k + 1) * spec] = high
            mixed[a, slots:, k * spec:(k + 1) * spec] = low

    def overlap(a, buffer, before, buffer_before):
        total = None
        for n in range(0, len(offsets), 2):
            total = gather(before, buffer_before, n, total)
            weigh(a, buffer, n)
            if n + 1 < len(offsets):
                weigh(a, buffer, n + 1)
        keep(before, total)

    def message_at(t, carry):
        a = 2 * t
        overlap(a, weights_a, jnp.maximum(a - 1, 0), weights_b)
        overlap(a + 1, weights_b, a, weights_a)
        return carry

    weights_b[...] = jnp.zeros_like(weights_b)
    lax.fori_loop(0, nax * nay // 2, message_at, 0)
    total = None
    for n in range(0, len(offsets), 2):
        total = gather(nax * nay - 1, weights_b, n, total)
    keep(nax * nay - 1, total)

    batch = 4

    def adjoint_at(t, carry):
        group = [t * batch + i for i in range(batch)]
        halves = dot(jnp.concatenate([mixed[a] for a in group], axis=0), table[...], NN)
        adjoints = []
        for i, a in enumerate(group):
            at = 2 * slots * i
            message = MSG_SCALE * (halves[at:at + slots] + halves[at + slots:at + 2 * slots])
            sigmoid = 1.0 / (1.0 + jnp.exp(-message))
            act[a] = (message * sigmoid).astype(bf)
            slope = sigmoid * (1.0 + message * (1.0 - sigmoid)) * readout[0:1]
            adjoints.append(jnp.where(anchors[a, 3] >= 0.0, slope, 0.0).astype(bf))
        turned = dot(jnp.concatenate(adjoints, axis=0), table[...], NT)
        for i, a in enumerate(group):
            for n, c in enumerate(chunks):
                high, low = split(turned[slots * i + c.start:slots * i + c.stop])
                for k in range(rad):
                    at = slice((n * rad + k) * step, (n * rad + k + 1) * step)
                    adj_table[a, at, 0:spec] = high[:, k * spec:(k + 1) * spec]
                    adj_table[a, at, spec:] = low[:, k * spec:(k + 1) * spec]
        return carry

    lax.fori_loop(0, nax * nay // batch, adjoint_at, 0, unroll=True)

    def pairs(a, n, x, y, gains, r):
        c = chunks[r]
        dx, dy, g = offsets[n]
        tx, ty, tz = target(x, y, g, (dx, dy))
        ex = tx - anchors[a, 0, c, :]
        ey = ty - anchors[a, 1, c, :]
        ez = z_image(tz - anchors[a, 2, c, :], g)
        f = kept[a, n, 0, c, :]
        e = kept[a, n, 1, c, :]
        e2 = e * e
        plain = None
        for k in range(rad):
            if k == 1:
                e = e * e2
            elif k > 1:
                e2 = e2 * e2 * e2
                e = e * e2
            term = e * gains[k * step:(k + 1) * step]
            scaled = (0.125 * 3.0 ** k) * term
            plain, steep = (term, scaled) if plain is None else (plain + term, steep + scaled)
        return f * (f * steep * 2.0 + plain), (ex, ey, ez)

    def both(hots):
        hots = jnp.concatenate(hots, axis=1)
        return jnp.concatenate([hots, hots], axis=0)

    def chunk_of(a, r):
        return adj_table[a, r * rad * step:(r + 1) * rad * step, :]

    scale = -4.0 * MSG_SCALE
    back[...] = jnp.zeros_like(back)
    wide = 2

    def add_back(column, forces):
        for q in range(3):
            back[column, q] += forces[q]

    def fold(values):
        return sum(values[i:i + 8] for i in range(8, step, 8)) + values[0:8]

    def forces_at(o, carry):
        ox, oy = o // cells[1], o % cells[1]
        a = (ox + 1) * nay + oy + 1
        sums = [[None] * len(chunks) for _ in range(3)]
        for first in range(0, len(offsets), wide):
            some = list(range(first, min(first + wide, len(offsets))))
            spots = [(ox + 2 + offsets[n][0], oy + 2 + offsets[n][1]) for n in some]
            hots = both([onehot_at(x, y, offsets[n][2]) for n, (x, y) in zip(some, spots)])
            totals = [[None] * 3 for _ in some]
            for r in range(len(chunks)):
                gains = dot(chunk_of(a, r), hots, NN)
                for i, (n, (x, y)) in enumerate(zip(some, spots)):
                    p, displace = pairs(a, n, x, y, gains[:, i * LANES:(i + 1) * LANES], r)
                    for q in range(3):
                        term = p * displace[q]
                        sums[q][r] = term if sums[q][r] is None else sums[q][r] + term
                        term = fold(term)
                        totals[i][q] = term if totals[i][q] is None else totals[i][q] + term
            for i, (n, (x, y)) in enumerate(zip(some, spots)):
                add_back((x * region.shape[1] + y) * groups + offsets[n][2], totals[i])
        for q in range(3):
            for r, c in enumerate(chunks):
                mine[o, q, c, :] = sums[q][r]
        return carry

    lax.fori_loop(0, cells[0] * cells[1], forces_at, 0)

    for ax in range(nax):
        for ay in range(nay):
            if 0 < ax < nax - 1 and 0 < ay < nay - 1:
                continue
            a = ax * nay + ay
            some = [
                n for n, (dx, dy, g) in enumerate(offsets)
                if 0 < ax + dx < nax - 1 and 0 < ay + dy < nay - 1
            ]
            for first in range(0, len(some), wide):
                part = some[first:first + wide]
                spots = [(ax + 1 + offsets[n][0], ay + 1 + offsets[n][1]) for n in part]
                hots = both([onehot_at(x, y, offsets[n][2]) for n, (x, y) in zip(part, spots)])
                totals = [[None] * 3 for _ in part]
                for r in range(len(chunks)):
                    gains = dot(chunk_of(a, r), hots, NN)
                    for i, (n, (x, y)) in enumerate(zip(part, spots)):
                        p, displace = pairs(a, n, x, y, gains[:, i * LANES:(i + 1) * LANES], r)
                        for q in range(3):
                            term = fold(p * displace[q])
                            totals[i][q] = term if totals[i][q] is None else totals[i][q] + term
                for i, (n, (x, y)) in enumerate(zip(part, spots)):
                    add_back((x * region.shape[1] + y) * groups + offsets[n][2], totals[i])

    inner = [(ox, oy) for ox in range(cells[0]) for oy in range(cells[1])]
    high, low = split(mine[...].reshape(len(inner) * 3 * slots, LANES))
    ones = jnp.ones((8, 2 * LANES), bf)
    rows = dot(ones, jnp.concatenate([high, low], axis=1), NT)[0:1]
    for o, (ox, oy) in enumerate(inner):
        column = ((ox + 2) * region.shape[1] + oy + 2) * groups
        sums = [jnp.sum(back[column, q], axis=0, keepdims=True)[:, 0:slots] for q in range(3)]
        for q in range(3):
            at = (o * 3 + q) * slots
            own[o:o + 1, q * slots:(q + 1) * slots] = scale * (rows[:, at:at + slots] - sums[q])
        for g in range(groups):
            start = slots if g == 0 else 0
            for q in range(3):
                row = jnp.sum(back[column + g, q], axis=0, keepdims=True)
                other[g, o:o + 1, q * slots:(q + 1) * slots] = -scale * row[:, start:start + slots]

    hots = jnp.concatenate([onehot_at(ox + 2, oy + 2, 0)[:, 0:slots] for ox, oy in inner], axis=1)
    acts = jnp.concatenate([act[(ox + 1) * nay + oy + 1] for ox, oy in inner], axis=0)
    energy = dot(thirds(emb_energy), hots, NN) + dot(thirds(readout), acts, NT)
    energy = jnp.sum(energy, axis=0, keepdims=True)
    for o, (ox, oy) in enumerate(inner):
        marked = region[ox + 2, oy + 2, 3:4, 0:slots]
        energies[o:o + 1, :] = jnp.where(marked >= 0.0, energy[:, o * slots:(o + 1) * slots], 0.0)


def layer(region, zrow, embed, filters, w_up, w_energy, block, merged, slots):
    width = embed.shape[1]
    rad = filters.shape[1] // width
    spec = -(-embed.shape[0] // LANES) * LANES
    groups = region.shape[2] // 4
    anchors = (block[0] + 2) * (block[1] + 2)
    cells = block[0] * block[1]
    columns = region.shape[0] * region.shape[1] * groups
    return pl.pallas_call(
        functools.partial(kernel, block, merged, rad),
        out_shape=(
            jax.ShapeDtypeStruct((cells, slots), jnp.float32),
            jax.ShapeDtypeStruct((cells, 3 * slots), jnp.float32),
            jax.ShapeDtypeStruct((groups, cells, 3 * slots), jnp.float32),
        ),
        in_specs=[pl.BlockSpec(memory_space=pltpu.VMEM)] * 6,
        out_specs=[pl.BlockSpec(memory_space=pltpu.VMEM)] * 3,
        scratch_shapes=[
            pltpu.VMEM((spec, width), jnp.float32),
            pltpu.VMEM((rad * spec, width), jnp.bfloat16),
            pltpu.VMEM((columns, spec, LANES), jnp.bfloat16),
            pltpu.VMEM((4, LANES, LANES), jnp.float32),
            pltpu.VMEM((anchors, 4, slots, LANES), jnp.float32),
            pltpu.VMEM((anchors, rad * slots, 2 * spec), jnp.bfloat16),
            pltpu.VMEM((anchors, 2 * slots, rad * spec), jnp.bfloat16),
            pltpu.VMEM((anchors, slots, width), jnp.bfloat16),
            pltpu.VMEM((rad * slots, 9 * groups * LANES), jnp.bfloat16),
            pltpu.VMEM((rad * slots, 9 * groups * LANES), jnp.bfloat16),
            pltpu.VMEM((anchors, 9 * groups, 2, slots, LANES), jnp.float32),
            pltpu.VMEM((columns, 3, 8, LANES), jnp.float32),
            pltpu.VMEM((cells, 3, slots, LANES), jnp.float32),
        ],
        compiler_params=pltpu.CompilerParams(vmem_limit_bytes=48 * 1024 * 1024),
    )(region, zrow, embed, filters, w_up, w_energy)


def on_device(positions, species, counts, embed, filters, w_up, w_energy):
    bx, by, bz = positions.shape[:3]
    slots = species.shape[-1]
    width = embed.shape[1]
    depth = lax.axis_size("gz")
    merged = depth * bz == 2
    occupied = jnp.arange(slots, dtype=jnp.int32) < counts[..., None]
    marked = jnp.where(occupied, species, -1).astype(jnp.float32)
    block = jnp.concatenate(
        [positions.reshape(bx, by, 3, slots), marked.reshape(bx, by, 1, slots)], axis=2
    )
    upward = [(i, (i + 1) % depth) for i in range(depth)]
    downward = [(b, a) for a, b in upward]
    low = lax.ppermute(block, "gz", upward)
    zero = jnp.zeros((slots,), jnp.float32)
    if merged:
        block = jnp.concatenate([block, low], axis=3)
        zrow = jnp.concatenate([zero, zero + 1.0])[None]
    else:
        high = lax.ppermute(block, "gz", downward)
        empty = jnp.full_like(block, -1.0)
        block = jnp.concatenate(
            [jnp.concatenate([block, low], axis=3), jnp.concatenate([high, empty], axis=3)], axis=2
        )
        zrow = jnp.stack([jnp.concatenate([zero, zero - 1.0]), jnp.concatenate([zero + 1.0, zero])])
    block = exchange(block, "gx", 0, HALO)
    region = exchange(block, "gy", 1, HALO)

    energies, own, other = layer(
        region, zrow, embed, filters, w_up, w_energy.reshape(1, width), (bx, by), merged, slots
    )

    forces = own + lax.ppermute(other[0], "gz", downward)
    if not merged:
        forces = forces + lax.ppermute(other[1], "gz", upward)
    return energies.reshape(species.shape), forces.reshape(positions.shape)


def solution(mesh):
    in_specs = (
        P("gx", "gy", "gz", None),
        P("gx", "gy", "gz", None),
        P("gx", "gy", "gz"),
        P(),
        P(),
        P(),
        P(),
    )
    out_specs = (P("gx", "gy", "gz", None), P("gx", "gy", "gz", None))
    return jax.shard_map(
        on_device, mesh=mesh, in_specs=in_specs, out_specs=out_specs, check_vma=False
    )
```

```python
import functools

import jax
import jax.numpy as jnp
from jax import lax
from jax.experimental import pallas as pl
from jax.experimental.pallas import tpu as pltpu
from jax.sharding import PartitionSpec as P

MSG_SCALE = 0.1
HALO = 2
FAR_VMEM = 36 * 1024 * 1024
LANES = 128
STEP = 16
WIDE = 2
LOG2E = 1.4426950408889634
NT = (((1,), (1,)), ((), ()))
NN = (((1,), (0,)), ((), ()))


def exchange(block, axis, dim, width):
    count = lax.axis_size(axis)
    first = lax.slice_in_dim(block, 0, width, axis=dim)
    last = lax.slice_in_dim(block, block.shape[dim] - width, None, axis=dim)
    if count % 2 == 0:
        odd = lax.axis_index(axis) % 2 == 1
        whole = block.shape[dim] == width
        up = block if whole else jnp.where(odd, last, first)
        down = block if whole else jnp.where(odd, first, last)
        far = [(i, (i + 1) % count if i % 2 else (i - 1) % count) for i in range(count)]
        near = [(i, i - 1 if i % 2 else i + 1) for i in range(count)]
        from_far = lax.ppermute(up, axis, far)
        from_near = lax.ppermute(down, axis, near)
        low = jnp.where(odd, from_near, from_far)
        high = jnp.where(odd, from_far, from_near)
    else:
        forward = [(i, (i + 1) % count) for i in range(count)]
        low = lax.ppermute(last, axis, forward)
        high = lax.ppermute(first, axis, [(b, a) for a, b in forward])
    return jnp.concatenate([low, block, high], axis=dim)


def dot(a, b, dims, precision=None):
    return lax.dot_general(a, b, dims, precision=precision, preferred_element_type=jnp.float32)


def split(values):
    high = values.astype(jnp.bfloat16)
    return high, (values - high.astype(jnp.float32)).astype(jnp.bfloat16)


def thirds(rows):
    high = rows.astype(jnp.bfloat16)
    middle, low = split(rows - high.astype(jnp.float32))
    at = lax.broadcasted_iota(jnp.int32, rows.shape, 0)
    parts = [part.astype(jnp.float32) for part in (high, middle, low)]
    kept = jnp.where(at == 0, parts[0], jnp.where(at == 1, parts[1], jnp.where(at == 2, parts[2], 0.0)))
    return kept.astype(jnp.bfloat16)


class Cells:
    def __init__(self, block, merged, rad, spec, slots):
        self.block, self.merged, self.rad, self.spec, self.slots = block, merged, rad, spec, slots
        self.groups = 1 if merged else 2
        self.nax, self.nay = block[0] + 2, block[1] + 2
        self.nx, self.ny = block[0] + 2 * HALO, block[1] + 2 * HALO
        self.offsets = [
            (dx, dy, g) for dx in (-1, 0, 1) for dy in (-1, 0, 1) for g in range(self.groups)
        ]
        self.rows = [slice(r, r + STEP) for r in range(0, slots, STEP)]

    def inner(self, ay):
        return 1 <= ay <= self.block[1]

    def split_offsets(self, ay):
        near = [n for n, (_, dy, _) in enumerate(self.offsets) if self.inner(ay) and self.inner(ay + dy)]
        return near, [n for n in range(len(self.offsets)) if n not in near]

    def z_shift(self, g):
        lane = lax.broadcasted_iota(jnp.int32, (1, LANES), 1)
        if self.merged:
            return jnp.where(lane < self.slots, 0.0, 1.0)
        if g == 0:
            return jnp.where(lane < self.slots, 0.0, -1.0)
        return jnp.where(lane < self.slots, 1.0, 0.0)


def place_anchors(z, stage, rows, out):
    for q in range(4):
        for i, (ref, x, y) in enumerate(rows):
            stage[q, i:i + 1, :] = ref[x, y, q:q + 1, :]
        columns = stage[q].T
        for i in range(len(rows)):
            out[i, q] = jnp.broadcast_to(columns[0:z.slots, i:i + 1], (z.slots, LANES))


def place_onehot(z, ref, x, y, g, out, at):
    ids = lax.broadcasted_iota(jnp.int32, (z.spec, LANES), 0).astype(jnp.float32)
    out[at] = (ref[x, y, g * 4 + 3:g * 4 + 4, :] == ids).astype(jnp.bfloat16)


def target(ref, x, y, offset):
    dx, dy, g = offset
    row = ref[x, y, g * 4:g * 4 + 3, :]
    return row[0:1] + dx, row[1:2] + dy, row[2:3]


def weigh(z, position, anchor, offset, buffer, lanes, keep):
    tx, ty, tz = position
    shift = z.z_shift(offset[2])
    for c in z.rows:
        ex = tx - anchor[0, c, :]
        ey = ty - anchor[1, c, :]
        dz = tz - anchor[2, c, :]
        ez = jnp.abs(dz) - shift if z.merged else dz + shift
        s = ex * ex + ey * ey + ez * ez
        f = jnp.maximum(1.0 - s, 0.0)
        power = s * (-0.5 * LOG2E)
        e = jnp.exp2(power)
        keep[0, c, :] = f
        keep[1, c, :] = e
        f = f * f
        if offset == (0, 0, 0):
            row = lax.broadcasted_iota(jnp.int32, (STEP, LANES), 0) + c.start
            lane = lax.broadcasted_iota(jnp.int32, (STEP, LANES), 1)
            f = jnp.where(row == lane, 0.0, f)
        for k in range(z.rad):
            if k:
                power = power * 3.0
                e = jnp.exp2(power)
            buffer[k * z.slots + c.start:k * z.slots + c.stop, lanes] = (e * f).astype(jnp.bfloat16)


def pack_kernel(counts_hbm, positions_hbm, species_hbm, out, counts, positions, species, arrived):
    arguments = [(counts_hbm, counts), (positions_hbm, positions), (species_hbm, species)]
    copies = [pltpu.make_async_copy(a, b, arrived.at[i]) for i, (a, b) in enumerate(arguments)]
    for copy in copies:
        copy.start()
    for copy in copies:
        copy.wait()
    slots = out.shape[3]
    lane = lax.broadcasted_iota(jnp.int32, (1, slots), 1)
    for x in range(out.shape[0]):
        for y in range(out.shape[1]):
            row = positions[x, y, 0:1, :]
            for q in range(3):
                out[x, y, q:q + 1, :] = row[:, q * slots:(q + 1) * slots]
            marked = jnp.where(lane < counts[x, y], species[x, y, 0:1, :], -1)
            out[x, y, 3:4, :] = marked.astype(jnp.float32)


def near_kernel(
    z, near, embed_hbm, filters_hbm, w_up_hbm, w_energy_hbm,
    table, readout, emb_energy, onehot, anchors, sums, kept,
    emb_pad, stage, embed, filters, w_up, w_energy, arrived, *buffers,
):
    nspec, width = embed.shape
    by = z.block[1]
    weights = [(embed_hbm, embed), (filters_hbm, filters), (w_up_hbm, w_up), (w_energy_hbm, w_energy)]
    copies = [pltpu.make_async_copy(a, b, arrived.at[i]) for i, (a, b) in enumerate(weights)]
    for copy in copies:
        copy.start()

    for x in range(z.nx):
        for y in range(by):
            for g in range(z.groups):
                place_onehot(z, near, x, y, g, onehot, (x * by + y) * z.groups + g)
    place_anchors(z, stage, [(near, ax + 1, y) for ax in range(z.nax) for y in range(by)], anchors)

    def message_at(ax, carry):
        for y in range(by):
            a = ax * by + y
            some = z.split_offsets(y + 1)[0]
            hots = []
            for i, n in enumerate(some):
                dx, dy, g = z.offsets[n]
                spot = target(near, ax + 1 + dx, y + dy, z.offsets[n])
                weigh(
                    z, spot, anchors.at[a], z.offsets[n], buffers[y],
                    slice(i * LANES, (i + 1) * LANES), kept.at[a, i],
                )
                hots.append(onehot[((ax + 1 + dx) * by + y + dy) * z.groups + g])
            weights = buffers[y][:, 0:len(some) * LANES]
            sums[a] = dot(weights, jnp.concatenate(hots, axis=1), NT)
        return carry

    lax.fori_loop(0, z.nax, message_at, 0)

    for copy in copies:
        copy.wait()
    emb_pad[...] = jnp.zeros_like(emb_pad)
    emb_pad[0:nspec, :] = embed[...].astype(jnp.float32)
    emb = emb_pad[...]
    rows = dot(emb.astype(jnp.bfloat16), filters[...], NN).astype(jnp.bfloat16)
    for k in range(z.rad):
        table[k * z.spec:(k + 1) * z.spec, :] = rows[:, k * width:(k + 1) * width]
    energy_row = jnp.broadcast_to(w_energy[...], (8, width))
    readout[...] = dot(energy_row, w_up[...].astype(jnp.float32), NT, lax.Precision.HIGHEST)
    emb_energy[...] = dot(energy_row, emb, NT, lax.Precision.HIGHEST)


def far_kernel(
    z, region, table, readout_ref, emb_energy_ref, onehot_near, anchors_near, sums_near, kept_near,
    energies, own, other,
    onehot_far, anchors_far, kept_far, stage, adj_table, mixed, act, back, mine, *buffers,
):
    by = z.block[1]
    bf = jnp.bfloat16
    slots, spec, rad = z.slots, z.spec, z.rad
    readout = readout_ref[...]
    outer = [y for y in range(z.ny) if not HALO <= y < HALO + by]

    for x in range(z.nx):
        for i, y in enumerate(outer):
            for g in range(z.groups):
                place_onehot(z, region, x, y, g, onehot_far, (x * len(outer) + i) * z.groups + g)
    place_anchors(
        z, stage, [(region, ax + 1, y) for ax in range(z.nax) for y in (1, z.ny - HALO)], anchors_far
    )

    def onehot_at(x, y, g):
        if y in outer:
            return onehot_far[(x * len(outer) + outer.index(y)) * z.groups + g]
        return onehot_near[(x * by + y - HALO) * z.groups + g]

    def anchor_at(ax, ay):
        if z.inner(ay):
            return anchors_near.at[ax * by + ay - 1]
        return anchors_far.at[ax * 2 + (ay > 0)]

    def kept_at(ax, ay, n):
        near, _ = z.split_offsets(ay)
        if n in near:
            return kept_near.at[ax * by + ay - 1, near.index(n)]
        return kept_far.at[ax * z.nay + ay, n]

    def message_at(ax, carry):
        for ay in range(z.nay):
            a = ax * z.nay + ay
            some = z.split_offsets(ay)[1]
            hots = []
            for i, n in enumerate(some):
                dx, dy, g = z.offsets[n]
                x, y = ax + 1 + dx, ay + 1 + dy
                weigh(
                    z, target(region, x, y, z.offsets[n]), anchor_at(ax, ay), z.offsets[n], buffers[ay],
                    slice(i * LANES, (i + 1) * LANES), kept_at(ax, ay, n),
                )
                hots.append(onehot_at(x, y, g))
            total = sums_near[ax * by + ay - 1] if z.inner(ay) else None
            if some:
                term = dot(buffers[ay][:, 0:len(some) * LANES], jnp.concatenate(hots, axis=1), NT)
                total = term if total is None else total + term
            for k in range(rad):
                high, low = split(total[k * slots:(k + 1) * slots])
                mixed[a, 0:slots, k * spec:(k + 1) * spec] = high
                mixed[a, slots:, k * spec:(k + 1) * spec] = low
        return carry

    lax.fori_loop(0, z.nax, message_at, 0)

    def adjoint_at(ax, carry):
        group = [ax * z.nay + ay for ay in range(z.nay)]
        halves = dot(jnp.concatenate([mixed[a] for a in group], axis=0), table[...], NN)
        adjoints = []
        for ay, a in enumerate(group):
            at = 2 * slots * ay
            message = MSG_SCALE * (halves[at:at + slots] + halves[at + slots:at + 2 * slots])
            sigmoid = 1.0 / (1.0 + jnp.exp(-message))
            act[a] = (message * sigmoid).astype(bf)
            slope = sigmoid * (1.0 + message * (1.0 - sigmoid)) * readout[0:1]
            adjoints.append(jnp.where(anchor_at(ax, ay)[3] >= 0.0, slope, 0.0).astype(bf))
        turned = dot(jnp.concatenate(adjoints, axis=0), table[...], NT)
        for ay, a in enumerate(group):
            for r, c in enumerate(z.rows):
                high, low = split(turned[slots * ay + c.start:slots * ay + c.stop])
                for k in range(rad):
                    at = slice((r * rad + k) * STEP, (r * rad + k + 1) * STEP)
                    adj_table[a, at, 0:spec] = high[:, k * spec:(k + 1) * spec]
                    adj_table[a, at, spec:] = low[:, k * spec:(k + 1) * spec]
        return carry

    lax.fori_loop(0, z.nax, adjoint_at, 0, unroll=True)

    def pairs(ax, ay, n, gains, r):
        c = z.rows[r]
        dx, dy, g = z.offsets[n]
        tx, ty, tz = target(region, ax + 1 + dx, ay + 1 + dy, z.offsets[n])
        anchor, keep = anchor_at(ax, ay), kept_at(ax, ay, n)
        ex = tx - anchor[0, c, :]
        ey = ty - anchor[1, c, :]
        ez = tz - anchor[2, c, :]
        shift = z.z_shift(g)
        ez = ez + jnp.where(ez > 0.0, -shift, shift) if z.merged else ez + shift
        f = keep[0, c, :]
        e = keep[1, c, :]
        e2 = e * e
        plain = None
        for k in range(rad):
            if k == 1:
                e = e * e2
            elif k > 1:
                e2 = e2 * e2 * e2
                e = e * e2
            term = e * gains[k * STEP:(k + 1) * STEP]
            scaled = (0.25 * 3.0 ** k) * term
            plain, steep = (term, scaled) if plain is None else (plain + term, steep + scaled)
        return f * (f * steep + plain), (ex, ey, ez)

    def blocks(ax, ay, some, sums):
        a = ax * z.nay + ay
        for first in range(0, len(some), WIDE):
            part = some[first:first + WIDE]
            spots = [(ax + 1 + z.offsets[n][0], ay + 1 + z.offsets[n][1], z.offsets[n][2]) for n in part]
            hots = jnp.concatenate([onehot_at(*spot) for spot in spots], axis=1)
            hots = jnp.concatenate([hots, hots], axis=0)
            totals = [[None] * 3 for _ in part]
            for r in range(len(z.rows)):
                gains = dot(adj_table[a, r * rad * STEP:(r + 1) * rad * STEP, :], hots, NN)
                for i, n in enumerate(part):
                    p, displace = pairs(ax, ay, n, gains[:, i * LANES:(i + 1) * LANES], r)
                    for q in range(3):
                        term = p * displace[q]
                        if sums is not None:
                            sums[q][r] = term if sums[q][r] is None else sums[q][r] + term
                        term = sum(term[j:j + 8] for j in range(8, STEP, 8)) + term[0:8]
                        totals[i][q] = term if totals[i][q] is None else totals[i][q] + term
            for (x, y, g), total in zip(spots, totals):
                for q in range(3):
                    back[(x * z.ny + y) * z.groups + g, q] += total[q]

    back[...] = jnp.zeros_like(back)

    def forces_at(ox, carry):
        for oy in range(by):
            sums = [[None] * len(z.rows) for _ in range(3)]
            blocks(ox + 1, oy + 1, range(len(z.offsets)), sums)
            for q in range(3):
                for r, c in enumerate(z.rows):
                    mine[ox * by + oy, q, c, :] = sums[q][r]
        return carry

    lax.fori_loop(0, z.block[0], forces_at, 0)

    for ax in range(z.nax):
        for ay in range(z.nay):
            if 0 < ax < z.nax - 1 and z.inner(ay):
                continue
            blocks(ax, ay, [
                n for n, (dx, dy, _) in enumerate(z.offsets) if 0 < ax + dx < z.nax - 1 and z.inner(ay + dy)
            ], None)

    scale = -4.0 * MSG_SCALE
    cells = [(ox, oy) for ox in range(z.block[0]) for oy in range(by)]
    high, low = split(mine[...].reshape(len(cells) * 3 * slots, LANES))
    ones = jnp.ones((8, 2 * LANES), bf)
    rows = dot(ones, jnp.concatenate([high, low], axis=1), NT)[0:1]
    for o, (ox, oy) in enumerate(cells):
        column = ((ox + HALO) * z.ny + oy + HALO) * z.groups
        sums = [jnp.sum(back[column, q], axis=0, keepdims=True)[:, 0:slots] for q in range(3)]
        for q in range(3):
            at = (o * 3 + q) * slots
            own[ox, oy, :, q * slots:(q + 1) * slots] = scale * (rows[:, at:at + slots] - sums[q])
        for g in range(z.groups):
            start = slots if g == 0 else 0
            for q in range(3):
                row = jnp.sum(back[column + g, q], axis=0, keepdims=True)
                other[g, ox, oy, :, q * slots:(q + 1) * slots] = -scale * row[:, start:start + slots]

    hots = jnp.concatenate([onehot_at(ox + HALO, oy + HALO, 0)[:, 0:slots] for ox, oy in cells], axis=1)
    acts = jnp.concatenate([act[(ox + 1) * z.nay + oy + 1] for ox, oy in cells], axis=0)
    energy = dot(thirds(emb_energy_ref[...]), hots, NN) + dot(thirds(readout), acts, NT)
    energy = jnp.sum(energy, axis=0, keepdims=True)
    for o, (ox, oy) in enumerate(cells):
        marked = region[ox + HALO, oy + HALO, 3:4, 0:slots]
        energies[ox, oy, :, :] = jnp.where(marked >= 0.0, energy[:, o * slots:(o + 1) * slots], 0.0)


VMEM = pl.BlockSpec(memory_space=pltpu.VMEM)
HBM = pl.BlockSpec(memory_space=pltpu.HBM)


def in_hbm(*arrays):
    return [pltpu.with_memory_space_constraint(array, pltpu.HBM) for array in arrays]


def pack(positions, species, counts):
    bx, by, _, slots = species.shape
    return pl.pallas_call(
        pack_kernel,
        out_shape=jax.ShapeDtypeStruct((bx, by, 4, slots), jnp.float32),
        in_specs=[HBM] * 3,
        out_specs=VMEM,
        scratch_shapes=[
            pltpu.SMEM(counts.shape, counts.dtype),
            pltpu.VMEM(positions.shape, positions.dtype),
            pltpu.VMEM(species.shape, species.dtype),
            pltpu.SemaphoreType.DMA((3,)),
        ],
        compiler_params=pltpu.CompilerParams(vmem_limit_bytes=1024 * 1024),
    )(*in_hbm(counts, positions, species))


def near_layer(z, near, embed, filters, w_up, w_energy):
    width = embed.shape[1]
    by = z.block[1]
    cells, most = z.nax * by, max(len(z.split_offsets(y + 1)[0]) for y in range(by))
    shapes = [
        ((z.rad * z.spec, width), jnp.bfloat16),
        ((8, width), jnp.float32),
        ((8, z.spec), jnp.float32),
        ((z.nx * by * z.groups, z.spec, LANES), jnp.bfloat16),
        ((cells, 4, z.slots, LANES), jnp.float32),
        ((cells, z.rad * z.slots, z.spec), jnp.float32),
        ((cells, most, 2, z.slots, LANES), jnp.float32),
    ]
    flops = 2 * cells * most * z.rad * z.slots * LANES * z.spec
    return pl.pallas_call(
        functools.partial(near_kernel, z),
        out_shape=[jax.ShapeDtypeStruct(*shape) for shape in shapes],
        in_specs=[VMEM] + [HBM] * 4,
        out_specs=[VMEM] * len(shapes),
        scratch_shapes=[
            pltpu.VMEM((z.spec, width), jnp.float32),
            pltpu.VMEM((4, LANES, LANES), jnp.float32),
            pltpu.VMEM(embed.shape, embed.dtype),
            pltpu.VMEM(filters.shape, filters.dtype),
            pltpu.VMEM(w_up.shape, w_up.dtype),
            pltpu.VMEM(w_energy.shape, w_energy.dtype),
            pltpu.SemaphoreType.DMA((4,)),
        ] + [pltpu.VMEM((z.rad * z.slots, most * LANES), jnp.bfloat16)] * by,
        compiler_params=pltpu.CompilerParams(vmem_limit_bytes=12 * 1024 * 1024),
        cost_estimate=pl.CostEstimate(flops=flops, bytes_accessed=1 << 20, transcendentals=0),
    )(near, *in_hbm(embed, filters, w_up, w_energy))


def far_layer(z, region, *near):
    width = near[0].shape[1]
    cells, anchors = z.block[0] * z.block[1], z.nax * z.nay
    columns = z.nx * z.ny * z.groups
    return pl.pallas_call(
        functools.partial(far_kernel, z),
        out_shape=(
            jax.ShapeDtypeStruct(z.block + (1, z.slots), jnp.float32),
            jax.ShapeDtypeStruct(z.block + (1, 3 * z.slots), jnp.float32),
            jax.ShapeDtypeStruct((z.groups,) + z.block + (1, 3 * z.slots), jnp.float32),
        ),
        in_specs=[VMEM] * (1 + len(near)),
        out_specs=[VMEM] * 3,
        scratch_shapes=[
            pltpu.VMEM((z.nx * 2 * HALO * z.groups, z.spec, LANES), jnp.bfloat16),
            pltpu.VMEM((z.nax * 2, 4, z.slots, LANES), jnp.float32),
            pltpu.VMEM((anchors, len(z.offsets), 2, z.slots, LANES), jnp.float32),
            pltpu.VMEM((4, LANES, LANES), jnp.float32),
            pltpu.VMEM((anchors, z.rad * z.slots, 2 * z.spec), jnp.bfloat16),
            pltpu.VMEM((anchors, 2 * z.slots, z.rad * z.spec), jnp.bfloat16),
            pltpu.VMEM((anchors, z.slots, width), jnp.bfloat16),
            pltpu.VMEM((columns, 3, 8, LANES), jnp.float32),
            pltpu.VMEM((cells, 3, z.slots, LANES), jnp.float32),
        ] + [pltpu.VMEM((z.rad * z.slots, len(z.offsets) * LANES), jnp.bfloat16)] * z.nay,
        compiler_params=pltpu.CompilerParams(vmem_limit_bytes=FAR_VMEM),
    )(region, *near)


def on_device(positions, species, counts, embed, filters, w_up, w_energy):
    bx, by = positions.shape[:2]
    slots = species.shape[-1]
    width = embed.shape[1]
    depth = lax.axis_size("gz")
    merged = depth * positions.shape[2] == 2
    spec = -(-embed.shape[0] // LANES) * LANES
    z = Cells((bx, by), merged, filters.shape[1] // width, spec, slots)
    block = pack(positions, species, counts.reshape(bx, by))
    upward = [(i, (i + 1) % depth) for i in range(depth)]
    downward = [(b, a) for a, b in upward]
    low = lax.ppermute(block, "gz", upward)
    if merged:
        block = jnp.concatenate([block, low], axis=3)
    else:
        high = lax.ppermute(block, "gz", downward)
        empty = jnp.full_like(block, -1.0)
        block = jnp.concatenate(
            [jnp.concatenate([block, low], axis=3), jnp.concatenate([high, empty], axis=3)], axis=2
        )
    block = exchange(block, "gx", 0, HALO)
    near = near_layer(z, block, embed, filters, w_up, w_energy.reshape(1, width))
    region = exchange(block, "gy", 1, HALO)
    energies, own, other = far_layer(z, region, *near)

    forces = own + lax.ppermute(other[0], "gz", downward)
    if not merged:
        forces = forces + lax.ppermute(other[1], "gz", upward)
    return energies, forces


def solution(mesh):
    in_specs = (
        P("gx", "gy", "gz", None),
        P("gx", "gy", "gz", None),
        P("gx", "gy", "gz"),
        P(),
        P(),
        P(),
        P(),
    )
    out_specs = (P("gx", "gy", "gz", None), P("gx", "gy", "gz", None))
    return jax.shard_map(
        on_device, mesh=mesh, in_specs=in_specs, out_specs=out_specs, check_vma=False
    )
```

```python
import functools

import jax
import jax.numpy as jnp
from jax import lax
from jax.experimental import pallas as pl
from jax.experimental.pallas import tpu as pltpu
from jax.sharding import PartitionSpec as P

MSG_SCALE = 0.1
HALO = 2
FAR_VMEM = 36 * 1024 * 1024
LANES = 128
STEP = 16
WIDE = 4
BATCH = 4
LOG2E = 1.4426950408889634
NT = (((1,), (1,)), ((), ()))
NN = (((1,), (0,)), ((), ()))


def exchange(block, axis, dim, width):
    count = lax.axis_size(axis)
    first = lax.slice_in_dim(block, 0, width, axis=dim)
    last = lax.slice_in_dim(block, block.shape[dim] - width, None, axis=dim)
    if count % 2 == 0:
        odd = lax.axis_index(axis) % 2 == 1
        whole = block.shape[dim] == width
        up = block if whole else jnp.where(odd, last, first)
        down = block if whole else jnp.where(odd, first, last)
        far = [(i, (i + 1) % count if i % 2 else (i - 1) % count) for i in range(count)]
        near = [(i, i - 1 if i % 2 else i + 1) for i in range(count)]
        from_far = lax.ppermute(up, axis, far)
        from_near = lax.ppermute(down, axis, near)
        low = jnp.where(odd, from_near, from_far)
        high = jnp.where(odd, from_far, from_near)
    else:
        forward = [(i, (i + 1) % count) for i in range(count)]
        low = lax.ppermute(last, axis, forward)
        high = lax.ppermute(first, axis, [(b, a) for a, b in forward])
    return jnp.concatenate([low, block, high], axis=dim)


def dot(a, b, dims, precision=None):
    return lax.dot_general(a, b, dims, precision=precision, preferred_element_type=jnp.float32)


def split(values):
    high = values.astype(jnp.bfloat16)
    return high, (values - high.astype(jnp.float32)).astype(jnp.bfloat16)


def thirds(rows):
    high = rows.astype(jnp.bfloat16)
    middle, low = split(rows - high.astype(jnp.float32))
    at = lax.broadcasted_iota(jnp.int32, rows.shape, 0)
    parts = [part.astype(jnp.float32) for part in (high, middle, low)]
    kept = jnp.where(at == 0, parts[0], jnp.where(at == 1, parts[1], jnp.where(at == 2, parts[2], 0.0)))
    return kept.astype(jnp.bfloat16)


class Cells:
    def __init__(self, block, merged, rad, spec, slots):
        self.block, self.merged, self.rad, self.spec, self.slots = block, merged, rad, spec, slots
        self.groups = 1 if merged else 2
        self.nax, self.nay = block[0] + 2, block[1] + 2
        self.nx, self.ny = block[0] + 2 * HALO, block[1] + 2 * HALO
        self.offsets = [
            (dx, dy, g) for dx in (-1, 0, 1) for dy in (-1, 0, 1) for g in range(self.groups)
        ]
        self.rows = [slice(r, r + STEP) for r in range(0, slots, STEP)]

    def inner(self, ay):
        return 1 <= ay <= self.block[1]

    def split_offsets(self, ay):
        near = [n for n, (_, dy, _) in enumerate(self.offsets) if self.inner(ay) and self.inner(ay + dy)]
        return near, [n for n in range(len(self.offsets)) if n not in near]

    def z_shift(self, g):
        lane = lax.broadcasted_iota(jnp.int32, (1, LANES), 1)
        if self.merged:
            return jnp.where(lane < self.slots, 0.0, 1.0)
        if g == 0:
            return jnp.where(lane < self.slots, 0.0, -1.0)
        return jnp.where(lane < self.slots, 1.0, 0.0)


def place_anchors(z, stage, rows, out):
    for q in range(4):
        for i, (ref, x, y) in enumerate(rows):
            stage[q, i:i + 1, :] = ref[x, y, q:q + 1, :]
        columns = stage[q].T
        for i in range(len(rows)):
            out[i, q] = jnp.broadcast_to(columns[0:z.slots, i:i + 1], (z.slots, LANES))


def place_onehot(z, ref, x, y, g, out, at):
    ids = lax.broadcasted_iota(jnp.int32, (z.spec, LANES), 0).astype(jnp.float32)
    out[at] = (ref[x, y, g * 4 + 3:g * 4 + 4, :] == ids).astype(jnp.bfloat16)


def target(ref, x, y, offset):
    dx, dy, g = offset
    row = ref[x, y, g * 4:g * 4 + 3, :]
    return row[0:1] + dx, row[1:2] + dy, row[2:3]


def weigh(z, position, anchor, offset, buffer, lanes, keep):
    tx, ty, tz = position
    shift = z.z_shift(offset[2])
    for c in z.rows:
        ex = tx - anchor[0, c, :]
        ey = ty - anchor[1, c, :]
        dz = tz - anchor[2, c, :]
        ez = jnp.abs(dz) - shift if z.merged else dz + shift
        s = ex * ex + ey * ey + ez * ez
        f = jnp.maximum(1.0 - s, 0.0)
        e = jnp.exp2(s * (-0.5 * LOG2E))
        keep[0, c, :] = f
        keep[1, c, :] = e
        f = f * f
        if offset == (0, 0, 0):
            row = lax.broadcasted_iota(jnp.int32, (STEP, LANES), 0) + c.start
            lane = lax.broadcasted_iota(jnp.int32, (STEP, LANES), 1)
            f = jnp.where(row == lane, 0.0, f)
        for k in range(z.rad):
            if k == 0:
                w = e * f
                e = e * e
            elif k == 1:
                w = w * e
            else:
                e = e * e * e
                w = w * e
            buffer[k * z.slots + c.start:k * z.slots + c.stop, lanes] = w.astype(jnp.bfloat16)


def pack_kernel(counts_hbm, positions_hbm, species_hbm, out, counts, positions, species, arrived):
    arguments = [(counts_hbm, counts), (positions_hbm, positions), (species_hbm, species)]
    copies = [pltpu.make_async_copy(a, b, arrived.at[i]) for i, (a, b) in enumerate(arguments)]
    for copy in copies:
        copy.start()
    for copy in copies:
        copy.wait()
    slots = out.shape[3]
    lane = lax.broadcasted_iota(jnp.int32, (1, slots), 1)
    for x in range(out.shape[0]):
        for y in range(out.shape[1]):
            row = positions[x, y, 0:1, :]
            for q in range(3):
                out[x, y, q:q + 1, :] = row[:, q * slots:(q + 1) * slots]
            marked = jnp.where(lane < counts[x, y], species[x, y, 0:1, :], -1)
            out[x, y, 3:4, :] = marked.astype(jnp.float32)


def near_kernel(
    z, near, embed_hbm, filters_hbm, w_up_hbm, w_energy_hbm,
    table, readout, emb_energy, onehot, anchors, sums, kept,
    emb_pad, stage, embed, filters, w_up, w_energy, arrived, *buffers,
):
    nspec, width = embed.shape
    by = z.block[1]
    weights = [(embed_hbm, embed), (filters_hbm, filters), (w_up_hbm, w_up), (w_energy_hbm, w_energy)]
    copies = [pltpu.make_async_copy(a, b, arrived.at[i]) for i, (a, b) in enumerate(weights)]
    for copy in copies:
        copy.start()

    for x in range(z.nx):
        for y in range(by):
            for g in range(z.groups):
                place_onehot(z, near, x, y, g, onehot, (x * by + y) * z.groups + g)
    place_anchors(z, stage, [(near, ax + 1, y) for ax in range(z.nax) for y in range(by)], anchors)

    def message_at(ax, carry):
        for y in range(by):
            a = ax * by + y
            some = z.split_offsets(y + 1)[0]
            hots = []
            for i, n in enumerate(some):
                dx, dy, g = z.offsets[n]
                spot = target(near, ax + 1 + dx, y + dy, z.offsets[n])
                weigh(
                    z, spot, anchors.at[a], z.offsets[n], buffers[y],
                    slice(i * LANES, (i + 1) * LANES), kept.at[a, i],
                )
                hots.append(onehot[((ax + 1 + dx) * by + y + dy) * z.groups + g])
            weights = buffers[y][:, 0:len(some) * LANES]
            sums[a] = dot(weights, jnp.concatenate(hots, axis=1), NT)
        return carry

    lax.fori_loop(0, z.nax, message_at, 0)

    for copy in copies:
        copy.wait()
    emb_pad[...] = jnp.zeros_like(emb_pad)
    emb_pad[0:nspec, :] = embed[...].astype(jnp.float32)
    emb = emb_pad[...]
    rows = dot(emb.astype(jnp.bfloat16), filters[...], NN).astype(jnp.bfloat16)
    for k in range(z.rad):
        table[k * z.spec:(k + 1) * z.spec, :] = rows[:, k * width:(k + 1) * width]
    energy_row = jnp.broadcast_to(w_energy[...], (8, width))
    readout[...] = dot(energy_row, w_up[...].astype(jnp.float32), NT, lax.Precision.HIGHEST)
    emb_energy[...] = dot(energy_row, emb, NT, lax.Precision.HIGHEST)


def far_kernel(
    z, region, table, readout_ref, emb_energy_ref, onehot_near, anchors_near, sums_near, kept_near,
    energies, own, other,
    onehot_far, anchors_far, kept_far, stage, adj_table, mixed, act, back, mine, *buffers,
):
    by = z.block[1]
    bf = jnp.bfloat16
    slots, spec, rad = z.slots, z.spec, z.rad
    readout = readout_ref[...]
    outer = [y for y in range(z.ny) if not HALO <= y < HALO + by]

    for x in range(z.nx):
        for i, y in enumerate(outer):
            for g in range(z.groups):
                place_onehot(z, region, x, y, g, onehot_far, (x * len(outer) + i) * z.groups + g)
    place_anchors(
        z, stage, [(region, ax + 1, y) for ax in range(z.nax) for y in (1, z.ny - HALO)], anchors_far
    )

    def onehot_at(x, y, g):
        if y in outer:
            return onehot_far[(x * len(outer) + outer.index(y)) * z.groups + g]
        return onehot_near[(x * by + y - HALO) * z.groups + g]

    def anchor_at(ax, ay):
        if z.inner(ay):
            return anchors_near.at[ax * by + ay - 1]
        return anchors_far.at[ax * 2 + (ay > 0)]

    def kept_at(ax, ay, n):
        near, _ = z.split_offsets(ay)
        if n in near:
            return kept_near.at[ax * by + ay - 1, near.index(n)]
        return kept_far.at[ax * z.nay + ay, n]

    def message_at(ax, carry):
        for ay in range(z.nay):
            a = ax * z.nay + ay
            some = z.split_offsets(ay)[1]
            hots = []
            for i, n in enumerate(some):
                dx, dy, g = z.offsets[n]
                x, y = ax + 1 + dx, ay + 1 + dy
                weigh(
                    z, target(region, x, y, z.offsets[n]), anchor_at(ax, ay), z.offsets[n], buffers[ay],
                    slice(i * LANES, (i + 1) * LANES), kept_at(ax, ay, n),
                )
                hots.append(onehot_at(x, y, g))
            total = sums_near[ax * by + ay - 1] if z.inner(ay) else None
            if some:
                term = dot(buffers[ay][:, 0:len(some) * LANES], jnp.concatenate(hots, axis=1), NT)
                total = term if total is None else total + term
            for k in range(rad):
                mixed[a, :, k * spec:(k + 1) * spec] = total[k * slots:(k + 1) * slots].astype(bf)
        return carry

    lax.fori_loop(0, z.nax, message_at, 0)

    def adjoint_of(group):
        cells = [ax * z.nay + ay for ax, ay in group]
        messages = dot(jnp.concatenate([mixed[a] for a in cells], axis=0), table[...], NN)
        adjoints = []
        for i, (a, spot) in enumerate(zip(cells, group)):
            message = MSG_SCALE * messages[i * slots:(i + 1) * slots]
            sigmoid = 1.0 / (1.0 + jnp.exp(-message))
            act[a] = (message * sigmoid).astype(bf)
            slope = sigmoid * (1.0 + message * (1.0 - sigmoid)) * readout[0:1]
            adjoints.append(jnp.where(anchor_at(*spot)[3] >= 0.0, slope, 0.0).astype(bf))
        turned = dot(jnp.concatenate(adjoints, axis=0), table[...], NT)
        for i, a in enumerate(cells):
            for r, c in enumerate(z.rows):
                high, low = split(turned[slots * i + c.start:slots * i + c.stop])
                for k in range(rad):
                    at = slice((r * rad + k) * STEP, (r * rad + k + 1) * STEP)
                    adj_table[a, at, 0:spec] = high[:, k * spec:(k + 1) * spec]
                    adj_table[a, at, spec:] = low[:, k * spec:(k + 1) * spec]

    for first in range(0, z.nax, BATCH):
        adjoint_of([(ax, ay) for ax in range(first, min(first + BATCH, z.nax)) for ay in range(z.nay)])

    def pairs(ax, ay, n, gains, r):
        c = z.rows[r]
        dx, dy, g = z.offsets[n]
        tx, ty, tz = target(region, ax + 1 + dx, ay + 1 + dy, z.offsets[n])
        anchor, keep = anchor_at(ax, ay), kept_at(ax, ay, n)
        ex = tx - anchor[0, c, :]
        ey = ty - anchor[1, c, :]
        ez = tz - anchor[2, c, :]
        shift = z.z_shift(g)
        ez = ez + jnp.where(ez > 0.0, -shift, shift) if z.merged else ez + shift
        f = keep[0, c, :]
        e = keep[1, c, :]
        e2 = e * e
        plain = None
        for k in range(rad):
            if k == 1:
                e = e * e2
            elif k > 1:
                e2 = e2 * e2 * e2
                e = e * e2
            term = e * gains[k * STEP:(k + 1) * STEP]
            scaled = (0.25 * 3.0 ** k) * term
            plain, steep = (term, scaled) if plain is None else (plain + term, steep + scaled)
        return f * (f * steep + plain), (ex, ey, ez)

    def blocks(ax, ay, some, sums):
        a = ax * z.nay + ay
        for first in range(0, len(some), WIDE):
            part = some[first:first + WIDE]
            spots = [(ax + 1 + z.offsets[n][0], ay + 1 + z.offsets[n][1], z.offsets[n][2]) for n in part]
            hots = jnp.concatenate([onehot_at(*spot) for spot in spots], axis=1)
            hots = jnp.concatenate([hots, hots], axis=0)
            totals = [[None] * 3 for _ in part]
            gains = dot(adj_table[a], hots, NN)
            for r in range(len(z.rows)):
                some_gains = gains[r * rad * STEP:(r + 1) * rad * STEP]
                for i, n in enumerate(part):
                    p, displace = pairs(ax, ay, n, some_gains[:, i * LANES:(i + 1) * LANES], r)
                    for q in range(3):
                        term = p * displace[q]
                        if sums is not None:
                            sums[q][r] = term if sums[q][r] is None else sums[q][r] + term
                        term = sum(term[j:j + 8] for j in range(8, STEP, 8)) + term[0:8]
                        totals[i][q] = term if totals[i][q] is None else totals[i][q] + term
            for (x, y, g), total in zip(spots, totals):
                for q in range(3):
                    back[(x * z.ny + y) * z.groups + g, q] += total[q]

    back[...] = jnp.zeros_like(back)

    def forces_at(ox, carry):
        for oy in range(by):
            sums = [[None] * len(z.rows) for _ in range(3)]
            blocks(ox + 1, oy + 1, range(len(z.offsets)), sums)
            for q in range(3):
                for r, c in enumerate(z.rows):
                    mine[ox * by + oy, q, c, :] = sums[q][r]
        return carry

    lax.fori_loop(0, z.block[0], forces_at, 0)

    for ax in range(z.nax):
        for ay in range(z.nay):
            if 0 < ax < z.nax - 1 and z.inner(ay):
                continue
            blocks(ax, ay, [
                n for n, (dx, dy, _) in enumerate(z.offsets) if 0 < ax + dx < z.nax - 1 and z.inner(ay + dy)
            ], None)

    scale = -4.0 * MSG_SCALE
    cells = [(ox, oy) for ox in range(z.block[0]) for oy in range(by)]
    high, low = split(mine[...].reshape(len(cells) * 3 * slots, LANES))
    ones = jnp.ones((8, 2 * LANES), bf)
    rows = dot(ones, jnp.concatenate([high, low], axis=1), NT)[0:1]
    for o, (ox, oy) in enumerate(cells):
        column = ((ox + HALO) * z.ny + oy + HALO) * z.groups
        sums = [jnp.sum(back[column, q], axis=0, keepdims=True)[:, 0:slots] for q in range(3)]
        for q in range(3):
            at = (o * 3 + q) * slots
            own[ox, oy, :, q * slots:(q + 1) * slots] = scale * (rows[:, at:at + slots] - sums[q])
        for g in range(z.groups):
            start = slots if g == 0 else 0
            for q in range(3):
                row = jnp.sum(back[column + g, q], axis=0, keepdims=True)
                other[g, ox, oy, :, q * slots:(q + 1) * slots] = -scale * row[:, start:start + slots]

    hots = jnp.concatenate([onehot_at(ox + HALO, oy + HALO, 0)[:, 0:slots] for ox, oy in cells], axis=1)
    acts = jnp.concatenate([act[(ox + 1) * z.nay + oy + 1] for ox, oy in cells], axis=0)
    energy = dot(thirds(emb_energy_ref[...]), hots, NN) + dot(thirds(readout), acts, NT)
    energy = jnp.sum(energy, axis=0, keepdims=True)
    for o, (ox, oy) in enumerate(cells):
        marked = region[ox + HALO, oy + HALO, 3:4, 0:slots]
        energies[ox, oy, :, :] = jnp.where(marked >= 0.0, energy[:, o * slots:(o + 1) * slots], 0.0)


VMEM = pl.BlockSpec(memory_space=pltpu.VMEM)
HBM = pl.BlockSpec(memory_space=pltpu.HBM)


def in_hbm(*arrays):
    return [pltpu.with_memory_space_constraint(array, pltpu.HBM) for array in arrays]


def pack(positions, species, counts):
    bx, by, _, slots = species.shape
    return pl.pallas_call(
        pack_kernel,
        out_shape=jax.ShapeDtypeStruct((bx, by, 4, slots), jnp.float32),
        in_specs=[HBM] * 3,
        out_specs=VMEM,
        scratch_shapes=[
            pltpu.SMEM(counts.shape, counts.dtype),
            pltpu.VMEM(positions.shape, positions.dtype),
            pltpu.VMEM(species.shape, species.dtype),
            pltpu.SemaphoreType.DMA((3,)),
        ],
        compiler_params=pltpu.CompilerParams(vmem_limit_bytes=1024 * 1024),
    )(*in_hbm(counts, positions, species))


def near_layer(z, near, embed, filters, w_up, w_energy):
    width = embed.shape[1]
    by = z.block[1]
    cells, most = z.nax * by, max(len(z.split_offsets(y + 1)[0]) for y in range(by))
    shapes = [
        ((z.rad * z.spec, width), jnp.bfloat16),
        ((8, width), jnp.float32),
        ((8, z.spec), jnp.float32),
        ((z.nx * by * z.groups, z.spec, LANES), jnp.bfloat16),
        ((cells, 4, z.slots, LANES), jnp.float32),
        ((cells, z.rad * z.slots, z.spec), jnp.float32),
        ((cells, most, 2, z.slots, LANES), jnp.float32),
    ]
    flops = 2 * cells * most * z.rad * z.slots * LANES * z.spec
    return pl.pallas_call(
        functools.partial(near_kernel, z),
        out_shape=[jax.ShapeDtypeStruct(*shape) for shape in shapes],
        in_specs=[VMEM] + [HBM] * 4,
        out_specs=[VMEM] * len(shapes),
        scratch_shapes=[
            pltpu.VMEM((z.spec, width), jnp.float32),
            pltpu.VMEM((4, LANES, LANES), jnp.float32),
            pltpu.VMEM(embed.shape, embed.dtype),
            pltpu.VMEM(filters.shape, filters.dtype),
            pltpu.VMEM(w_up.shape, w_up.dtype),
            pltpu.VMEM(w_energy.shape, w_energy.dtype),
            pltpu.SemaphoreType.DMA((4,)),
        ] + [pltpu.VMEM((z.rad * z.slots, most * LANES), jnp.bfloat16)] * by,
        compiler_params=pltpu.CompilerParams(vmem_limit_bytes=12 * 1024 * 1024),
        cost_estimate=pl.CostEstimate(flops=flops, bytes_accessed=1 << 20, transcendentals=0),
    )(near, *in_hbm(embed, filters, w_up, w_energy))


def far_layer(z, region, *near):
    width = near[0].shape[1]
    cells, anchors = z.block[0] * z.block[1], z.nax * z.nay
    columns = z.nx * z.ny * z.groups
    return pl.pallas_call(
        functools.partial(far_kernel, z),
        out_shape=(
            jax.ShapeDtypeStruct(z.block + (1, z.slots), jnp.float32),
            jax.ShapeDtypeStruct(z.block + (1, 3 * z.slots), jnp.float32),
            jax.ShapeDtypeStruct((z.groups,) + z.block + (1, 3 * z.slots), jnp.float32),
        ),
        in_specs=[VMEM] * (1 + len(near)),
        out_specs=[VMEM] * 3,
        scratch_shapes=[
            pltpu.VMEM((z.nx * 2 * HALO * z.groups, z.spec, LANES), jnp.bfloat16),
            pltpu.VMEM((z.nax * 2, 4, z.slots, LANES), jnp.float32),
            pltpu.VMEM((anchors, len(z.offsets), 2, z.slots, LANES), jnp.float32),
            pltpu.VMEM((4, LANES, LANES), jnp.float32),
            pltpu.VMEM((anchors, z.rad * z.slots, 2 * z.spec), jnp.bfloat16),
            pltpu.VMEM((anchors, z.slots, z.rad * z.spec), jnp.bfloat16),
            pltpu.VMEM((anchors, z.slots, width), jnp.bfloat16),
            pltpu.VMEM((columns, 3, 8, LANES), jnp.float32),
            pltpu.VMEM((cells, 3, z.slots, LANES), jnp.float32),
        ] + [pltpu.VMEM((z.rad * z.slots, len(z.offsets) * LANES), jnp.bfloat16)] * z.nay,
        compiler_params=pltpu.CompilerParams(vmem_limit_bytes=FAR_VMEM),
    )(region, *near)


def on_device(positions, species, counts, embed, filters, w_up, w_energy):
    bx, by = positions.shape[:2]
    slots = species.shape[-1]
    width = embed.shape[1]
    depth = lax.axis_size("gz")
    merged = depth * positions.shape[2] == 2
    spec = -(-embed.shape[0] // LANES) * LANES
    z = Cells((bx, by), merged, filters.shape[1] // width, spec, slots)
    block = pack(positions, species, counts.reshape(bx, by))
    upward = [(i, (i + 1) % depth) for i in range(depth)]
    downward = [(b, a) for a, b in upward]
    low = lax.ppermute(block, "gz", upward)
    if merged:
        block = jnp.concatenate([block, low], axis=3)
    else:
        high = lax.ppermute(block, "gz", downward)
        empty = jnp.full_like(block, -1.0)
        block = jnp.concatenate(
            [jnp.concatenate([block, low], axis=3), jnp.concatenate([high, empty], axis=3)], axis=2
        )
    block = exchange(block, "gx", 0, HALO)
    near = near_layer(z, block, embed, filters, w_up, w_energy.reshape(1, width))
    region = exchange(block, "gy", 1, HALO)
    energies, own, other = far_layer(z, region, *near)

    forces = own + lax.ppermute(other[0], "gz", downward)
    if not merged:
        forces = forces + lax.ppermute(other[1], "gz", upward)
    return energies, forces


def solution(mesh):
    in_specs = (
        P("gx", "gy", "gz", None),
        P("gx", "gy", "gz", None),
        P("gx", "gy", "gz"),
        P(),
        P(),
        P(),
        P(),
    )
    out_specs = (P("gx", "gy", "gz", None), P("gx", "gy", "gz", None))
    return jax.shard_map(
        on_device, mesh=mesh, in_specs=in_specs, out_specs=out_specs, check_vma=False
    )
```

```python
import functools

import jax
import jax.numpy as jnp
from jax import lax
from jax.experimental import pallas as pl
from jax.experimental.pallas import tpu as pltpu
from jax.sharding import PartitionSpec as P

MSG_SCALE = 0.1
HALO = 2
FAR_VMEM = 30 * 1024 * 1024
OWN_VMEM = 8 * 1024 * 1024
LANES = 128
STEP = 16
WIDE = 4
BATCH = 4
FORCE_SCALE = 4.0 * MSG_SCALE
LOG2E = 1.4426950408889634
NT = (((1,), (1,)), ((), ()))
NN = (((1,), (0,)), ((), ()))


def exchange(block, axis, dim, width):
    count = lax.axis_size(axis)
    first = lax.slice_in_dim(block, 0, width, axis=dim)
    last = lax.slice_in_dim(block, block.shape[dim] - width, None, axis=dim)
    if count % 2 == 0:
        odd = lax.axis_index(axis) % 2 == 1
        whole = block.shape[dim] == width
        up = block if whole else jnp.where(odd, last, first)
        down = block if whole else jnp.where(odd, first, last)
        far = [(i, (i + 1) % count if i % 2 else (i - 1) % count) for i in range(count)]
        near = [(i, i - 1 if i % 2 else i + 1) for i in range(count)]
        from_far = lax.ppermute(up, axis, far)
        from_near = lax.ppermute(down, axis, near)
        low = jnp.where(odd, from_near, from_far)
        high = jnp.where(odd, from_far, from_near)
    else:
        forward = [(i, (i + 1) % count) for i in range(count)]
        low = lax.ppermute(last, axis, forward)
        high = lax.ppermute(first, axis, [(b, a) for a, b in forward])
    return jnp.concatenate([low, block, high], axis=dim)


def dot(a, b, dims, precision=None):
    return lax.dot_general(a, b, dims, precision=precision, preferred_element_type=jnp.float32)


def split(values):
    high = values.astype(jnp.bfloat16)
    return high, (values - high.astype(jnp.float32)).astype(jnp.bfloat16)


def thirds(rows):
    high = rows.astype(jnp.bfloat16)
    middle, low = split(rows - high.astype(jnp.float32))
    at = lax.broadcasted_iota(jnp.int32, rows.shape, 0)
    parts = [part.astype(jnp.float32) for part in (high, middle, low)]
    kept = jnp.where(at == 0, parts[0], jnp.where(at == 1, parts[1], jnp.where(at == 2, parts[2], 0.0)))
    return kept.astype(jnp.bfloat16)


class Cells:
    def __init__(self, block, merged, rad, spec, slots):
        self.block, self.merged, self.rad, self.spec, self.slots = block, merged, rad, spec, slots
        self.groups = 1 if merged else 2
        self.nax, self.nay = block[0] + 2, block[1] + 2
        self.nx, self.ny = block[0] + 2 * HALO, block[1] + 2 * HALO
        self.offsets = [
            (dx, dy, g) for dx in (-1, 0, 1) for dy in (-1, 0, 1) for g in range(self.groups)
        ]
        self.rows = [slice(r, r + STEP) for r in range(0, slots, STEP)]

    def inner(self, ay):
        return 1 <= ay <= self.block[1]

    def cell(self, ax, ay):
        if 1 <= ax <= self.block[0] and self.inner(ay):
            return (ax - 1) * self.block[1] + ay - 1
        return None

    def split_offsets(self, ay):
        near = [n for n, (_, dy, _) in enumerate(self.offsets) if self.inner(ay) and self.inner(ay + dy)]
        return near, [n for n in range(len(self.offsets)) if n not in near]

    def z_shift(self, g):
        lane = lax.broadcasted_iota(jnp.int32, (1, LANES), 1)
        if self.merged:
            return jnp.where(lane < self.slots, 0.0, 1.0)
        if g == 0:
            return jnp.where(lane < self.slots, 0.0, -1.0)
        return jnp.where(lane < self.slots, 1.0, 0.0)


def place_anchors(z, stage, rows, out):
    for q in range(4):
        for i, (ref, x, y) in enumerate(rows):
            stage[q, i:i + 1, :] = ref[x, y, q:q + 1, :]
        columns = stage[q].T
        for i in range(len(rows)):
            out[i, q] = jnp.broadcast_to(columns[0:z.slots, i:i + 1], (z.slots, LANES))


def place_onehot(z, ref, x, y, g, out, at):
    ids = lax.broadcasted_iota(jnp.int32, (z.spec, LANES), 0).astype(jnp.float32)
    out[at] = (ref[x, y, g * 4 + 3:g * 4 + 4, :] == ids).astype(jnp.bfloat16)


def target(ref, x, y, offset):
    dx, dy, g = offset
    row = ref[x, y, g * 4:g * 4 + 3, :]
    return row[0:1] + dx, row[1:2] + dy, row[2:3]


def weigh(z, position, anchor, offset, buffer, lanes, keep):
    tx, ty, tz = position
    shift = z.z_shift(offset[2])
    for c in z.rows:
        ex = tx - anchor[0, c, :]
        ey = ty - anchor[1, c, :]
        dz = tz - anchor[2, c, :]
        ez = jnp.abs(dz) - shift if z.merged else dz + shift
        s = ex * ex + ey * ey + ez * ez
        f = jnp.maximum(1.0 - s, 0.0)
        e = jnp.exp2(s * (-0.5 * LOG2E))
        keep[0, c, :] = f
        keep[1, c, :] = e
        f = f * f
        if offset == (0, 0, 0):
            row = lax.broadcasted_iota(jnp.int32, (STEP, LANES), 0) + c.start
            lane = lax.broadcasted_iota(jnp.int32, (STEP, LANES), 1)
            f = jnp.where(row == lane, 0.0, f)
        for k in range(z.rad):
            if k == 0:
                w = e * f
                e = e * e
            elif k == 1:
                w = w * e
            else:
                e = e * e * e
                w = w * e
            buffer[k * z.slots + c.start:k * z.slots + c.stop, lanes] = w.astype(jnp.bfloat16)


def pack_kernel(counts_hbm, positions_hbm, species_hbm, out, counts, positions, species, arrived):
    arguments = [(counts_hbm, counts), (positions_hbm, positions), (species_hbm, species)]
    copies = [pltpu.make_async_copy(a, b, arrived.at[i]) for i, (a, b) in enumerate(arguments)]
    for copy in copies:
        copy.start()
    for copy in copies:
        copy.wait()
    slots = out.shape[3]
    lane = lax.broadcasted_iota(jnp.int32, (1, slots), 1)
    for x in range(out.shape[0]):
        for y in range(out.shape[1]):
            row = positions[x, y, 0:1, :]
            for q in range(3):
                out[x, y, q:q + 1, :] = row[:, q * slots:(q + 1) * slots]
            marked = jnp.where(lane < counts[x, y], species[x, y, 0:1, :], -1)
            out[x, y, 3:4, :] = marked.astype(jnp.float32)


def near_kernel(
    z, near, embed_hbm, filters_hbm, w_up_hbm, w_energy_hbm,
    table, readout, emb_energy, onehot, anchors, sums, kept,
    emb_pad, stage, embed, filters, w_up, w_energy, arrived, *buffers,
):
    nspec, width = embed.shape
    by = z.block[1]
    weights = [(embed_hbm, embed), (filters_hbm, filters), (w_up_hbm, w_up), (w_energy_hbm, w_energy)]
    copies = [pltpu.make_async_copy(a, b, arrived.at[i]) for i, (a, b) in enumerate(weights)]
    for copy in copies:
        copy.start()

    for x in range(z.nx):
        for y in range(by):
            for g in range(z.groups):
                place_onehot(z, near, x, y, g, onehot, (x * by + y) * z.groups + g)
    place_anchors(z, stage, [(near, ax + 1, y) for ax in range(z.nax) for y in range(by)], anchors)

    def message_at(ax, carry):
        for y in range(by):
            a = ax * by + y
            some = z.split_offsets(y + 1)[0]
            hots = []
            for i, n in enumerate(some):
                dx, dy, g = z.offsets[n]
                spot = target(near, ax + 1 + dx, y + dy, z.offsets[n])
                weigh(
                    z, spot, anchors.at[a], z.offsets[n], buffers[y],
                    slice(i * LANES, (i + 1) * LANES), kept.at[a, i],
                )
                hots.append(onehot[((ax + 1 + dx) * by + y + dy) * z.groups + g])
            weights = buffers[y][:, 0:len(some) * LANES]
            sums[a] = dot(weights, jnp.concatenate(hots, axis=1), NT)
        return carry

    lax.fori_loop(0, z.nax, message_at, 0)

    for copy in copies:
        copy.wait()
    emb_pad[...] = jnp.zeros_like(emb_pad)
    emb_pad[0:nspec, :] = embed[...].astype(jnp.float32)
    emb = emb_pad[...]
    rows = dot(emb.astype(jnp.bfloat16), filters[...], NN).astype(jnp.bfloat16)
    for k in range(z.rad):
        table[k * z.spec:(k + 1) * z.spec, :] = rows[:, k * width:(k + 1) * width]
    energy_row = jnp.broadcast_to(w_energy[...], (8, width))
    readout[...] = dot(energy_row, w_up[...].astype(jnp.float32), NT, lax.Precision.HIGHEST)
    emb_energy[...] = dot(energy_row, emb, NT, lax.Precision.HIGHEST)


class Store:
    def __init__(self, z, onehot_near, onehot_far, anchors_near, anchors_far, kept_near, kept_own, kept_far):
        self.z = z
        self.onehots = (onehot_near, onehot_far)
        self.anchors = (anchors_near, anchors_far)
        self.kept = (kept_near, kept_own, kept_far)
        self.outer = [y for y in range(z.ny) if not HALO <= y < HALO + z.block[1]]

    def onehot(self, x, y, g):
        z = self.z
        if y in self.outer:
            return self.onehots[1][(x * len(self.outer) + self.outer.index(y)) * z.groups + g]
        return self.onehots[0][(x * z.block[1] + y - HALO) * z.groups + g]

    def anchor(self, ax, ay):
        if self.z.inner(ay):
            return self.anchors[0].at[ax * self.z.block[1] + ay - 1]
        return self.anchors[1].at[ax * 2 + (ay > 0)]

    def radial(self, ax, ay, n):
        if not self.z.inner(ay):
            return self.kept[2].at[ax * 2 + (ay > 0), n]
        near, far = self.z.split_offsets(ay)
        if n in near:
            return self.kept[0].at[ax * self.z.block[1] + ay - 1, near.index(n)]
        return self.kept[1].at[ax * self.z.block[1] + ay - 1, far.index(n)]


def pairs(z, store, region, ax, ay, n, gains, r):
    c = z.rows[r]
    dx, dy, g = z.offsets[n]
    tx, ty, tz = target(region, ax + 1 + dx, ay + 1 + dy, z.offsets[n])
    anchor, keep = store.anchor(ax, ay), store.radial(ax, ay, n)
    ex = tx - anchor[0, c, :]
    ey = ty - anchor[1, c, :]
    ez = tz - anchor[2, c, :]
    shift = z.z_shift(g)
    ez = ez + jnp.where(ez > 0.0, -shift, shift) if z.merged else ez + shift
    f = keep[0, c, :]
    e = keep[1, c, :]
    e2 = e * e
    plain = None
    for k in range(z.rad):
        if k == 1:
            e = e * e2
        elif k > 1:
            e2 = e2 * e2 * e2
            e = e * e2
        term = e * gains[k * STEP:(k + 1) * STEP]
        scaled = (0.25 * 3.0 ** k) * term
        plain, steep = (term, scaled) if plain is None else (plain + term, steep + scaled)
    return f * (f * steep + plain), (ex, ey, ez)


def blocks(z, store, region, adj_table, ax, ay, some, sums, back):
    for first in range(0, len(some), WIDE):
        part = some[first:first + WIDE]
        spots = [(ax + 1 + z.offsets[n][0], ay + 1 + z.offsets[n][1], z.offsets[n][2]) for n in part]
        hots = jnp.concatenate([store.onehot(*spot) for spot in spots], axis=1)
        gains = dot(adj_table[...], jnp.concatenate([hots, hots], axis=0), NN)
        totals = [[None] * 3 for _ in part]
        for r in range(len(z.rows)):
            some_gains = gains[r * z.rad * STEP:(r + 1) * z.rad * STEP]
            for i, n in enumerate(part):
                p, displace = pairs(z, store, region, ax, ay, n, some_gains[:, i * LANES:(i + 1) * LANES], r)
                for q in range(3):
                    term = p * displace[q]
                    if sums is not None:
                        sums[q][r] = term if sums[q][r] is None else sums[q][r] + term
                    if back is not None:
                        term = sum(term[j:j + 8] for j in range(8, STEP, 8)) + term[0:8]
                        totals[i][q] = term if totals[i][q] is None else totals[i][q] + term
        if back is not None:
            for (x, y, g), total in zip(spots, totals):
                for q in range(3):
                    back[((x - HALO) * z.block[1] + y - HALO) * z.groups + g, q] += total[q]


def far_kernel(
    z, region, table, readout_ref, onehot_near, anchors_near, sums_near, kept_near,
    other, part, mine, adj_own, act_own, onehot_far, kept_own,
    anchors_far, kept_far, stage, adj_table, mixed, back, *buffers,
):
    by = z.block[1]
    bf = jnp.bfloat16
    slots, spec, rad = z.slots, z.spec, z.rad
    readout = readout_ref[...]
    store = Store(z, onehot_near, onehot_far, anchors_near, anchors_far, kept_near, kept_own, kept_far)
    outer = store.outer

    for x in range(z.nx):
        for i, y in enumerate(outer):
            for g in range(z.groups):
                place_onehot(z, region, x, y, g, onehot_far, (x * len(outer) + i) * z.groups + g)
    place_anchors(
        z, stage, [(region, ax + 1, y) for ax in range(z.nax) for y in (1, z.ny - HALO)], anchors_far
    )

    def message_at(ax, carry):
        for ay in range(z.nay):
            a = ax * z.nay + ay
            some = z.split_offsets(ay)[1]
            hots = []
            for i, n in enumerate(some):
                dx, dy, g = z.offsets[n]
                x, y = ax + 1 + dx, ay + 1 + dy
                weigh(
                    z, target(region, x, y, z.offsets[n]), store.anchor(ax, ay), z.offsets[n], buffers[ay],
                    slice(i * LANES, (i + 1) * LANES), store.radial(ax, ay, n),
                )
                hots.append(store.onehot(x, y, g))
            total = sums_near[ax * by + ay - 1] if z.inner(ay) else None
            if some:
                term = dot(buffers[ay][:, 0:len(some) * LANES], jnp.concatenate(hots, axis=1), NT)
                total = term if total is None else total + term
            for k in range(rad):
                mixed[a, :, k * spec:(k + 1) * spec] = total[k * slots:(k + 1) * slots].astype(bf)
        return carry

    lax.fori_loop(0, z.nax, message_at, 0)

    def adj_at(ax, ay):
        if 0 < ax < z.nax - 1 and z.inner(ay):
            return adj_own.at[(ax - 1) * by + ay - 1]
        return adj_table.at[ax * z.nay + ay]

    def adjoint_of(group):
        cells = [ax * z.nay + ay for ax, ay in group]
        messages = dot(jnp.concatenate([mixed[a] for a in cells], axis=0), table[...], NN)
        adjoints = []
        for i, (a, spot) in enumerate(zip(cells, group)):
            message = MSG_SCALE * messages[i * slots:(i + 1) * slots]
            sigmoid = 1.0 / (1.0 + jnp.exp(-message))
            ax, ay = spot
            inside = 0 < ax < z.nax - 1 and z.inner(ay)
            if inside:
                act_own[(ax - 1) * by + ay - 1] = (message * sigmoid).astype(bf)
            slope = sigmoid * (1.0 + message * (1.0 - sigmoid)) * readout[0:1]
            adjoints.append(jnp.where(store.anchor(*spot)[3] >= 0.0, slope, 0.0).astype(bf))
        turned = dot(jnp.concatenate(adjoints, axis=0), table[...], NT)
        for i, spot in enumerate(group):
            out = adj_at(*spot)
            for r, c in enumerate(z.rows):
                high, low = split(turned[slots * i + c.start:slots * i + c.stop])
                for k in range(rad):
                    at = slice((r * rad + k) * STEP, (r * rad + k + 1) * STEP)
                    out[at, 0:spec] = high[:, k * spec:(k + 1) * spec]
                    out[at, spec:] = low[:, k * spec:(k + 1) * spec]

    for first in range(0, z.nax, BATCH):
        adjoint_of([(ax, ay) for ax in range(first, min(first + BATCH, z.nax)) for ay in range(z.nay)])

    back[...] = jnp.zeros_like(back)

    for ax in range(z.nax):
        for ay in range(z.nay):
            o = z.cell(ax, ay)
            some = [n for n, (dx, dy, _) in enumerate(z.offsets) if z.cell(ax + dx, ay + dy) is not None]
            sums = None if o is None else [[None] * len(z.rows) for _ in range(3)]
            blocks(z, store, region, adj_at(ax, ay), ax, ay, some, sums, back)
            if o is not None:
                for q in range(3):
                    for r, c in enumerate(z.rows):
                        mine[o, q, c, :] = sums[q][r]

    for ox in range(z.block[0]):
        for oy in range(by):
            for g in range(z.groups):
                start = slots if g == 0 else 0
                for q in range(3):
                    row = FORCE_SCALE * jnp.sum(back[(ox * by + oy) * z.groups + g, q], axis=0, keepdims=True)
                    other[g, ox, oy, :, q * slots:(q + 1) * slots] = row[:, start:start + slots]
                    if g == 0:
                        part[ox, oy, :, q * slots:(q + 1) * slots] = row[:, 0:slots]


def own_kernel(
    z, region, readout, emb_energy, onehot_near, anchors_near, kept_near,
    part, mine_part, adj_own, act_own, onehot_far, kept_own,
    energies, own, mine,
):
    slots = z.slots
    store = Store(z, onehot_near, onehot_far, anchors_near, None, kept_near, kept_own, None)
    cells = [(ox, oy) for ox in range(z.block[0]) for oy in range(z.block[1])]
    for o, (ox, oy) in enumerate(cells):
        ax, ay = ox + 1, oy + 1
        some = [n for n, (dx, dy, _) in enumerate(z.offsets) if z.cell(ax + dx, ay + dy) is None]
        sums = [[mine_part[o, q, c, :] for c in z.rows] for q in range(3)]
        blocks(z, store, region, adj_own.at[o], ax, ay, some, sums, None)
        for q in range(3):
            for r, c in enumerate(z.rows):
                mine[o, q, c, :] = sums[q][r]

    high, low = split(mine[...].reshape(len(cells) * 3 * slots, LANES))
    ones = jnp.ones((8, 2 * LANES), jnp.bfloat16)
    rows = dot(ones, jnp.concatenate([high, low], axis=1), NT)[0:1]
    for o, (ox, oy) in enumerate(cells):
        for q in range(3):
            at = (o * 3 + q) * slots
            lanes = slice(q * slots, (q + 1) * slots)
            own[ox, oy, :, lanes] = part[ox, oy, :, lanes] - FORCE_SCALE * rows[:, at:at + slots]

    hots = jnp.concatenate([store.onehot(ox + HALO, oy + HALO, 0)[:, 0:slots] for ox, oy in cells], axis=1)
    acts = jnp.concatenate([act_own[o] for o in range(len(cells))], axis=0)
    energy = dot(thirds(emb_energy[...]), hots, NN) + dot(thirds(readout[...]), acts, NT)
    energy = jnp.sum(energy, axis=0, keepdims=True)
    for o, (ox, oy) in enumerate(cells):
        marked = region[ox + HALO, oy + HALO, 3:4, 0:slots]
        energies[ox, oy, :, :] = jnp.where(marked >= 0.0, energy[:, o * slots:(o + 1) * slots], 0.0)


VMEM = pl.BlockSpec(memory_space=pltpu.VMEM)
HBM = pl.BlockSpec(memory_space=pltpu.HBM)


def in_hbm(*arrays):
    return [pltpu.with_memory_space_constraint(array, pltpu.HBM) for array in arrays]


def pack(positions, species, counts):
    bx, by, _, slots = species.shape
    return pl.pallas_call(
        pack_kernel,
        out_shape=jax.ShapeDtypeStruct((bx, by, 4, slots), jnp.float32),
        in_specs=[HBM] * 3,
        out_specs=VMEM,
        scratch_shapes=[
            pltpu.SMEM(counts.shape, counts.dtype),
            pltpu.VMEM(positions.shape, positions.dtype),
            pltpu.VMEM(species.shape, species.dtype),
            pltpu.SemaphoreType.DMA((3,)),
        ],
        compiler_params=pltpu.CompilerParams(vmem_limit_bytes=1024 * 1024),
    )(*in_hbm(counts, positions, species))


def near_layer(z, near, embed, filters, w_up, w_energy):
    width = embed.shape[1]
    by = z.block[1]
    cells, most = z.nax * by, max(len(z.split_offsets(y + 1)[0]) for y in range(by))
    shapes = [
        ((z.rad * z.spec, width), jnp.bfloat16),
        ((8, width), jnp.float32),
        ((8, z.spec), jnp.float32),
        ((z.nx * by * z.groups, z.spec, LANES), jnp.bfloat16),
        ((cells, 4, z.slots, LANES), jnp.float32),
        ((cells, z.rad * z.slots, z.spec), jnp.float32),
        ((cells, most, 2, z.slots, LANES), jnp.float32),
    ]
    flops = 2 * cells * most * z.rad * z.slots * LANES * z.spec
    return pl.pallas_call(
        functools.partial(near_kernel, z),
        out_shape=[jax.ShapeDtypeStruct(*shape) for shape in shapes],
        in_specs=[VMEM] + [HBM] * 4,
        out_specs=[VMEM] * len(shapes),
        scratch_shapes=[
            pltpu.VMEM((z.spec, width), jnp.float32),
            pltpu.VMEM((4, LANES, LANES), jnp.float32),
            pltpu.VMEM(embed.shape, embed.dtype),
            pltpu.VMEM(filters.shape, filters.dtype),
            pltpu.VMEM(w_up.shape, w_up.dtype),
            pltpu.VMEM(w_energy.shape, w_energy.dtype),
            pltpu.SemaphoreType.DMA((4,)),
        ] + [pltpu.VMEM((z.rad * z.slots, most * LANES), jnp.bfloat16)] * by,
        compiler_params=pltpu.CompilerParams(vmem_limit_bytes=12 * 1024 * 1024),
        cost_estimate=pl.CostEstimate(flops=flops, bytes_accessed=1 << 20, transcendentals=0),
    )(near, *in_hbm(embed, filters, w_up, w_energy))


def call(kernel, z, shapes, scratch, limit, operands):
    return pl.pallas_call(
        functools.partial(kernel, z),
        out_shape=[jax.ShapeDtypeStruct(*shape) for shape in shapes],
        in_specs=[VMEM] * len(operands),
        out_specs=[VMEM] * len(shapes),
        scratch_shapes=[pltpu.VMEM(*shape) for shape in scratch],
        compiler_params=pltpu.CompilerParams(vmem_limit_bytes=limit),
    )(*operands)


def far_layer(z, region, near):
    table, readout, emb_energy, onehot, anchors, sums, kept = near
    width = table.shape[1]
    cells, ring = z.block[0] * z.block[1], z.nax * z.nay
    offsets, most = len(z.offsets), max(len(z.split_offsets(y + 1)[1]) for y in range(z.block[1]))
    pair = (2, z.slots, LANES)
    shapes = [
        ((z.groups,) + z.block + (1, 3 * z.slots), jnp.float32),
        (z.block + (1, 3 * z.slots), jnp.float32),
        ((cells, 3, z.slots, LANES), jnp.float32),
        ((cells, z.rad * z.slots, 2 * z.spec), jnp.bfloat16),
        ((cells, z.slots, width), jnp.bfloat16),
        ((z.nx * 2 * HALO * z.groups, z.spec, LANES), jnp.bfloat16),
        ((z.nax * z.block[1], most) + pair, jnp.float32),
    ]
    scratch = [
        ((z.nax * 2, 4, z.slots, LANES), jnp.float32),
        ((z.nax * 2, offsets) + pair, jnp.float32),
        ((4, LANES, LANES), jnp.float32),
        ((ring, z.rad * z.slots, 2 * z.spec), jnp.bfloat16),
        ((ring, z.slots, z.rad * z.spec), jnp.bfloat16),
        ((cells * z.groups, 3, 8, LANES), jnp.float32),
    ] + [((z.rad * z.slots, offsets * LANES), jnp.bfloat16)] * z.nay
    operands = (region, table, readout, onehot, anchors, sums, kept)
    return call(far_kernel, z, shapes, scratch, FAR_VMEM, operands)


def own_layer(z, region, near, far):
    table, readout, emb_energy, onehot, anchors, sums, kept = near
    shapes = [
        (z.block + (1, z.slots), jnp.float32),
        (z.block + (1, 3 * z.slots), jnp.float32),
    ]
    scratch = [((z.block[0] * z.block[1], 3, z.slots, LANES), jnp.float32)]
    operands = (region, readout, emb_energy, onehot, anchors, kept) + tuple(far)
    return call(own_kernel, z, shapes, scratch, OWN_VMEM, operands)


def on_device(positions, species, counts, embed, filters, w_up, w_energy):
    bx, by = positions.shape[:2]
    slots = species.shape[-1]
    width = embed.shape[1]
    depth = lax.axis_size("gz")
    merged = depth * positions.shape[2] == 2
    spec = -(-embed.shape[0] // LANES) * LANES
    z = Cells((bx, by), merged, filters.shape[1] // width, spec, slots)
    block = pack(positions, species, counts.reshape(bx, by))
    upward = [(i, (i + 1) % depth) for i in range(depth)]
    downward = [(b, a) for a, b in upward]
    low = lax.ppermute(block, "gz", upward)
    if merged:
        block = jnp.concatenate([block, low], axis=3)
    else:
        high = lax.ppermute(block, "gz", downward)
        empty = jnp.full_like(block, -1.0)
        block = jnp.concatenate(
            [jnp.concatenate([block, low], axis=3), jnp.concatenate([high, empty], axis=3)], axis=2
        )
    block = exchange(block, "gx", 0, HALO)
    near = near_layer(z, block, embed, filters, w_up, w_energy.reshape(1, width))
    region = exchange(block, "gy", 1, HALO)
    other, *far = far_layer(z, region, near)
    energies, own = own_layer(z, region, near, far)

    forces = own + lax.ppermute(other[0], "gz", downward)
    if not merged:
        forces = forces + lax.ppermute(other[1], "gz", upward)
    return energies, forces


def solution(mesh):
    in_specs = (
        P("gx", "gy", "gz", None),
        P("gx", "gy", "gz", None),
        P("gx", "gy", "gz"),
        P(),
        P(),
        P(),
        P(),
    )
    out_specs = (P("gx", "gy", "gz", None), P("gx", "gy", "gz", None))
    return jax.shard_map(
        on_device, mesh=mesh, in_specs=in_specs, out_specs=out_specs, check_vma=False
    )
```

```python
import functools

import jax
import jax.numpy as jnp
from jax import lax
from jax.experimental import pallas as pl
from jax.experimental.pallas import tpu as pltpu
from jax.sharding import PartitionSpec as P

MSG_SCALE = 0.1
HALO = 2
FAR_VMEM = 30 * 1024 * 1024
OWN_VMEM = 8 * 1024 * 1024
LANES = 128
STEP = 16
WIDE = 4
LAG = 2
GROUP = 2
LATER = 0
BATCH = 4
FORCE_SCALE = 4.0 * MSG_SCALE
LOG2E = 1.4426950408889634
NT = (((1,), (1,)), ((), ()))
NN = (((1,), (0,)), ((), ()))


def exchange(block, axis, dim, width):
    count = lax.axis_size(axis)
    first = lax.slice_in_dim(block, 0, width, axis=dim)
    last = lax.slice_in_dim(block, block.shape[dim] - width, None, axis=dim)
    if count % 2 == 0:
        odd = lax.axis_index(axis) % 2 == 1
        whole = block.shape[dim] == width
        up = block if whole else jnp.where(odd, last, first)
        down = block if whole else jnp.where(odd, first, last)
        far = [(i, (i + 1) % count if i % 2 else (i - 1) % count) for i in range(count)]
        near = [(i, i - 1 if i % 2 else i + 1) for i in range(count)]
        from_far = lax.ppermute(up, axis, far)
        from_near = lax.ppermute(down, axis, near)
        low = jnp.where(odd, from_near, from_far)
        high = jnp.where(odd, from_far, from_near)
    else:
        forward = [(i, (i + 1) % count) for i in range(count)]
        low = lax.ppermute(last, axis, forward)
        high = lax.ppermute(first, axis, [(b, a) for a, b in forward])
    return jnp.concatenate([low, block, high], axis=dim)


def dot(a, b, dims, precision=None):
    return lax.dot_general(a, b, dims, precision=precision, preferred_element_type=jnp.float32)


def split(values):
    high = values.astype(jnp.bfloat16)
    return high, (values - high.astype(jnp.float32)).astype(jnp.bfloat16)


def thirds(rows):
    high = rows.astype(jnp.bfloat16)
    middle, low = split(rows - high.astype(jnp.float32))
    at = lax.broadcasted_iota(jnp.int32, rows.shape, 0)
    parts = [part.astype(jnp.float32) for part in (high, middle, low)]
    kept = jnp.where(at == 0, parts[0], jnp.where(at == 1, parts[1], jnp.where(at == 2, parts[2], 0.0)))
    return kept.astype(jnp.bfloat16)


class Cells:
    def __init__(self, block, merged, rad, spec, slots):
        self.block, self.merged, self.rad, self.spec, self.slots = block, merged, rad, spec, slots
        self.groups = 1 if merged else 2
        self.nax, self.nay = block[0] + 2, block[1] + 2
        self.nx, self.ny = block[0] + 2 * HALO, block[1] + 2 * HALO
        self.offsets = [
            (dx, dy, g) for dx in (-1, 0, 1) for dy in (-1, 0, 1) for g in range(self.groups)
        ]
        self.rows = [slice(r, r + STEP) for r in range(0, slots, STEP)]

    def inner(self, ay):
        return 1 <= ay <= self.block[1]

    def cell(self, ax, ay):
        if 1 <= ax <= self.block[0] and self.inner(ay):
            return (ax - 1) * self.block[1] + ay - 1
        return None

    def split_offsets(self, ay):
        near = [n for n, (_, dy, _) in enumerate(self.offsets) if self.inner(ay) and self.inner(ay + dy)]
        return near, [n for n in range(len(self.offsets)) if n not in near]

    def z_shift(self, g):
        lane = lax.broadcasted_iota(jnp.int32, (1, LANES), 1)
        if self.merged:
            return jnp.where(lane < self.slots, 0.0, 1.0)
        if g == 0:
            return jnp.where(lane < self.slots, 0.0, -1.0)
        return jnp.where(lane < self.slots, 1.0, 0.0)


def place_anchors(z, stage, rows, out):
    for q in range(4):
        for i, (ref, x, y) in enumerate(rows):
            stage[q, i:i + 1, :] = ref[x, y, q:q + 1, :]
        columns = stage[q].T
        for i in range(len(rows)):
            out[i, q] = jnp.broadcast_to(columns[0:z.slots, i:i + 1], (z.slots, LANES))


def place_onehot(z, ref, x, y, g, out, at):
    ids = lax.broadcasted_iota(jnp.int32, (z.spec, LANES), 0).astype(jnp.float32)
    out[at] = (ref[x, y, g * 4 + 3:g * 4 + 4, :] == ids).astype(jnp.bfloat16)


def target(ref, x, y, offset):
    dx, dy, g = offset
    row = ref[x, y, g * 4:g * 4 + 3, :]
    return row[0:1] + dx, row[1:2] + dy, row[2:3]


def weigh(z, position, anchor, offset, keep):
    tx, ty, tz = position
    shift = z.z_shift(offset[2])
    weights = [[] for _ in range(z.rad)]
    for c in z.rows:
        ex = tx - anchor[0, c, :]
        ey = ty - anchor[1, c, :]
        dz = tz - anchor[2, c, :]
        ez = jnp.abs(dz) - shift if z.merged else dz + shift
        s = ex * ex + ey * ey + ez * ez
        f = jnp.maximum(1.0 - s, 0.0)
        e = jnp.exp2(s * (-0.5 * LOG2E))
        keep[0, c, :] = f
        keep[1, c, :] = e
        f = f * f
        if offset == (0, 0, 0):
            row = lax.broadcasted_iota(jnp.int32, (STEP, LANES), 0) + c.start
            lane = lax.broadcasted_iota(jnp.int32, (STEP, LANES), 1)
            f = jnp.where(row == lane, 0.0, f)
        for k in range(z.rad):
            if k == 0:
                w = e * f
                e = e * e
            elif k == 1:
                w = w * e
            else:
                e = e * e * e
                w = w * e
            weights[k].append(w.astype(jnp.bfloat16))
    return jnp.concatenate([part for parts in weights for part in parts], axis=0)


def grouped(values):
    return [values[i:i + GROUP] for i in range(0, len(values), GROUP)]


def staggered(tasks, first, second, lag):
    results = []
    for t in range(len(tasks) + lag):
        if t < len(tasks):
            results.append(first(*tasks[t]))
        if t >= lag:
            second(results[t - lag], *tasks[t - lag])


def pack_kernel(counts_hbm, positions_hbm, species_hbm, out, counts, positions, species, arrived):
    arguments = [(counts_hbm, counts), (positions_hbm, positions), (species_hbm, species)]
    copies = [pltpu.make_async_copy(a, b, arrived.at[i]) for i, (a, b) in enumerate(arguments)]
    for copy in copies:
        copy.start()
    for copy in copies:
        copy.wait()
    slots = out.shape[3]
    lane = lax.broadcasted_iota(jnp.int32, (1, slots), 1)
    for x in range(out.shape[0]):
        for y in range(out.shape[1]):
            row = positions[x, y, 0:1, :]
            for q in range(3):
                out[x, y, q:q + 1, :] = row[:, q * slots:(q + 1) * slots]
            marked = jnp.where(lane < counts[x, y], species[x, y, 0:1, :], -1)
            out[x, y, 3:4, :] = marked.astype(jnp.float32)


def near_kernel(
    z, near, embed_hbm, filters_hbm, w_up_hbm, w_energy_hbm,
    table, readout, emb_energy, onehot, anchors, sums, kept,
    emb_pad, stage, embed, filters, w_up, w_energy, arrived,
):
    nspec, width = embed.shape
    by = z.block[1]
    weights = [(embed_hbm, embed), (filters_hbm, filters), (w_up_hbm, w_up), (w_energy_hbm, w_energy)]
    copies = [pltpu.make_async_copy(a, b, arrived.at[i]) for i, (a, b) in enumerate(weights)]
    for copy in copies:
        copy.start()

    for x in range(z.nx):
        for y in range(by):
            for g in range(z.groups):
                place_onehot(z, near, x, y, g, onehot, (x * by + y) * z.groups + g)
    place_anchors(z, stage, [(near, ax + 1, y) for ax in range(z.nax) for y in range(by)], anchors)

    def message_at(ax, carry):
        totals = {}

        def weigh_some(y, some):
            weights = []
            for n in some:
                dx, dy, _ = z.offsets[n]
                keep = kept.at[ax * by + y, z.split_offsets(y + 1)[0].index(n)]
                spot = target(near, ax + 1 + dx, y + dy, z.offsets[n])
                weights.append(weigh(z, spot, anchors.at[ax * by + y], z.offsets[n], keep))
            return jnp.concatenate(weights, axis=1)

        def gather_some(weights, y, some):
            spots = [z.offsets[n] for n in some]
            hots = [onehot[((ax + 1 + dx) * by + y + dy) * z.groups + g] for dx, dy, g in spots]
            term = dot(weights, jnp.concatenate(hots, axis=1), NT)
            totals[y] = totals[y] + term if y in totals else term

        staggered([(y, some) for y in range(by) for some in grouped(z.split_offsets(y + 1)[0])], weigh_some, gather_some, LAG)
        for y in range(by):
            sums[ax * by + y] = totals[y]
        return carry

    lax.fori_loop(0, z.nax, message_at, 0)

    for copy in copies:
        copy.wait()
    emb_pad[...] = jnp.zeros_like(emb_pad)
    emb_pad[0:nspec, :] = embed[...].astype(jnp.float32)
    emb = emb_pad[...]
    rows = dot(emb.astype(jnp.bfloat16), filters[...], NN).astype(jnp.bfloat16)
    for k in range(z.rad):
        table[k * z.spec:(k + 1) * z.spec, :] = rows[:, k * width:(k + 1) * width]
    energy_row = jnp.broadcast_to(w_energy[...], (8, width))
    readout[...] = dot(energy_row, w_up[...].astype(jnp.float32), NT, lax.Precision.HIGHEST)
    emb_energy[...] = dot(energy_row, emb, NT, lax.Precision.HIGHEST)


class Store:
    def __init__(self, z, onehot_near, onehot_far, anchors_near, anchors_far, kept_near, kept_own, kept_far):
        self.z = z
        self.onehots = (onehot_near, onehot_far)
        self.anchors = (anchors_near, anchors_far)
        self.kept = (kept_near, kept_own, kept_far)
        self.outer = [y for y in range(z.ny) if not HALO <= y < HALO + z.block[1]]

    def onehot(self, x, y, g):
        z = self.z
        if y in self.outer:
            return self.onehots[1][(x * len(self.outer) + self.outer.index(y)) * z.groups + g]
        return self.onehots[0][(x * z.block[1] + y - HALO) * z.groups + g]

    def anchor(self, ax, ay):
        if self.z.inner(ay):
            return self.anchors[0].at[ax * self.z.block[1] + ay - 1]
        return self.anchors[1].at[ax * 2 + (ay > 0)]

    def radial(self, ax, ay, n):
        if not self.z.inner(ay):
            return self.kept[2].at[ax * 2 + (ay > 0), n]
        near, far = self.z.split_offsets(ay)
        if n in near:
            return self.kept[0].at[ax * self.z.block[1] + ay - 1, near.index(n)]
        return self.kept[1].at[ax * self.z.block[1] + ay - 1, far.index(n)]


def pairs(z, store, region, ax, ay, n, gains, r):
    c = z.rows[r]
    dx, dy, g = z.offsets[n]
    tx, ty, tz = target(region, ax + 1 + dx, ay + 1 + dy, z.offsets[n])
    anchor, keep = store.anchor(ax, ay), store.radial(ax, ay, n)
    ex = tx - anchor[0, c, :]
    ey = ty - anchor[1, c, :]
    ez = tz - anchor[2, c, :]
    shift = z.z_shift(g)
    ez = ez + jnp.where(ez > 0.0, -shift, shift) if z.merged else ez + shift
    f = keep[0, c, :]
    e = keep[1, c, :]
    e2 = e * e
    plain = None
    for k in range(z.rad):
        if k == 1:
            e = e * e2
        elif k > 1:
            e2 = e2 * e2 * e2
            e = e * e2
        term = e * gains[k * STEP:(k + 1) * STEP]
        scaled = (0.25 * 3.0 ** k) * term
        plain, steep = (term, scaled) if plain is None else (plain + term, steep + scaled)
    return f * (f * steep + plain), (ex, ey, ez)


def blocks(z, store, region, work, back):
    tasks = [
        (ax, ay, table, some[first:first + WIDE], sums)
        for ax, ay, table, some, sums in work for first in range(0, len(some), WIDE)
    ]

    def spots_of(ax, ay, part):
        return [(ax + 1 + z.offsets[n][0], ay + 1 + z.offsets[n][1], z.offsets[n][2]) for n in part]

    def multiply(ax, ay, table, part, sums):
        hots = jnp.concatenate([store.onehot(*spot) for spot in spots_of(ax, ay, part)], axis=1)
        return dot(table[...], jnp.concatenate([hots, hots], axis=0), NN)

    def add_forces(gains, ax, ay, table, part, sums):
        totals = [[None] * 3 for _ in part]
        for r in range(len(z.rows)):
            some_gains = gains[r * z.rad * STEP:(r + 1) * z.rad * STEP]
            for i, n in enumerate(part):
                p, displace = pairs(z, store, region, ax, ay, n, some_gains[:, i * LANES:(i + 1) * LANES], r)
                for q in range(3):
                    term = p * displace[q]
                    if sums is not None:
                        sums[q][r] = term if sums[q][r] is None else sums[q][r] + term
                    if back is not None:
                        term = sum(term[j:j + 8] for j in range(8, STEP, 8)) + term[0:8]
                        totals[i][q] = term if totals[i][q] is None else totals[i][q] + term
        if back is not None:
            for (x, y, g), total in zip(spots_of(ax, ay, part), totals):
                for q in range(3):
                    back[((x - HALO) * z.block[1] + y - HALO) * z.groups + g, q] += total[q]

    staggered(tasks, multiply, add_forces, LATER)


def far_kernel(
    z, region, table, readout_ref, onehot_near, anchors_near, sums_near, kept_near,
    other, part, mine, adj_own, act_own, onehot_far, kept_own,
    anchors_far, kept_far, stage, adj_table, mixed, back,
):
    by = z.block[1]
    bf = jnp.bfloat16
    slots, spec, rad = z.slots, z.spec, z.rad
    readout = readout_ref[...]
    store = Store(z, onehot_near, onehot_far, anchors_near, anchors_far, kept_near, kept_own, kept_far)
    outer = store.outer

    for x in range(z.nx):
        for i, y in enumerate(outer):
            for g in range(z.groups):
                place_onehot(z, region, x, y, g, onehot_far, (x * len(outer) + i) * z.groups + g)
    place_anchors(
        z, stage, [(region, ax + 1, y) for ax in range(z.nax) for y in (1, z.ny - HALO)], anchors_far
    )

    def message_at(ax, carry):
        totals = {ay: sums_near[ax * by + ay - 1] for ay in range(z.nay) if z.inner(ay)}

        def weigh_some(ay, some):
            weights = []
            for n in some:
                dx, dy, _ = z.offsets[n]
                spot = target(region, ax + 1 + dx, ay + 1 + dy, z.offsets[n])
                weights.append(weigh(z, spot, store.anchor(ax, ay), z.offsets[n], store.radial(ax, ay, n)))
            return jnp.concatenate(weights, axis=1)

        def gather_some(weights, ay, some):
            spots = [z.offsets[n] for n in some]
            hots = [store.onehot(ax + 1 + dx, ay + 1 + dy, g) for dx, dy, g in spots]
            term = dot(weights, jnp.concatenate(hots, axis=1), NT)
            totals[ay] = totals[ay] + term if ay in totals else term

        staggered([(ay, some) for ay in range(z.nay) for some in grouped(z.split_offsets(ay)[1])], weigh_some, gather_some, LAG)
        for ay in range(z.nay):
            for k in range(rad):
                part_sum = totals[ay][k * slots:(k + 1) * slots].astype(bf)
                mixed[ax * z.nay + ay, :, k * spec:(k + 1) * spec] = part_sum
        return carry

    lax.fori_loop(0, z.nax, message_at, 0)

    def adj_at(ax, ay):
        if 0 < ax < z.nax - 1 and z.inner(ay):
            return adj_own.at[(ax - 1) * by + ay - 1]
        return adj_table.at[ax * z.nay + ay]

    def adjoint_of(group):
        cells = [ax * z.nay + ay for ax, ay in group]
        messages = dot(jnp.concatenate([mixed[a] for a in cells], axis=0), table[...], NN)
        adjoints = []
        for i, (a, spot) in enumerate(zip(cells, group)):
            message = MSG_SCALE * messages[i * slots:(i + 1) * slots]
            sigmoid = 1.0 / (1.0 + jnp.exp(-message))
            ax, ay = spot
            inside = 0 < ax < z.nax - 1 and z.inner(ay)
            if inside:
                act_own[(ax - 1) * by + ay - 1] = (message * sigmoid).astype(bf)
            slope = sigmoid * (1.0 + message * (1.0 - sigmoid)) * readout[0:1]
            adjoints.append(jnp.where(store.anchor(*spot)[3] >= 0.0, slope, 0.0).astype(bf))
        turned = dot(jnp.concatenate(adjoints, axis=0), table[...], NT)
        for i, spot in enumerate(group):
            out = adj_at(*spot)
            for r, c in enumerate(z.rows):
                high, low = split(turned[slots * i + c.start:slots * i + c.stop])
                for k in range(rad):
                    at = slice((r * rad + k) * STEP, (r * rad + k + 1) * STEP)
                    out[at, 0:spec] = high[:, k * spec:(k + 1) * spec]
                    out[at, spec:] = low[:, k * spec:(k + 1) * spec]

    for first in range(0, z.nax, BATCH):
        adjoint_of([(ax, ay) for ax in range(first, min(first + BATCH, z.nax)) for ay in range(z.nay)])

    back[...] = jnp.zeros_like(back)

    work = []
    for ax in range(z.nax):
        for ay in range(z.nay):
            some = [n for n, (dx, dy, _) in enumerate(z.offsets) if z.cell(ax + dx, ay + dy) is not None]
            sums = None if z.cell(ax, ay) is None else [[None] * len(z.rows) for _ in range(3)]
            work.append((ax, ay, adj_at(ax, ay), some, sums))
    blocks(z, store, region, work, back)
    for ax, ay, _, _, sums in work:
        if sums is not None:
            for q in range(3):
                for r, c in enumerate(z.rows):
                    mine[z.cell(ax, ay), q, c, :] = sums[q][r]

    for ox in range(z.block[0]):
        for oy in range(by):
            for g in range(z.groups):
                start = slots if g == 0 else 0
                for q in range(3):
                    row = FORCE_SCALE * jnp.sum(back[(ox * by + oy) * z.groups + g, q], axis=0, keepdims=True)
                    other[g, ox, oy, :, q * slots:(q + 1) * slots] = row[:, start:start + slots]
                    if g == 0:
                        part[ox, oy, :, q * slots:(q + 1) * slots] = row[:, 0:slots]


def own_kernel(
    z, region, readout, emb_energy, onehot_near, anchors_near, kept_near,
    part, mine_part, adj_own, act_own, onehot_far, kept_own,
    energies, own, mine,
):
    slots = z.slots
    store = Store(z, onehot_near, onehot_far, anchors_near, None, kept_near, kept_own, None)
    cells = [(ox, oy) for ox in range(z.block[0]) for oy in range(z.block[1])]
    work = []
    for o, (ox, oy) in enumerate(cells):
        some = [n for n, (dx, dy, _) in enumerate(z.offsets) if z.cell(ox + 1 + dx, oy + 1 + dy) is None]
        sums = [[mine_part[o, q, c, :] for c in z.rows] for q in range(3)]
        work.append((ox + 1, oy + 1, adj_own.at[o], some, sums))
    blocks(z, store, region, work, None)
    for o, (_, _, _, _, sums) in enumerate(work):
        for q in range(3):
            for r, c in enumerate(z.rows):
                mine[o, q, c, :] = sums[q][r]

    high, low = split(mine[...].reshape(len(cells) * 3 * slots, LANES))
    ones = jnp.ones((8, 2 * LANES), jnp.bfloat16)
    rows = dot(ones, jnp.concatenate([high, low], axis=1), NT)[0:1]
    for o, (ox, oy) in enumerate(cells):
        for q in range(3):
            at = (o * 3 + q) * slots
            lanes = slice(q * slots, (q + 1) * slots)
            own[ox, oy, :, lanes] = part[ox, oy, :, lanes] - FORCE_SCALE * rows[:, at:at + slots]

    hots = jnp.concatenate([store.onehot(ox + HALO, oy + HALO, 0)[:, 0:slots] for ox, oy in cells], axis=1)
    acts = jnp.concatenate([act_own[o] for o in range(len(cells))], axis=0)
    energy = dot(thirds(emb_energy[...]), hots, NN) + dot(thirds(readout[...]), acts, NT)
    energy = jnp.sum(energy, axis=0, keepdims=True)
    for o, (ox, oy) in enumerate(cells):
        marked = region[ox + HALO, oy + HALO, 3:4, 0:slots]
        energies[ox, oy, :, :] = jnp.where(marked >= 0.0, energy[:, o * slots:(o + 1) * slots], 0.0)


VMEM = pl.BlockSpec(memory_space=pltpu.VMEM)
HBM = pl.BlockSpec(memory_space=pltpu.HBM)


def in_hbm(*arrays):
    return [pltpu.with_memory_space_constraint(array, pltpu.HBM) for array in arrays]


def pack(positions, species, counts):
    bx, by, _, slots = species.shape
    return pl.pallas_call(
        pack_kernel,
        out_shape=jax.ShapeDtypeStruct((bx, by, 4, slots), jnp.float32),
        in_specs=[HBM] * 3,
        out_specs=VMEM,
        scratch_shapes=[
            pltpu.SMEM(counts.shape, counts.dtype),
            pltpu.VMEM(positions.shape, positions.dtype),
            pltpu.VMEM(species.shape, species.dtype),
            pltpu.SemaphoreType.DMA((3,)),
        ],
        compiler_params=pltpu.CompilerParams(vmem_limit_bytes=1024 * 1024),
    )(*in_hbm(counts, positions, species))


def near_layer(z, near, embed, filters, w_up, w_energy):
    width = embed.shape[1]
    by = z.block[1]
    cells, most = z.nax * by, max(len(z.split_offsets(y + 1)[0]) for y in range(by))
    shapes = [
        ((z.rad * z.spec, width), jnp.bfloat16),
        ((8, width), jnp.float32),
        ((8, z.spec), jnp.float32),
        ((z.nx * by * z.groups, z.spec, LANES), jnp.bfloat16),
        ((cells, 4, z.slots, LANES), jnp.float32),
        ((cells, z.rad * z.slots, z.spec), jnp.float32),
        ((cells, most, 2, z.slots, LANES), jnp.float32),
    ]
    flops = 2 * cells * most * z.rad * z.slots * LANES * z.spec
    return pl.pallas_call(
        functools.partial(near_kernel, z),
        out_shape=[jax.ShapeDtypeStruct(*shape) for shape in shapes],
        in_specs=[VMEM] + [HBM] * 4,
        out_specs=[VMEM] * len(shapes),
        scratch_shapes=[
            pltpu.VMEM((z.spec, width), jnp.float32),
            pltpu.VMEM((4, LANES, LANES), jnp.float32),
            pltpu.VMEM(embed.shape, embed.dtype),
            pltpu.VMEM(filters.shape, filters.dtype),
            pltpu.VMEM(w_up.shape, w_up.dtype),
            pltpu.VMEM(w_energy.shape, w_energy.dtype),
            pltpu.SemaphoreType.DMA((4,)),
        ],
        compiler_params=pltpu.CompilerParams(vmem_limit_bytes=12 * 1024 * 1024),
        cost_estimate=pl.CostEstimate(flops=flops, bytes_accessed=1 << 20, transcendentals=0),
    )(near, *in_hbm(embed, filters, w_up, w_energy))


def call(kernel, z, shapes, scratch, limit, operands):
    return pl.pallas_call(
        functools.partial(kernel, z),
        out_shape=[jax.ShapeDtypeStruct(*shape) for shape in shapes],
        in_specs=[VMEM] * len(operands),
        out_specs=[VMEM] * len(shapes),
        scratch_shapes=[pltpu.VMEM(*shape) for shape in scratch],
        compiler_params=pltpu.CompilerParams(vmem_limit_bytes=limit),
    )(*operands)


def far_layer(z, region, near):
    table, readout, emb_energy, onehot, anchors, sums, kept = near
    width = table.shape[1]
    cells, ring = z.block[0] * z.block[1], z.nax * z.nay
    offsets, most = len(z.offsets), max(len(z.split_offsets(y + 1)[1]) for y in range(z.block[1]))
    pair = (2, z.slots, LANES)
    shapes = [
        ((z.groups,) + z.block + (1, 3 * z.slots), jnp.float32),
        (z.block + (1, 3 * z.slots), jnp.float32),
        ((cells, 3, z.slots, LANES), jnp.float32),
        ((cells, z.rad * z.slots, 2 * z.spec), jnp.bfloat16),
        ((cells, z.slots, width), jnp.bfloat16),
        ((z.nx * 2 * HALO * z.groups, z.spec, LANES), jnp.bfloat16),
        ((z.nax * z.block[1], most) + pair, jnp.float32),
    ]
    scratch = [
        ((z.nax * 2, 4, z.slots, LANES), jnp.float32),
        ((z.nax * 2, offsets) + pair, jnp.float32),
        ((4, LANES, LANES), jnp.float32),
        ((ring, z.rad * z.slots, 2 * z.spec), jnp.bfloat16),
        ((ring, z.slots, z.rad * z.spec), jnp.bfloat16),
        ((cells * z.groups, 3, 8, LANES), jnp.float32),
    ]
    operands = (region, table, readout, onehot, anchors, sums, kept)
    return call(far_kernel, z, shapes, scratch, FAR_VMEM, operands)


def own_layer(z, region, near, far):
    table, readout, emb_energy, onehot, anchors, sums, kept = near
    shapes = [
        (z.block + (1, z.slots), jnp.float32),
        (z.block + (1, 3 * z.slots), jnp.float32),
    ]
    scratch = [((z.block[0] * z.block[1], 3, z.slots, LANES), jnp.float32)]
    operands = (region, readout, emb_energy, onehot, anchors, kept) + tuple(far)
    return call(own_kernel, z, shapes, scratch, OWN_VMEM, operands)


def on_device(positions, species, counts, embed, filters, w_up, w_energy):
    bx, by = positions.shape[:2]
    slots = species.shape[-1]
    width = embed.shape[1]
    depth = lax.axis_size("gz")
    merged = depth * positions.shape[2] == 2
    spec = -(-embed.shape[0] // LANES) * LANES
    z = Cells((bx, by), merged, filters.shape[1] // width, spec, slots)
    block = pack(positions, species, counts.reshape(bx, by))
    upward = [(i, (i + 1) % depth) for i in range(depth)]
    downward = [(b, a) for a, b in upward]
    low = lax.ppermute(block, "gz", upward)
    if merged:
        block = jnp.concatenate([block, low], axis=3)
    else:
        high = lax.ppermute(block, "gz", downward)
        empty = jnp.full_like(block, -1.0)
        block = jnp.concatenate(
            [jnp.concatenate([block, low], axis=3), jnp.concatenate([high, empty], axis=3)], axis=2
        )
    block = exchange(block, "gx", 0, HALO)
    near = near_layer(z, block, embed, filters, w_up, w_energy.reshape(1, width))
    region = exchange(block, "gy", 1, HALO)
    other, *far = far_layer(z, region, near)
    energies, own = own_layer(z, region, near, far)

    forces = own + lax.ppermute(other[0], "gz", downward)
    if not merged:
        forces = forces + lax.ppermute(other[1], "gz", upward)
    return energies, forces


def solution(mesh):
    in_specs = (
        P("gx", "gy", "gz", None),
        P("gx", "gy", "gz", None),
        P("gx", "gy", "gz"),
        P(),
        P(),
        P(),
        P(),
    )
    out_specs = (P("gx", "gy", "gz", None), P("gx", "gy", "gz", None))
    return jax.shard_map(
        on_device, mesh=mesh, in_specs=in_specs, out_specs=out_specs, check_vma=False
    )
```

```python
import functools

import jax
import jax.numpy as jnp
from jax import lax
from jax.experimental import pallas as pl
from jax.experimental.pallas import tpu as pltpu
from jax.sharding import PartitionSpec as P

MSG_SCALE = 0.1
HALO = 2
FAR_VMEM = 30 * 1024 * 1024
OWN_VMEM = 8 * 1024 * 1024
LANES = 128
STEP = 16
WIDE = 4
LAG = 2
GROUP = 2
LATER = 0
BEHIND = 0
FORCE_SCALE = 4.0 * MSG_SCALE
LOG2E = 1.4426950408889634
NT = (((1,), (1,)), ((), ()))
NN = (((1,), (0,)), ((), ()))


def exchange(block, axis, dim, width):
    count = lax.axis_size(axis)
    first = lax.slice_in_dim(block, 0, width, axis=dim)
    last = lax.slice_in_dim(block, block.shape[dim] - width, None, axis=dim)
    if count % 2 == 0:
        odd = lax.axis_index(axis) % 2 == 1
        whole = block.shape[dim] == width
        up = block if whole else jnp.where(odd, last, first)
        down = block if whole else jnp.where(odd, first, last)
        far = [(i, (i + 1) % count if i % 2 else (i - 1) % count) for i in range(count)]
        near = [(i, i - 1 if i % 2 else i + 1) for i in range(count)]
        from_far = lax.ppermute(up, axis, far)
        from_near = lax.ppermute(down, axis, near)
        low = jnp.where(odd, from_near, from_far)
        high = jnp.where(odd, from_far, from_near)
    else:
        forward = [(i, (i + 1) % count) for i in range(count)]
        low = lax.ppermute(last, axis, forward)
        high = lax.ppermute(first, axis, [(b, a) for a, b in forward])
    return jnp.concatenate([low, block, high], axis=dim)


def dot(a, b, dims, precision=None):
    return lax.dot_general(a, b, dims, precision=precision, preferred_element_type=jnp.float32)


def split(values):
    high = values.astype(jnp.bfloat16)
    return high, (values - high.astype(jnp.float32)).astype(jnp.bfloat16)


def thirds(rows):
    high = rows.astype(jnp.bfloat16)
    middle, low = split(rows - high.astype(jnp.float32))
    at = lax.broadcasted_iota(jnp.int32, rows.shape, 0)
    parts = [part.astype(jnp.float32) for part in (high, middle, low)]
    kept = jnp.where(at == 0, parts[0], jnp.where(at == 1, parts[1], jnp.where(at == 2, parts[2], 0.0)))
    return kept.astype(jnp.bfloat16)


class Cells:
    def __init__(self, block, merged, rad, spec, slots):
        self.block, self.merged, self.rad, self.spec, self.slots = block, merged, rad, spec, slots
        self.groups = 1 if merged else 2
        self.nax, self.nay = block[0] + 2, block[1] + 2
        self.nx, self.ny = block[0] + 2 * HALO, block[1] + 2 * HALO
        self.offsets = [
            (dx, dy, g) for dx in (-1, 0, 1) for dy in (-1, 0, 1) for g in range(self.groups)
        ]
        self.rows = [slice(r, r + STEP) for r in range(0, slots, STEP)]

    def inner(self, ay):
        return 1 <= ay <= self.block[1]

    def cell(self, ax, ay):
        if 1 <= ax <= self.block[0] and self.inner(ay):
            return (ax - 1) * self.block[1] + ay - 1
        return None

    def split_offsets(self, ay):
        near = [n for n, (_, dy, _) in enumerate(self.offsets) if self.inner(ay) and self.inner(ay + dy)]
        return near, [n for n in range(len(self.offsets)) if n not in near]

    def z_shift(self, g):
        lane = lax.broadcasted_iota(jnp.int32, (1, LANES), 1)
        if self.merged:
            return jnp.where(lane < self.slots, 0.0, 1.0)
        if g == 0:
            return jnp.where(lane < self.slots, 0.0, -1.0)
        return jnp.where(lane < self.slots, 1.0, 0.0)


def place_anchors(z, stage, rows, out):
    for q in range(4):
        for i, (ref, x, y) in enumerate(rows):
            stage[q, i:i + 1, :] = ref[x, y, q:q + 1, :]
        columns = stage[q].T
        for i in range(len(rows)):
            out[i, q] = jnp.broadcast_to(columns[0:z.slots, i:i + 1], (z.slots, LANES))


def place_onehot(z, ref, x, y, g, out, at):
    ids = lax.broadcasted_iota(jnp.int32, (z.spec, LANES), 0).astype(jnp.float32)
    out[at] = (ref[x, y, g * 4 + 3:g * 4 + 4, :] == ids).astype(jnp.bfloat16)


def target(ref, x, y, offset):
    dx, dy, g = offset
    row = ref[x, y, g * 4:g * 4 + 3, :]
    return row[0:1] + dx, row[1:2] + dy, row[2:3]


def weigh(z, position, anchor, offset, keep):
    tx, ty, tz = position
    shift = z.z_shift(offset[2])
    weights = [[] for _ in range(z.rad)]
    for c in z.rows:
        ex = tx - anchor[0, c, :]
        ey = ty - anchor[1, c, :]
        dz = tz - anchor[2, c, :]
        ez = jnp.abs(dz) - shift if z.merged else dz + shift
        s = ex * ex + ey * ey + ez * ez
        f = jnp.maximum(1.0 - s, 0.0)
        e = jnp.exp2(s * (-0.5 * LOG2E))
        keep[0, c, :] = f
        keep[1, c, :] = e
        f = f * f
        if offset == (0, 0, 0):
            row = lax.broadcasted_iota(jnp.int32, (STEP, LANES), 0) + c.start
            lane = lax.broadcasted_iota(jnp.int32, (STEP, LANES), 1)
            f = jnp.where(row == lane, 0.0, f)
        for k in range(z.rad):
            if k == 0:
                w = e * f
                e = e * e
            elif k == 1:
                w = w * e
            else:
                e = e * e * e
                w = w * e
            weights[k].append(w.astype(jnp.bfloat16))
    return jnp.concatenate([part for parts in weights for part in parts], axis=0)


def grouped(values):
    return [values[i:i + GROUP] for i in range(0, len(values), GROUP)]


def staggered(tasks, first, second, lag):
    results = []
    for t in range(len(tasks) + lag):
        if t < len(tasks):
            results.append(first(*tasks[t]))
        if t >= lag:
            second(results[t - lag], *tasks[t - lag])


def pack_kernel(counts_hbm, positions_hbm, species_hbm, out, counts, positions, species, arrived):
    arguments = [(counts_hbm, counts), (positions_hbm, positions), (species_hbm, species)]
    copies = [pltpu.make_async_copy(a, b, arrived.at[i]) for i, (a, b) in enumerate(arguments)]
    for copy in copies:
        copy.start()
    for copy in copies:
        copy.wait()
    slots = out.shape[3]
    lane = lax.broadcasted_iota(jnp.int32, (1, slots), 1)
    for x in range(out.shape[0]):
        for y in range(out.shape[1]):
            row = positions[x, y, 0:1, :]
            for q in range(3):
                out[x, y, q:q + 1, :] = row[:, q * slots:(q + 1) * slots]
            marked = jnp.where(lane < counts[x, y], species[x, y, 0:1, :], -1)
            out[x, y, 3:4, :] = marked.astype(jnp.float32)


def near_kernel(
    z, near, embed_hbm, filters_hbm, w_up_hbm, w_energy_hbm,
    table, readout, emb_energy, onehot, anchors, sums, kept,
    emb_pad, stage, embed, filters, w_up, w_energy, arrived,
):
    nspec, width = embed.shape
    by = z.block[1]
    weights = [(embed_hbm, embed), (filters_hbm, filters), (w_up_hbm, w_up), (w_energy_hbm, w_energy)]
    copies = [pltpu.make_async_copy(a, b, arrived.at[i]) for i, (a, b) in enumerate(weights)]
    for copy in copies:
        copy.start()

    for x in range(z.nx):
        for y in range(by):
            for g in range(z.groups):
                place_onehot(z, near, x, y, g, onehot, (x * by + y) * z.groups + g)
    place_anchors(z, stage, [(near, ax + 1, y) for ax in range(z.nax) for y in range(by)], anchors)

    def message_at(ax, carry):
        totals = {}

        def weigh_some(y, some):
            weights = []
            for n in some:
                dx, dy, _ = z.offsets[n]
                keep = kept.at[ax * by + y, z.split_offsets(y + 1)[0].index(n)]
                spot = target(near, ax + 1 + dx, y + dy, z.offsets[n])
                weights.append(weigh(z, spot, anchors.at[ax * by + y], z.offsets[n], keep))
            return jnp.concatenate(weights, axis=1)

        def gather_some(weights, y, some):
            spots = [z.offsets[n] for n in some]
            hots = [onehot[((ax + 1 + dx) * by + y + dy) * z.groups + g] for dx, dy, g in spots]
            term = dot(weights, jnp.concatenate(hots, axis=1), NT)
            totals[y] = totals[y] + term if y in totals else term

        staggered([(y, some) for y in range(by) for some in grouped(z.split_offsets(y + 1)[0])], weigh_some, gather_some, LAG)
        for y in range(by):
            sums[ax * by + y] = totals[y]
        return carry

    lax.fori_loop(0, z.nax, message_at, 0)

    for copy in copies:
        copy.wait()
    emb_pad[...] = jnp.zeros_like(emb_pad)
    emb_pad[0:nspec, :] = embed[...].astype(jnp.float32)
    emb = emb_pad[...]
    rows = dot(emb.astype(jnp.bfloat16), filters[...], NN).astype(jnp.bfloat16)
    for k in range(z.rad):
        table[k * z.spec:(k + 1) * z.spec, :] = rows[:, k * width:(k + 1) * width]
    energy_row = jnp.broadcast_to(w_energy[...], (8, width))
    readout[...] = dot(energy_row, w_up[...].astype(jnp.float32), NT, lax.Precision.HIGHEST)
    emb_energy[...] = dot(energy_row, emb, NT, lax.Precision.HIGHEST)


class Store:
    def __init__(self, z, onehot_near, onehot_far, anchors_near, anchors_far, kept_near, kept_own, kept_far):
        self.z = z
        self.onehots = (onehot_near, onehot_far)
        self.anchors = (anchors_near, anchors_far)
        self.kept = (kept_near, kept_own, kept_far)
        self.outer = [y for y in range(z.ny) if not HALO <= y < HALO + z.block[1]]

    def onehot(self, x, y, g):
        z = self.z
        if y in self.outer:
            return self.onehots[1][(x * len(self.outer) + self.outer.index(y)) * z.groups + g]
        return self.onehots[0][(x * z.block[1] + y - HALO) * z.groups + g]

    def anchor(self, ax, ay):
        if self.z.inner(ay):
            return self.anchors[0].at[ax * self.z.block[1] + ay - 1]
        return self.anchors[1].at[ax * 2 + (ay > 0)]

    def radial(self, ax, ay, n):
        if not self.z.inner(ay):
            return self.kept[2].at[ax * 2 + (ay > 0), n]
        near, far = self.z.split_offsets(ay)
        if n in near:
            return self.kept[0].at[ax * self.z.block[1] + ay - 1, near.index(n)]
        return self.kept[1].at[ax * self.z.block[1] + ay - 1, far.index(n)]


def pairs(z, store, region, ax, ay, n, gains, r):
    c = z.rows[r]
    dx, dy, g = z.offsets[n]
    tx, ty, tz = target(region, ax + 1 + dx, ay + 1 + dy, z.offsets[n])
    anchor, keep = store.anchor(ax, ay), store.radial(ax, ay, n)
    ex = tx - anchor[0, c, :]
    ey = ty - anchor[1, c, :]
    ez = tz - anchor[2, c, :]
    shift = z.z_shift(g)
    ez = ez + jnp.where(ez > 0.0, -shift, shift) if z.merged else ez + shift
    f = keep[0, c, :]
    e = keep[1, c, :]
    e2 = e * e
    plain = None
    for k in range(z.rad):
        if k == 1:
            e = e * e2
        elif k > 1:
            e2 = e2 * e2 * e2
            e = e * e2
        term = e * gains[k * STEP:(k + 1) * STEP]
        scaled = (0.25 * 3.0 ** k) * term
        plain, steep = (term, scaled) if plain is None else (plain + term, steep + scaled)
    return f * (f * steep + plain), (ex, ey, ez)


def blocks(z, store, region, work, back):
    tasks = [
        (ax, ay, table, some[first:first + WIDE], sums)
        for ax, ay, table, some, sums in work for first in range(0, len(some), WIDE)
    ]

    def spots_of(ax, ay, part):
        return [(ax + 1 + z.offsets[n][0], ay + 1 + z.offsets[n][1], z.offsets[n][2]) for n in part]

    def multiply(ax, ay, table, part, sums):
        hots = jnp.concatenate([store.onehot(*spot) for spot in spots_of(ax, ay, part)], axis=1)
        return dot(table[...], jnp.concatenate([hots, hots], axis=0), NN)

    def add_forces(gains, ax, ay, table, part, sums):
        totals = [[None] * 3 for _ in part]
        for r in range(len(z.rows)):
            some_gains = gains[r * z.rad * STEP:(r + 1) * z.rad * STEP]
            for i, n in enumerate(part):
                p, displace = pairs(z, store, region, ax, ay, n, some_gains[:, i * LANES:(i + 1) * LANES], r)
                for q in range(3):
                    term = p * displace[q]
                    if sums is not None:
                        sums[q][r] = term if sums[q][r] is None else sums[q][r] + term
                    if back is not None:
                        term = sum(term[j:j + 8] for j in range(8, STEP, 8)) + term[0:8]
                        totals[i][q] = term if totals[i][q] is None else totals[i][q] + term
        if back is not None:
            for (x, y, g), total in zip(spots_of(ax, ay, part), totals):
                for q in range(3):
                    back[((x - HALO) * z.block[1] + y - HALO) * z.groups + g, q] += total[q]

    staggered(tasks, multiply, add_forces, LATER)


def far_kernel(
    z, region, table, readout_ref, onehot_near, anchors_near, sums_near, kept_near,
    other, part, mine, adj_own, act_own, onehot_far, kept_own,
    anchors_far, kept_far, stage, adj_table, back,
):
    by = z.block[1]
    bf = jnp.bfloat16
    slots, spec, rad = z.slots, z.spec, z.rad
    readout = readout_ref[...]
    store = Store(z, onehot_near, onehot_far, anchors_near, anchors_far, kept_near, kept_own, kept_far)
    outer = store.outer

    for x in range(z.nx):
        for i, y in enumerate(outer):
            for g in range(z.groups):
                place_onehot(z, region, x, y, g, onehot_far, (x * len(outer) + i) * z.groups + g)
    place_anchors(
        z, stage, [(region, ax + 1, y) for ax in range(z.nax) for y in (1, z.ny - HALO)], anchors_far
    )

    def message_at(ax):
        totals = {ay: sums_near[ax * by + ay - 1] for ay in range(z.nay) if z.inner(ay)}

        def weigh_some(ay, some):
            weights = []
            for n in some:
                dx, dy, _ = z.offsets[n]
                spot = target(region, ax + 1 + dx, ay + 1 + dy, z.offsets[n])
                weights.append(weigh(z, spot, store.anchor(ax, ay), z.offsets[n], store.radial(ax, ay, n)))
            return jnp.concatenate(weights, axis=1)

        def gather_some(weights, ay, some):
            spots = [z.offsets[n] for n in some]
            hots = [store.onehot(ax + 1 + dx, ay + 1 + dy, g) for dx, dy, g in spots]
            term = dot(weights, jnp.concatenate(hots, axis=1), NT)
            totals[ay] = totals[ay] + term if ay in totals else term

        staggered([(ay, some) for ay in range(z.nay) for some in grouped(z.split_offsets(ay)[1])], weigh_some, gather_some, LAG)
        return [
            jnp.concatenate(
                [totals[ay][k * slots:(k + 1) * slots].astype(bf) for k in range(rad)], axis=1
            ) for ay in range(z.nay)
        ]

    def adj_at(ax, ay):
        if 0 < ax < z.nax - 1 and z.inner(ay):
            return adj_own.at[(ax - 1) * by + ay - 1]
        return adj_table.at[ax * z.nay + ay]

    def adjoint_of(mixed, ax):
        group = [(ax, ay) for ay in range(z.nay)]
        messages = dot(jnp.concatenate(mixed, axis=0), table[...], NN)
        adjoints = []
        for i, spot in enumerate(group):
            message = MSG_SCALE * messages[i * slots:(i + 1) * slots]
            sigmoid = 1.0 / (1.0 + jnp.exp(-message))
            if z.cell(*spot) is not None:
                act_own[z.cell(*spot)] = (message * sigmoid).astype(bf)
            slope = sigmoid * (1.0 + message * (1.0 - sigmoid)) * readout[0:1]
            adjoints.append(jnp.where(store.anchor(*spot)[3] >= 0.0, slope, 0.0).astype(bf))
        turned = dot(jnp.concatenate(adjoints, axis=0), table[...], NT)
        for i, spot in enumerate(group):
            out = adj_at(*spot)
            for r, c in enumerate(z.rows):
                high, low = split(turned[slots * i + c.start:slots * i + c.stop])
                for k in range(rad):
                    at = slice((r * rad + k) * STEP, (r * rad + k + 1) * STEP)
                    out[at, 0:spec] = high[:, k * spec:(k + 1) * spec]
                    out[at, spec:] = low[:, k * spec:(k + 1) * spec]

    staggered([(ax,) for ax in range(z.nax)], message_at, adjoint_of, BEHIND)

    back[...] = jnp.zeros_like(back)

    work = []
    for ax in range(z.nax):
        for ay in range(z.nay):
            some = [n for n, (dx, dy, _) in enumerate(z.offsets) if z.cell(ax + dx, ay + dy) is not None]
            sums = None if z.cell(ax, ay) is None else [[None] * len(z.rows) for _ in range(3)]
            work.append((ax, ay, adj_at(ax, ay), some, sums))
    blocks(z, store, region, work, back)
    for ax, ay, _, _, sums in work:
        if sums is not None:
            for q in range(3):
                for r, c in enumerate(z.rows):
                    mine[z.cell(ax, ay), q, c, :] = sums[q][r]

    for ox in range(z.block[0]):
        for oy in range(by):
            for g in range(z.groups):
                start = slots if g == 0 else 0
                for q in range(3):
                    row = FORCE_SCALE * jnp.sum(back[(ox * by + oy) * z.groups + g, q], axis=0, keepdims=True)
                    other[g, ox, oy, :, q * slots:(q + 1) * slots] = row[:, start:start + slots]
                    if g == 0:
                        part[ox, oy, :, q * slots:(q + 1) * slots] = row[:, 0:slots]


def own_kernel(
    z, region, readout, emb_energy, onehot_near, anchors_near, kept_near,
    part, mine_part, adj_own, act_own, onehot_far, kept_own,
    energies, own, mine,
):
    slots = z.slots
    store = Store(z, onehot_near, onehot_far, anchors_near, None, kept_near, kept_own, None)
    cells = [(ox, oy) for ox in range(z.block[0]) for oy in range(z.block[1])]
    work = []
    for o, (ox, oy) in enumerate(cells):
        some = [n for n, (dx, dy, _) in enumerate(z.offsets) if z.cell(ox + 1 + dx, oy + 1 + dy) is None]
        sums = [[mine_part[o, q, c, :] for c in z.rows] for q in range(3)]
        work.append((ox + 1, oy + 1, adj_own.at[o], some, sums))
    blocks(z, store, region, work, None)
    for o, (_, _, _, _, sums) in enumerate(work):
        for q in range(3):
            for r, c in enumerate(z.rows):
                mine[o, q, c, :] = sums[q][r]

    high, low = split(mine[...].reshape(len(cells) * 3 * slots, LANES))
    ones = jnp.ones((8, 2 * LANES), jnp.bfloat16)
    rows = dot(ones, jnp.concatenate([high, low], axis=1), NT)[0:1]
    for o, (ox, oy) in enumerate(cells):
        for q in range(3):
            at = (o * 3 + q) * slots
            lanes = slice(q * slots, (q + 1) * slots)
            own[ox, oy, :, lanes] = part[ox, oy, :, lanes] - FORCE_SCALE * rows[:, at:at + slots]

    hots = jnp.concatenate([store.onehot(ox + HALO, oy + HALO, 0)[:, 0:slots] for ox, oy in cells], axis=1)
    acts = jnp.concatenate([act_own[o] for o in range(len(cells))], axis=0)
    energy = dot(thirds(emb_energy[...]), hots, NN) + dot(thirds(readout[...]), acts, NT)
    energy = jnp.sum(energy, axis=0, keepdims=True)
    for o, (ox, oy) in enumerate(cells):
        marked = region[ox + HALO, oy + HALO, 3:4, 0:slots]
        energies[ox, oy, :, :] = jnp.where(marked >= 0.0, energy[:, o * slots:(o + 1) * slots], 0.0)


VMEM = pl.BlockSpec(memory_space=pltpu.VMEM)
HBM = pl.BlockSpec(memory_space=pltpu.HBM)


def in_hbm(*arrays):
    return [pltpu.with_memory_space_constraint(array, pltpu.HBM) for array in arrays]


def pack(positions, species, counts):
    bx, by, _, slots = species.shape
    return pl.pallas_call(
        pack_kernel,
        out_shape=jax.ShapeDtypeStruct((bx, by, 4, slots), jnp.float32),
        in_specs=[HBM] * 3,
        out_specs=VMEM,
        scratch_shapes=[
            pltpu.SMEM(counts.shape, counts.dtype),
            pltpu.VMEM(positions.shape, positions.dtype),
            pltpu.VMEM(species.shape, species.dtype),
            pltpu.SemaphoreType.DMA((3,)),
        ],
        compiler_params=pltpu.CompilerParams(vmem_limit_bytes=1024 * 1024),
    )(*in_hbm(counts, positions, species))


def near_layer(z, near, embed, filters, w_up, w_energy):
    width = embed.shape[1]
    by = z.block[1]
    cells, most = z.nax * by, max(len(z.split_offsets(y + 1)[0]) for y in range(by))
    shapes = [
        ((z.rad * z.spec, width), jnp.bfloat16),
        ((8, width), jnp.float32),
        ((8, z.spec), jnp.float32),
        ((z.nx * by * z.groups, z.spec, LANES), jnp.bfloat16),
        ((cells, 4, z.slots, LANES), jnp.float32),
        ((cells, z.rad * z.slots, z.spec), jnp.float32),
        ((cells, most, 2, z.slots, LANES), jnp.float32),
    ]
    flops = 2 * cells * most * z.rad * z.slots * LANES * z.spec
    return pl.pallas_call(
        functools.partial(near_kernel, z),
        out_shape=[jax.ShapeDtypeStruct(*shape) for shape in shapes],
        in_specs=[VMEM] + [HBM] * 4,
        out_specs=[VMEM] * len(shapes),
        scratch_shapes=[
            pltpu.VMEM((z.spec, width), jnp.float32),
            pltpu.VMEM((4, LANES, LANES), jnp.float32),
            pltpu.VMEM(embed.shape, embed.dtype),
            pltpu.VMEM(filters.shape, filters.dtype),
            pltpu.VMEM(w_up.shape, w_up.dtype),
            pltpu.VMEM(w_energy.shape, w_energy.dtype),
            pltpu.SemaphoreType.DMA((4,)),
        ],
        compiler_params=pltpu.CompilerParams(vmem_limit_bytes=12 * 1024 * 1024),
        cost_estimate=pl.CostEstimate(flops=flops, bytes_accessed=1 << 20, transcendentals=0),
    )(near, *in_hbm(embed, filters, w_up, w_energy))


def call(kernel, z, shapes, scratch, limit, operands):
    return pl.pallas_call(
        functools.partial(kernel, z),
        out_shape=[jax.ShapeDtypeStruct(*shape) for shape in shapes],
        in_specs=[VMEM] * len(operands),
        out_specs=[VMEM] * len(shapes),
        scratch_shapes=[pltpu.VMEM(*shape) for shape in scratch],
        compiler_params=pltpu.CompilerParams(vmem_limit_bytes=limit),
    )(*operands)


def far_layer(z, region, near):
    table, readout, emb_energy, onehot, anchors, sums, kept = near
    width = table.shape[1]
    cells, ring = z.block[0] * z.block[1], z.nax * z.nay
    offsets, most = len(z.offsets), max(len(z.split_offsets(y + 1)[1]) for y in range(z.block[1]))
    pair = (2, z.slots, LANES)
    shapes = [
        ((z.groups,) + z.block + (1, 3 * z.slots), jnp.float32),
        (z.block + (1, 3 * z.slots), jnp.float32),
        ((cells, 3, z.slots, LANES), jnp.float32),
        ((cells, z.rad * z.slots, 2 * z.spec), jnp.bfloat16),
        ((cells, z.slots, width), jnp.bfloat16),
        ((z.nx * 2 * HALO * z.groups, z.spec, LANES), jnp.bfloat16),
        ((z.nax * z.block[1], most) + pair, jnp.float32),
    ]
    scratch = [
        ((z.nax * 2, 4, z.slots, LANES), jnp.float32),
        ((z.nax * 2, offsets) + pair, jnp.float32),
        ((4, LANES, LANES), jnp.float32),
        ((ring, z.rad * z.slots, 2 * z.spec), jnp.bfloat16),
        ((cells * z.groups, 3, 8, LANES), jnp.float32),
    ]
    operands = (region, table, readout, onehot, anchors, sums, kept)
    return call(far_kernel, z, shapes, scratch, FAR_VMEM, operands)


def own_layer(z, region, near, far):
    table, readout, emb_energy, onehot, anchors, sums, kept = near
    shapes = [
        (z.block + (1, z.slots), jnp.float32),
        (z.block + (1, 3 * z.slots), jnp.float32),
    ]
    scratch = [((z.block[0] * z.block[1], 3, z.slots, LANES), jnp.float32)]
    operands = (region, readout, emb_energy, onehot, anchors, kept) + tuple(far)
    return call(own_kernel, z, shapes, scratch, OWN_VMEM, operands)


def on_device(positions, species, counts, embed, filters, w_up, w_energy):
    bx, by = positions.shape[:2]
    slots = species.shape[-1]
    width = embed.shape[1]
    depth = lax.axis_size("gz")
    merged = depth * positions.shape[2] == 2
    spec = -(-embed.shape[0] // LANES) * LANES
    z = Cells((bx, by), merged, filters.shape[1] // width, spec, slots)
    block = pack(positions, species, counts.reshape(bx, by))
    upward = [(i, (i + 1) % depth) for i in range(depth)]
    downward = [(b, a) for a, b in upward]
    low = lax.ppermute(block, "gz", upward)
    if merged:
        block = jnp.concatenate([block, low], axis=3)
    else:
        high = lax.ppermute(block, "gz", downward)
        empty = jnp.full_like(block, -1.0)
        block = jnp.concatenate(
            [jnp.concatenate([block, low], axis=3), jnp.concatenate([high, empty], axis=3)], axis=2
        )
    block = exchange(block, "gx", 0, HALO)
    near = near_layer(z, block, embed, filters, w_up, w_energy.reshape(1, width))
    region = exchange(block, "gy", 1, HALO)
    other, *far = far_layer(z, region, near)
    energies, own = own_layer(z, region, near, far)

    forces = own + lax.ppermute(other[0], "gz", downward)
    if not merged:
        forces = forces + lax.ppermute(other[1], "gz", upward)
    return energies, forces


def solution(mesh):
    in_specs = (
        P("gx", "gy", "gz", None),
        P("gx", "gy", "gz", None),
        P("gx", "gy", "gz"),
        P(),
        P(),
        P(),
        P(),
    )
    out_specs = (P("gx", "gy", "gz", None), P("gx", "gy", "gz", None))
    return jax.shard_map(
        on_device, mesh=mesh, in_specs=in_specs, out_specs=out_specs, check_vma=False
    )
```

```python
import functools

import jax
import jax.numpy as jnp
from jax import lax
from jax.experimental import pallas as pl
from jax.experimental.pallas import tpu as pltpu
from jax.sharding import PartitionSpec as P

MSG_SCALE = 0.1
HALO = 2
FAR_VMEM = 30 * 1024 * 1024
OWN_VMEM = 8 * 1024 * 1024
LANES = 128
STEP = 16
WIDE = 4
LAG = 0
GROUP = 2
LATER = 0
BEHIND = 0
FORCE_SCALE = 4.0 * MSG_SCALE
LOG2E = 1.4426950408889634
NT = (((1,), (1,)), ((), ()))
NN = (((1,), (0,)), ((), ()))


def exchange(block, axis, dim, width):
    count = lax.axis_size(axis)
    first = lax.slice_in_dim(block, 0, width, axis=dim)
    last = lax.slice_in_dim(block, block.shape[dim] - width, None, axis=dim)
    if count % 2 == 0:
        odd = lax.axis_index(axis) % 2 == 1
        whole = block.shape[dim] == width
        up = block if whole else jnp.where(odd, last, first)
        down = block if whole else jnp.where(odd, first, last)
        far = [(i, (i + 1) % count if i % 2 else (i - 1) % count) for i in range(count)]
        near = [(i, i - 1 if i % 2 else i + 1) for i in range(count)]
        from_far = lax.ppermute(up, axis, far)
        from_near = lax.ppermute(down, axis, near)
        low = jnp.where(odd, from_near, from_far)
        high = jnp.where(odd, from_far, from_near)
    else:
        forward = [(i, (i + 1) % count) for i in range(count)]
        low = lax.ppermute(last, axis, forward)
        high = lax.ppermute(first, axis, [(b, a) for a, b in forward])
    return jnp.concatenate([low, block, high], axis=dim)


def dot(a, b, dims, precision=None):
    return lax.dot_general(a, b, dims, precision=precision, preferred_element_type=jnp.float32)


def split(values):
    high = values.astype(jnp.bfloat16)
    return high, (values - high.astype(jnp.float32)).astype(jnp.bfloat16)


def thirds(rows):
    high = rows.astype(jnp.bfloat16)
    middle, low = split(rows - high.astype(jnp.float32))
    at = lax.broadcasted_iota(jnp.int32, rows.shape, 0)
    parts = [part.astype(jnp.float32) for part in (high, middle, low)]
    kept = jnp.where(at == 0, parts[0], jnp.where(at == 1, parts[1], jnp.where(at == 2, parts[2], 0.0)))
    return kept.astype(jnp.bfloat16)


class Cells:
    def __init__(self, block, merged, rad, spec, slots):
        self.block, self.merged, self.rad, self.spec, self.slots = block, merged, rad, spec, slots
        self.groups = 1 if merged else 2
        self.nax, self.nay = block[0] + 2, block[1] + 2
        self.nx, self.ny = block[0] + 2 * HALO, block[1] + 2 * HALO
        self.offsets = [
            (dx, dy, g) for dx in (-1, 0, 1) for dy in (-1, 0, 1) for g in range(self.groups)
        ]
        self.rows = [slice(r, r + STEP) for r in range(0, slots, STEP)]

    def inner(self, ay):
        return 1 <= ay <= self.block[1]

    def cell(self, ax, ay):
        if 1 <= ax <= self.block[0] and self.inner(ay):
            return (ax - 1) * self.block[1] + ay - 1
        return None

    def split_offsets(self, ay):
        near = [n for n, (_, dy, _) in enumerate(self.offsets) if self.inner(ay) and self.inner(ay + dy)]
        return near, [n for n in range(len(self.offsets)) if n not in near]

    def z_shift(self, g):
        lane = lax.broadcasted_iota(jnp.int32, (1, LANES), 1)
        if self.merged:
            return jnp.where(lane < self.slots, 0.0, 1.0)
        if g == 0:
            return jnp.where(lane < self.slots, 0.0, -1.0)
        return jnp.where(lane < self.slots, 1.0, 0.0)


def place_anchors(z, stage, rows, out):
    for q in range(4):
        for i, (ref, x, y) in enumerate(rows):
            stage[q, i:i + 1, :] = ref[x, y, q:q + 1, :]
        columns = stage[q].T
        for i in range(len(rows)):
            out[i, q] = jnp.broadcast_to(columns[0:z.slots, i:i + 1], (z.slots, LANES))


def place_onehot(z, ref, x, y, g, out, at):
    ids = lax.broadcasted_iota(jnp.int32, (z.spec, LANES), 0).astype(jnp.float32)
    out[at] = (ref[x, y, g * 4 + 3:g * 4 + 4, :] == ids).astype(jnp.bfloat16)


def target(ref, x, y, offset):
    dx, dy, g = offset
    row = ref[x, y, g * 4:g * 4 + 3, :]
    return row[0:1] + dx, row[1:2] + dy, row[2:3]


def weigh(z, position, anchor, offset, keep):
    tx, ty, tz = position
    shift = z.z_shift(offset[2])
    weights = [[] for _ in range(z.rad)]
    for c in z.rows:
        ex = tx - anchor[0, c, :]
        ey = ty - anchor[1, c, :]
        dz = tz - anchor[2, c, :]
        ez = jnp.abs(dz) - shift if z.merged else dz + shift
        s = ex * ex + ey * ey + ez * ez
        f = jnp.maximum(1.0 - s, 0.0)
        e = jnp.exp2(s * (-0.5 * LOG2E))
        keep[0, c, :] = f
        keep[1, c, :] = e
        f = f * f
        if offset == (0, 0, 0):
            row = lax.broadcasted_iota(jnp.int32, (STEP, LANES), 0) + c.start
            lane = lax.broadcasted_iota(jnp.int32, (STEP, LANES), 1)
            f = jnp.where(row == lane, 0.0, f)
        for k in range(z.rad):
            if k == 0:
                w = e * f
                e = e * e
            elif k == 1:
                w = w * e
            else:
                e = e * e * e
                w = w * e
            weights[k].append(w.astype(jnp.bfloat16))
    return jnp.concatenate([part for parts in weights for part in parts], axis=0)


def grouped(values):
    return [values[i:i + GROUP] for i in range(0, len(values), GROUP)]


def staggered(tasks, first, second, lag):
    results = []
    for t in range(len(tasks) + lag):
        if t < len(tasks):
            results.append(first(*tasks[t]))
        if t >= lag:
            second(results[t - lag], *tasks[t - lag])


def pack_kernel(counts_hbm, positions_hbm, species_hbm, out, counts, positions, species, arrived):
    arguments = [(counts_hbm, counts), (positions_hbm, positions), (species_hbm, species)]
    copies = [pltpu.make_async_copy(a, b, arrived.at[i]) for i, (a, b) in enumerate(arguments)]
    for copy in copies:
        copy.start()
    for copy in copies:
        copy.wait()
    slots = out.shape[3]
    lane = lax.broadcasted_iota(jnp.int32, (1, slots), 1)
    for x in range(out.shape[0]):
        for y in range(out.shape[1]):
            row = positions[x, y, 0:1, :]
            for q in range(3):
                out[x, y, q:q + 1, :] = row[:, q * slots:(q + 1) * slots]
            marked = jnp.where(lane < counts[x, y], species[x, y, 0:1, :], -1)
            out[x, y, 3:4, :] = marked.astype(jnp.float32)


def near_kernel(
    z, near, embed_hbm, filters_hbm, w_up_hbm, w_energy_hbm,
    table, readout, emb_energy, onehot, anchors, sums, kept,
    emb_pad, stage, embed, filters, w_up, w_energy, arrived,
):
    nspec, width = embed.shape
    by = z.block[1]
    weights = [(embed_hbm, embed), (filters_hbm, filters), (w_up_hbm, w_up), (w_energy_hbm, w_energy)]
    copies = [pltpu.make_async_copy(a, b, arrived.at[i]) for i, (a, b) in enumerate(weights)]
    for copy in copies:
        copy.start()

    for x in range(z.nx):
        for y in range(by):
            for g in range(z.groups):
                place_onehot(z, near, x, y, g, onehot, (x * by + y) * z.groups + g)
    place_anchors(z, stage, [(near, ax + 1, y) for ax in range(z.nax) for y in range(by)], anchors)

    def message_at(ax, carry):
        totals = {}

        def weigh_some(y, some):
            weights = []
            for n in some:
                dx, dy, _ = z.offsets[n]
                keep = kept.at[ax * by + y, z.split_offsets(y + 1)[0].index(n)]
                spot = target(near, ax + 1 + dx, y + dy, z.offsets[n])
                weights.append(weigh(z, spot, anchors.at[ax * by + y], z.offsets[n], keep))
            return jnp.concatenate(weights, axis=1)

        def gather_some(weights, y, some):
            spots = [z.offsets[n] for n in some]
            hots = [onehot[((ax + 1 + dx) * by + y + dy) * z.groups + g] for dx, dy, g in spots]
            term = dot(weights, jnp.concatenate(hots, axis=1), NT)
            totals[y] = totals[y] + term if y in totals else term

        staggered([(y, some) for y in range(by) for some in grouped(z.split_offsets(y + 1)[0])], weigh_some, gather_some, LAG)
        for y in range(by):
            sums[ax * by + y] = totals[y]
        return carry

    lax.fori_loop(0, z.nax, message_at, 0)

    for copy in copies:
        copy.wait()
    emb_pad[...] = jnp.zeros_like(emb_pad)
    emb_pad[0:nspec, :] = embed[...].astype(jnp.float32)
    emb = emb_pad[...]
    rows = dot(emb.astype(jnp.bfloat16), filters[...], NN).astype(jnp.bfloat16)
    for k in range(z.rad):
        table[k * z.spec:(k + 1) * z.spec, :] = rows[:, k * width:(k + 1) * width]
    energy_row = jnp.broadcast_to(w_energy[...], (8, width))
    readout[...] = dot(energy_row, w_up[...].astype(jnp.float32), NT, lax.Precision.HIGHEST)
    emb_energy[...] = dot(energy_row, emb, NT, lax.Precision.HIGHEST)


class Store:
    def __init__(self, z, onehot_near, onehot_far, anchors_near, anchors_far, kept_near, kept_own, kept_far):
        self.z = z
        self.onehots = (onehot_near, onehot_far)
        self.anchors = (anchors_near, anchors_far)
        self.kept = (kept_near, kept_own, kept_far)
        self.outer = [y for y in range(z.ny) if not HALO <= y < HALO + z.block[1]]

    def onehot(self, x, y, g):
        z = self.z
        if y in self.outer:
            return self.onehots[1][(x * len(self.outer) + self.outer.index(y)) * z.groups + g]
        return self.onehots[0][(x * z.block[1] + y - HALO) * z.groups + g]

    def anchor(self, ax, ay):
        if self.z.inner(ay):
            return self.anchors[0].at[ax * self.z.block[1] + ay - 1]
        return self.anchors[1].at[ax * 2 + (ay > 0)]

    def radial(self, ax, ay, n):
        if not self.z.inner(ay):
            return self.kept[2].at[ax * 2 + (ay > 0), n]
        near, far = self.z.split_offsets(ay)
        if n in near:
            return self.kept[0].at[ax * self.z.block[1] + ay - 1, near.index(n)]
        return self.kept[1].at[ax * self.z.block[1] + ay - 1, far.index(n)]


def pairs(z, store, region, ax, ay, n, gains, r):
    c = z.rows[r]
    dx, dy, g = z.offsets[n]
    tx, ty, tz = target(region, ax + 1 + dx, ay + 1 + dy, z.offsets[n])
    anchor, keep = store.anchor(ax, ay), store.radial(ax, ay, n)
    ex = tx - anchor[0, c, :]
    ey = ty - anchor[1, c, :]
    ez = tz - anchor[2, c, :]
    shift = z.z_shift(g)
    ez = ez + jnp.where(ez > 0.0, -shift, shift) if z.merged else ez + shift
    f = keep[0, c, :]
    e = keep[1, c, :]
    e2 = e * e
    plain = None
    for k in range(z.rad):
        if k == 1:
            e = e * e2
        elif k > 1:
            e2 = e2 * e2 * e2
            e = e * e2
        term = e * gains[k * STEP:(k + 1) * STEP]
        scaled = (0.25 * 3.0 ** k) * term
        plain, steep = (term, scaled) if plain is None else (plain + term, steep + scaled)
    return f * (f * steep + plain), (ex, ey, ez)


def blocks(z, store, region, work, back):
    tasks = [
        (ax, ay, table, some[first:first + WIDE], sums)
        for ax, ay, table, some, sums in work for first in range(0, len(some), WIDE)
    ]

    def spots_of(ax, ay, part):
        return [(ax + 1 + z.offsets[n][0], ay + 1 + z.offsets[n][1], z.offsets[n][2]) for n in part]

    def multiply(ax, ay, table, part, sums):
        hots = jnp.concatenate([store.onehot(*spot) for spot in spots_of(ax, ay, part)], axis=1)
        return dot(table[...], jnp.concatenate([hots, hots], axis=0), NN)

    def add_forces(gains, ax, ay, table, part, sums):
        totals = [[None] * 3 for _ in part]
        for r in range(len(z.rows)):
            some_gains = gains[r * z.rad * STEP:(r + 1) * z.rad * STEP]
            for i, n in enumerate(part):
                p, displace = pairs(z, store, region, ax, ay, n, some_gains[:, i * LANES:(i + 1) * LANES], r)
                for q in range(3):
                    term = p * displace[q]
                    if sums is not None:
                        sums[q][r] = term if sums[q][r] is None else sums[q][r] + term
                    if back is not None:
                        term = sum(term[j:j + 8] for j in range(8, STEP, 8)) + term[0:8]
                        totals[i][q] = term if totals[i][q] is None else totals[i][q] + term
        if back is not None:
            for (x, y, g), total in zip(spots_of(ax, ay, part), totals):
                for q in range(3):
                    back[((x - HALO) * z.block[1] + y - HALO) * z.groups + g, q] += total[q]

    staggered(tasks, multiply, add_forces, LATER)


def far_kernel(
    z, region, table, readout_ref, onehot_near, anchors_near, sums_near, kept_near,
    other, part, mine, adj_own, act_own, onehot_far, kept_own,
    anchors_far, kept_far, stage, adj_table, back,
):
    by = z.block[1]
    bf = jnp.bfloat16
    slots, spec, rad = z.slots, z.spec, z.rad
    readout = readout_ref[...]
    store = Store(z, onehot_near, onehot_far, anchors_near, anchors_far, kept_near, kept_own, kept_far)
    outer = store.outer

    for x in range(z.nx):
        for i, y in enumerate(outer):
            for g in range(z.groups):
                place_onehot(z, region, x, y, g, onehot_far, (x * len(outer) + i) * z.groups + g)
    place_anchors(
        z, stage, [(region, ax + 1, y) for ax in range(z.nax) for y in (1, z.ny - HALO)], anchors_far
    )

    def message_at(ax):
        totals = {ay: sums_near[ax * by + ay - 1] for ay in range(z.nay) if z.inner(ay)}

        def weigh_some(ay, some):
            weights = []
            for n in some:
                dx, dy, _ = z.offsets[n]
                spot = target(region, ax + 1 + dx, ay + 1 + dy, z.offsets[n])
                weights.append(weigh(z, spot, store.anchor(ax, ay), z.offsets[n], store.radial(ax, ay, n)))
            return jnp.concatenate(weights, axis=1)

        def gather_some(weights, ay, some):
            spots = [z.offsets[n] for n in some]
            hots = [store.onehot(ax + 1 + dx, ay + 1 + dy, g) for dx, dy, g in spots]
            term = dot(weights, jnp.concatenate(hots, axis=1), NT)
            totals[ay] = totals[ay] + term if ay in totals else term

        staggered([(ay, some) for ay in range(z.nay) for some in grouped(z.split_offsets(ay)[1])], weigh_some, gather_some, LAG)
        return [
            jnp.concatenate(
                [totals[ay][k * slots:(k + 1) * slots].astype(bf) for k in range(rad)], axis=1
            ) for ay in range(z.nay)
        ]

    def adj_at(ax, ay):
        if 0 < ax < z.nax - 1 and z.inner(ay):
            return adj_own.at[(ax - 1) * by + ay - 1]
        return adj_table.at[ax * z.nay + ay]

    def adjoint_of(mixed, ax):
        group = [(ax, ay) for ay in range(z.nay)]
        messages = dot(jnp.concatenate(mixed, axis=0), table[...], NN)
        adjoints = []
        for i, spot in enumerate(group):
            message = MSG_SCALE * messages[i * slots:(i + 1) * slots]
            sigmoid = 1.0 / (1.0 + jnp.exp(-message))
            if z.cell(*spot) is not None:
                act_own[z.cell(*spot)] = (message * sigmoid).astype(bf)
            slope = sigmoid * (1.0 + message * (1.0 - sigmoid)) * readout[0:1]
            adjoints.append(jnp.where(store.anchor(*spot)[3] >= 0.0, slope, 0.0).astype(bf))
        turned = dot(jnp.concatenate(adjoints, axis=0), table[...], NT)
        for i, spot in enumerate(group):
            out = adj_at(*spot)
            for r, c in enumerate(z.rows):
                high, low = split(turned[slots * i + c.start:slots * i + c.stop])
                for k in range(rad):
                    at = slice((r * rad + k) * STEP, (r * rad + k + 1) * STEP)
                    out[at, 0:spec] = high[:, k * spec:(k + 1) * spec]
                    out[at, spec:] = low[:, k * spec:(k + 1) * spec]

    staggered([(ax,) for ax in range(z.nax)], message_at, adjoint_of, BEHIND)

    back[...] = jnp.zeros_like(back)

    work = []
    for ax in range(z.nax):
        for ay in range(z.nay):
            some = [n for n, (dx, dy, _) in enumerate(z.offsets) if z.cell(ax + dx, ay + dy) is not None]
            sums = None if z.cell(ax, ay) is None else [[None] * len(z.rows) for _ in range(3)]
            work.append((ax, ay, adj_at(ax, ay), some, sums))
    blocks(z, store, region, work, back)
    for ax, ay, _, _, sums in work:
        if sums is not None:
            for q in range(3):
                for r, c in enumerate(z.rows):
                    mine[z.cell(ax, ay), q, c, :] = sums[q][r]

    for ox in range(z.block[0]):
        for oy in range(by):
            for g in range(z.groups):
                start = slots if g == 0 else 0
                for q in range(3):
                    row = FORCE_SCALE * jnp.sum(back[(ox * by + oy) * z.groups + g, q], axis=0, keepdims=True)
                    other[g, ox, oy, :, q * slots:(q + 1) * slots] = row[:, start:start + slots]
                    if g == 0:
                        part[ox, oy, :, q * slots:(q + 1) * slots] = row[:, 0:slots]


def own_kernel(
    z, region, readout, emb_energy, onehot_near, anchors_near, kept_near,
    part, mine_part, adj_own, act_own, onehot_far, kept_own,
    energies, own, mine,
):
    slots = z.slots
    store = Store(z, onehot_near, onehot_far, anchors_near, None, kept_near, kept_own, None)
    cells = [(ox, oy) for ox in range(z.block[0]) for oy in range(z.block[1])]
    hots = jnp.concatenate([store.onehot(ox + HALO, oy + HALO, 0)[:, 0:slots] for ox, oy in cells], axis=1)
    acts = jnp.concatenate([act_own[o] for o in range(len(cells))], axis=0)
    energy = dot(thirds(emb_energy[...]), hots, NN) + dot(thirds(readout[...]), acts, NT)
    energy = jnp.sum(energy, axis=0, keepdims=True)
    for o, (ox, oy) in enumerate(cells):
        marked = region[ox + HALO, oy + HALO, 3:4, 0:slots]
        energies[ox, oy, :, :] = jnp.where(marked >= 0.0, energy[:, o * slots:(o + 1) * slots], 0.0)

    work = []
    for o, (ox, oy) in enumerate(cells):
        some = [n for n, (dx, dy, _) in enumerate(z.offsets) if z.cell(ox + 1 + dx, oy + 1 + dy) is None]
        sums = [[mine_part[o, q, c, :] for c in z.rows] for q in range(3)]
        work.append((ox + 1, oy + 1, adj_own.at[o], some, sums))
    blocks(z, store, region, work, None)
    for o, (_, _, _, _, sums) in enumerate(work):
        for q in range(3):
            for r, c in enumerate(z.rows):
                mine[o, q, c, :] = sums[q][r]

    high, low = split(mine[...].reshape(len(cells) * 3 * slots, LANES))
    ones = jnp.ones((8, 2 * LANES), jnp.bfloat16)
    rows = dot(ones, jnp.concatenate([high, low], axis=1), NT)[0:1]
    for o, (ox, oy) in enumerate(cells):
        for q in range(3):
            at = (o * 3 + q) * slots
            lanes = slice(q * slots, (q + 1) * slots)
            own[ox, oy, :, lanes] = part[ox, oy, :, lanes] - FORCE_SCALE * rows[:, at:at + slots]


VMEM = pl.BlockSpec(memory_space=pltpu.VMEM)
HBM = pl.BlockSpec(memory_space=pltpu.HBM)


def in_hbm(*arrays):
    return [pltpu.with_memory_space_constraint(array, pltpu.HBM) for array in arrays]


def pack(positions, species, counts):
    bx, by, _, slots = species.shape
    return pl.pallas_call(
        pack_kernel,
        out_shape=jax.ShapeDtypeStruct((bx, by, 4, slots), jnp.float32),
        in_specs=[HBM] * 3,
        out_specs=VMEM,
        scratch_shapes=[
            pltpu.SMEM(counts.shape, counts.dtype),
            pltpu.VMEM(positions.shape, positions.dtype),
            pltpu.VMEM(species.shape, species.dtype),
            pltpu.SemaphoreType.DMA((3,)),
        ],
        compiler_params=pltpu.CompilerParams(vmem_limit_bytes=1024 * 1024),
    )(*in_hbm(counts, positions, species))


def near_layer(z, near, embed, filters, w_up, w_energy):
    width = embed.shape[1]
    by = z.block[1]
    cells, most = z.nax * by, max(len(z.split_offsets(y + 1)[0]) for y in range(by))
    shapes = [
        ((z.rad * z.spec, width), jnp.bfloat16),
        ((8, width), jnp.float32),
        ((8, z.spec), jnp.float32),
        ((z.nx * by * z.groups, z.spec, LANES), jnp.bfloat16),
        ((cells, 4, z.slots, LANES), jnp.float32),
        ((cells, z.rad * z.slots, z.spec), jnp.float32),
        ((cells, most, 2, z.slots, LANES), jnp.float32),
    ]
    flops = 2 * cells * most * z.rad * z.slots * LANES * z.spec
    return pl.pallas_call(
        functools.partial(near_kernel, z),
        out_shape=[jax.ShapeDtypeStruct(*shape) for shape in shapes],
        in_specs=[VMEM] + [HBM] * 4,
        out_specs=[VMEM] * len(shapes),
        scratch_shapes=[
            pltpu.VMEM((z.spec, width), jnp.float32),
            pltpu.VMEM((4, LANES, LANES), jnp.float32),
            pltpu.VMEM(embed.shape, embed.dtype),
            pltpu.VMEM(filters.shape, filters.dtype),
            pltpu.VMEM(w_up.shape, w_up.dtype),
            pltpu.VMEM(w_energy.shape, w_energy.dtype),
            pltpu.SemaphoreType.DMA((4,)),
        ],
        compiler_params=pltpu.CompilerParams(vmem_limit_bytes=12 * 1024 * 1024),
        cost_estimate=pl.CostEstimate(flops=flops, bytes_accessed=1 << 20, transcendentals=0),
    )(near, *in_hbm(embed, filters, w_up, w_energy))


def call(kernel, z, shapes, scratch, limit, operands):
    return pl.pallas_call(
        functools.partial(kernel, z),
        out_shape=[jax.ShapeDtypeStruct(*shape) for shape in shapes],
        in_specs=[VMEM] * len(operands),
        out_specs=[VMEM] * len(shapes),
        scratch_shapes=[pltpu.VMEM(*shape) for shape in scratch],
        compiler_params=pltpu.CompilerParams(vmem_limit_bytes=limit),
    )(*operands)


def far_layer(z, region, near):
    table, readout, emb_energy, onehot, anchors, sums, kept = near
    width = table.shape[1]
    cells, ring = z.block[0] * z.block[1], z.nax * z.nay
    offsets, most = len(z.offsets), max(len(z.split_offsets(y + 1)[1]) for y in range(z.block[1]))
    pair = (2, z.slots, LANES)
    shapes = [
        ((z.groups,) + z.block + (1, 3 * z.slots), jnp.float32),
        (z.block + (1, 3 * z.slots), jnp.float32),
        ((cells, 3, z.slots, LANES), jnp.float32),
        ((cells, z.rad * z.slots, 2 * z.spec), jnp.bfloat16),
        ((cells, z.slots, width), jnp.bfloat16),
        ((z.nx * 2 * HALO * z.groups, z.spec, LANES), jnp.bfloat16),
        ((z.nax * z.block[1], most) + pair, jnp.float32),
    ]
    scratch = [
        ((z.nax * 2, 4, z.slots, LANES), jnp.float32),
        ((z.nax * 2, offsets) + pair, jnp.float32),
        ((4, LANES, LANES), jnp.float32),
        ((ring, z.rad * z.slots, 2 * z.spec), jnp.bfloat16),
        ((cells * z.groups, 3, 8, LANES), jnp.float32),
    ]
    operands = (region, table, readout, onehot, anchors, sums, kept)
    return call(far_kernel, z, shapes, scratch, FAR_VMEM, operands)


def own_layer(z, region, near, far):
    table, readout, emb_energy, onehot, anchors, sums, kept = near
    shapes = [
        (z.block + (1, z.slots), jnp.float32),
        (z.block + (1, 3 * z.slots), jnp.float32),
    ]
    scratch = [((z.block[0] * z.block[1], 3, z.slots, LANES), jnp.float32)]
    operands = (region, readout, emb_energy, onehot, anchors, kept) + tuple(far)
    return call(own_kernel, z, shapes, scratch, OWN_VMEM, operands)


def on_device(positions, species, counts, embed, filters, w_up, w_energy):
    bx, by = positions.shape[:2]
    slots = species.shape[-1]
    width = embed.shape[1]
    depth = lax.axis_size("gz")
    merged = depth * positions.shape[2] == 2
    spec = -(-embed.shape[0] // LANES) * LANES
    z = Cells((bx, by), merged, filters.shape[1] // width, spec, slots)
    block = pack(positions, species, counts.reshape(bx, by))
    upward = [(i, (i + 1) % depth) for i in range(depth)]
    downward = [(b, a) for a, b in upward]
    low = lax.ppermute(block, "gz", upward)
    if merged:
        block = jnp.concatenate([block, low], axis=3)
    else:
        high = lax.ppermute(block, "gz", downward)
        empty = jnp.full_like(block, -1.0)
        block = jnp.concatenate(
            [jnp.concatenate([block, low], axis=3), jnp.concatenate([high, empty], axis=3)], axis=2
        )
    block = exchange(block, "gx", 0, HALO)
    near = near_layer(z, block, embed, filters, w_up, w_energy.reshape(1, width))
    region = exchange(block, "gy", 1, HALO)
    other, *far = far_layer(z, region, near)
    energies, own = own_layer(z, region, near, far)

    forces = own + lax.ppermute(other[0], "gz", downward)
    if not merged:
        forces = forces + lax.ppermute(other[1], "gz", upward)
    return energies, forces


def solution(mesh):
    in_specs = (
        P("gx", "gy", "gz", None),
        P("gx", "gy", "gz", None),
        P("gx", "gy", "gz"),
        P(),
        P(),
        P(),
        P(),
    )
    out_specs = (P("gx", "gy", "gz", None), P("gx", "gy", "gz", None))
    return jax.shard_map(
        on_device, mesh=mesh, in_specs=in_specs, out_specs=out_specs, check_vma=False
    )
```

```python
import functools

import jax
import jax.numpy as jnp
from jax import lax
from jax.experimental import pallas as pl
from jax.experimental.pallas import tpu as pltpu
from jax.sharding import PartitionSpec as P

MSG_SCALE = 0.1
HALO = 2
FAR_VMEM = 30 * 1024 * 1024
OWN_VMEM = 8 * 1024 * 1024
LANES = 128
STEP = 16
WIDE = 4
LAG = 0
GROUP = 2
LATER = 0
BEHIND = 0
FORCE_SCALE = 4.0 * MSG_SCALE
LOG2E = 1.4426950408889634
NT = (((1,), (1,)), ((), ()))
NN = (((1,), (0,)), ((), ()))


def exchange(block, axis, dim, width):
    count = lax.axis_size(axis)
    first = lax.slice_in_dim(block, 0, width, axis=dim)
    last = lax.slice_in_dim(block, block.shape[dim] - width, None, axis=dim)
    if count % 2 == 0:
        odd = lax.axis_index(axis) % 2 == 1
        whole = block.shape[dim] == width
        up = block if whole else jnp.where(odd, last, first)
        down = block if whole else jnp.where(odd, first, last)
        far = [(i, (i + 1) % count if i % 2 else (i - 1) % count) for i in range(count)]
        near = [(i, i - 1 if i % 2 else i + 1) for i in range(count)]
        from_far = lax.ppermute(up, axis, far)
        from_near = lax.ppermute(down, axis, near)
        low = jnp.where(odd, from_near, from_far)
        high = jnp.where(odd, from_far, from_near)
    else:
        forward = [(i, (i + 1) % count) for i in range(count)]
        low = lax.ppermute(last, axis, forward)
        high = lax.ppermute(first, axis, [(b, a) for a, b in forward])
    return jnp.concatenate([low, block, high], axis=dim)


def dot(a, b, dims, precision=None):
    return lax.dot_general(a, b, dims, precision=precision, preferred_element_type=jnp.float32)


def split(values):
    high = values.astype(jnp.bfloat16)
    return high, (values - high.astype(jnp.float32)).astype(jnp.bfloat16)


def thirds(rows):
    high = rows.astype(jnp.bfloat16)
    middle, low = split(rows - high.astype(jnp.float32))
    at = lax.broadcasted_iota(jnp.int32, rows.shape, 0)
    parts = [part.astype(jnp.float32) for part in (high, middle, low)]
    kept = jnp.where(at == 0, parts[0], jnp.where(at == 1, parts[1], jnp.where(at == 2, parts[2], 0.0)))
    return kept.astype(jnp.bfloat16)


class Cells:
    def __init__(self, block, merged, rad, spec, slots):
        self.block, self.merged, self.rad, self.spec, self.slots = block, merged, rad, spec, slots
        self.groups = 1 if merged else 2
        self.nax, self.nay = block[0] + 2, block[1] + 2
        self.nx, self.ny = block[0] + 2 * HALO, block[1] + 2 * HALO
        self.offsets = [
            (dx, dy, g) for dx in (-1, 0, 1) for dy in (-1, 0, 1) for g in range(self.groups)
        ]
        self.rows = [slice(r, r + STEP) for r in range(0, slots, STEP)]

    def inner(self, ay):
        return 1 <= ay <= self.block[1]

    def cell(self, ax, ay):
        if 1 <= ax <= self.block[0] and self.inner(ay):
            return (ax - 1) * self.block[1] + ay - 1
        return None

    def split_offsets(self, ay):
        near = [n for n, (_, dy, _) in enumerate(self.offsets) if self.inner(ay) and self.inner(ay + dy)]
        return near, [n for n in range(len(self.offsets)) if n not in near]

    def z_shift(self, g):
        lane = lax.broadcasted_iota(jnp.int32, (1, LANES), 1)
        if self.merged:
            return jnp.where(lane < self.slots, 0.0, 1.0)
        if g == 0:
            return jnp.where(lane < self.slots, 0.0, -1.0)
        return jnp.where(lane < self.slots, 1.0, 0.0)


def place_anchors(z, stage, rows, out):
    for q in range(4):
        for i, (ref, x, y) in enumerate(rows):
            stage[q, i:i + 1, :] = ref[x, y, q:q + 1, :]
        columns = stage[q].T
        for i in range(len(rows)):
            out[i, q] = jnp.broadcast_to(columns[0:z.slots, i:i + 1], (z.slots, LANES))


def place_onehot(z, ref, x, y, g, out, at):
    ids = lax.broadcasted_iota(jnp.int32, (z.spec, LANES), 0).astype(jnp.float32)
    out[at] = (ref[x, y, g * 4 + 3:g * 4 + 4, :] == ids).astype(jnp.bfloat16)


def target(ref, x, y, offset):
    dx, dy, g = offset
    row = ref[x, y, g * 4:g * 4 + 3, :]
    return row[0:1] + dx, row[1:2] + dy, row[2:3]


def weigh(z, position, anchor, offset, keep):
    tx, ty, tz = position
    shift = z.z_shift(offset[2])
    weights = [[] for _ in range(z.rad)]
    for c in z.rows:
        ex = tx - anchor[0, c, :]
        ey = ty - anchor[1, c, :]
        dz = tz - anchor[2, c, :]
        ez = jnp.abs(dz) - shift if z.merged else dz + shift
        s = ex * ex + ey * ey + ez * ez
        f = jnp.maximum(1.0 - s, 0.0)
        e = jnp.exp2(s * (-0.5 * LOG2E))
        keep[0, c, :] = f
        keep[1, c, :] = e
        f = f * f
        if offset == (0, 0, 0):
            row = lax.broadcasted_iota(jnp.int32, (STEP, LANES), 0) + c.start
            lane = lax.broadcasted_iota(jnp.int32, (STEP, LANES), 1)
            f = jnp.where(row == lane, 0.0, f)
        for k in range(z.rad):
            if k == 0:
                w = e * f
                e = e * e
            elif k == 1:
                w = w * e
            else:
                e = e * e * e
                w = w * e
            weights[k].append(w.astype(jnp.bfloat16))
    return jnp.concatenate([part for parts in weights for part in parts], axis=0)


def grouped(values):
    return [values[i:i + GROUP] for i in range(0, len(values), GROUP)]


def staggered(tasks, first, second, lag):
    results = []
    for t in range(len(tasks) + lag):
        if t < len(tasks):
            results.append(first(*tasks[t]))
        if t >= lag:
            second(results[t - lag], *tasks[t - lag])


def pack_kernel(counts_hbm, positions_hbm, species_hbm, out, counts, positions, species, arrived):
    arguments = [(counts_hbm, counts), (positions_hbm, positions), (species_hbm, species)]
    copies = [pltpu.make_async_copy(a, b, arrived.at[i]) for i, (a, b) in enumerate(arguments)]
    for copy in copies:
        copy.start()
    for copy in copies:
        copy.wait()
    slots = out.shape[3]
    lane = lax.broadcasted_iota(jnp.int32, (1, slots), 1)
    for x in range(out.shape[0]):
        for y in range(out.shape[1]):
            row = positions[x, y, 0:1, :]
            for q in range(3):
                out[x, y, q:q + 1, :] = row[:, q * slots:(q + 1) * slots]
            marked = jnp.where(lane < counts[x, y], species[x, y, 0:1, :], -1)
            out[x, y, 3:4, :] = marked.astype(jnp.float32)


def near_kernel(
    z, near, embed_hbm, filters_hbm, w_up_hbm, w_energy_hbm,
    table, readout, emb_energy, onehot, anchors, sums, kept,
    emb_pad, stage, embed, filters, w_up, w_energy, arrived,
):
    nspec, width = embed.shape
    by = z.block[1]
    weights = [(embed_hbm, embed), (filters_hbm, filters), (w_up_hbm, w_up), (w_energy_hbm, w_energy)]
    copies = [pltpu.make_async_copy(a, b, arrived.at[i]) for i, (a, b) in enumerate(weights)]
    for copy in copies:
        copy.start()

    for x in range(z.nx):
        for y in range(by):
            for g in range(z.groups):
                place_onehot(z, near, x, y, g, onehot, (x * by + y) * z.groups + g)
    place_anchors(z, stage, [(near, ax + 1, y) for ax in range(z.nax) for y in range(by)], anchors)

    def message_at(ax, carry):
        totals = {}

        def weigh_some(y, some):
            weights = []
            for n in some:
                dx, dy, _ = z.offsets[n]
                keep = kept.at[ax * by + y, z.split_offsets(y + 1)[0].index(n)]
                spot = target(near, ax + 1 + dx, y + dy, z.offsets[n])
                weights.append(weigh(z, spot, anchors.at[ax * by + y], z.offsets[n], keep))
            return jnp.concatenate(weights, axis=1)

        def gather_some(weights, y, some):
            spots = [z.offsets[n] for n in some]
            hots = [onehot[((ax + 1 + dx) * by + y + dy) * z.groups + g] for dx, dy, g in spots]
            term = dot(weights, jnp.concatenate(hots, axis=1), NT)
            totals[y] = totals[y] + term if y in totals else term

        staggered([(y, some) for y in range(by) for some in grouped(z.split_offsets(y + 1)[0])], weigh_some, gather_some, LAG)
        for y in range(by):
            sums[ax * by + y] = totals[y]
        return carry

    lax.fori_loop(0, z.nax, message_at, 0)

    for copy in copies:
        copy.wait()
    emb_pad[...] = jnp.zeros_like(emb_pad)
    emb_pad[0:nspec, :] = embed[...].astype(jnp.float32)
    emb = emb_pad[...]
    rows = dot(emb.astype(jnp.bfloat16), filters[...], NN).astype(jnp.bfloat16)
    for k in range(z.rad):
        table[k * z.spec:(k + 1) * z.spec, :] = rows[:, k * width:(k + 1) * width]
    energy_row = jnp.broadcast_to(w_energy[...], (8, width))
    readout[...] = dot(energy_row, w_up[...].astype(jnp.float32), NT, lax.Precision.HIGHEST)
    emb_energy[...] = dot(energy_row, emb, NT, lax.Precision.HIGHEST)


class Store:
    def __init__(self, z, onehot_near, onehot_far, anchors_near, anchors_far, kept_near, kept_own, kept_far):
        self.z = z
        self.onehots = (onehot_near, onehot_far)
        self.anchors = (anchors_near, anchors_far)
        self.kept = (kept_near, kept_own, kept_far)
        self.outer = [y for y in range(z.ny) if not HALO <= y < HALO + z.block[1]]

    def onehot(self, x, y, g):
        z = self.z
        if y in self.outer:
            return self.onehots[1][(x * len(self.outer) + self.outer.index(y)) * z.groups + g]
        return self.onehots[0][(x * z.block[1] + y - HALO) * z.groups + g]

    def anchor(self, ax, ay):
        if self.z.inner(ay):
            return self.anchors[0].at[ax * self.z.block[1] + ay - 1]
        return self.anchors[1].at[ax * 2 + (ay > 0)]

    def radial(self, ax, ay, n):
        if not self.z.inner(ay):
            return self.kept[2].at[ax * 2 + (ay > 0), n]
        near, far = self.z.split_offsets(ay)
        if n in near:
            return self.kept[0].at[ax * self.z.block[1] + ay - 1, near.index(n)]
        return self.kept[1].at[ax * self.z.block[1] + ay - 1, far.index(n)]


def pairs(z, store, region, ax, ay, n, gains, r):
    c = z.rows[r]
    dx, dy, g = z.offsets[n]
    tx, ty, tz = target(region, ax + 1 + dx, ay + 1 + dy, z.offsets[n])
    anchor, keep = store.anchor(ax, ay), store.radial(ax, ay, n)
    ex = tx - anchor[0, c, :]
    ey = ty - anchor[1, c, :]
    ez = tz - anchor[2, c, :]
    shift = z.z_shift(g)
    ez = ez + jnp.where(ez > 0.0, -shift, shift) if z.merged else ez + shift
    f = keep[0, c, :]
    e = keep[1, c, :]
    e2 = e * e
    plain = None
    for k in range(z.rad):
        if k == 1:
            e = e * e2
        elif k > 1:
            e2 = e2 * e2 * e2
            e = e * e2
        term = e * gains[k * STEP:(k + 1) * STEP]
        scaled = (0.25 * 3.0 ** k) * term
        plain, steep = (term, scaled) if plain is None else (plain + term, steep + scaled)
    return f * (f * steep + plain), (ex, ey, ez)


def blocks(z, store, region, work, back):
    tasks = [
        (ax, ay, table, some[first:first + WIDE], sums)
        for ax, ay, table, some, sums in work for first in range(0, len(some), WIDE)
    ]

    def spots_of(ax, ay, part):
        return [(ax + 1 + z.offsets[n][0], ay + 1 + z.offsets[n][1], z.offsets[n][2]) for n in part]

    def multiply(ax, ay, table, part, sums):
        hots = jnp.concatenate([store.onehot(*spot) for spot in spots_of(ax, ay, part)], axis=1)
        return dot(table[...], jnp.concatenate([hots, hots], axis=0), NN)

    def add_forces(gains, ax, ay, table, part, sums):
        totals = [[None] * 3 for _ in part]
        for r in range(len(z.rows)):
            some_gains = gains[r * z.rad * STEP:(r + 1) * z.rad * STEP]
            for i, n in enumerate(part):
                p, displace = pairs(z, store, region, ax, ay, n, some_gains[:, i * LANES:(i + 1) * LANES], r)
                for q in range(3):
                    term = p * displace[q]
                    if sums is not None:
                        sums[q][r] = term if sums[q][r] is None else sums[q][r] + term
                    if back is not None:
                        term = sum(term[j:j + 8] for j in range(8, STEP, 8)) + term[0:8]
                        totals[i][q] = term if totals[i][q] is None else totals[i][q] + term
        if back is not None:
            for (x, y, g), total in zip(spots_of(ax, ay, part), totals):
                for q in range(3):
                    back[((x - HALO) * z.block[1] + y - HALO) * z.groups + g, q] += total[q]

    staggered(tasks, multiply, add_forces, LATER)


def far_kernel(
    z, region, table, readout_ref, onehot_near, anchors_near, sums_near, kept_near,
    other, part, mine, adj_own, act_own, onehot_far, kept_own,
    anchors_far, kept_far, stage, adj_table, back,
):
    by = z.block[1]
    bf = jnp.bfloat16
    slots, spec, rad = z.slots, z.spec, z.rad
    readout = readout_ref[...]
    store = Store(z, onehot_near, onehot_far, anchors_near, anchors_far, kept_near, kept_own, kept_far)
    outer = store.outer

    place_anchors(
        z, stage, [(region, ax + 1, y) for ax in range(z.nax) for y in (1, z.ny - HALO)], anchors_far
    )
    for x in range(z.nx):
        for i, y in enumerate(outer):
            for g in range(z.groups):
                place_onehot(z, region, x, y, g, onehot_far, (x * len(outer) + i) * z.groups + g)

    def message_at(ax):
        totals = {ay: sums_near[ax * by + ay - 1] for ay in range(z.nay) if z.inner(ay)}

        def weigh_some(ay, some):
            weights = []
            for n in some:
                dx, dy, _ = z.offsets[n]
                spot = target(region, ax + 1 + dx, ay + 1 + dy, z.offsets[n])
                weights.append(weigh(z, spot, store.anchor(ax, ay), z.offsets[n], store.radial(ax, ay, n)))
            return jnp.concatenate(weights, axis=1)

        def gather_some(weights, ay, some):
            spots = [z.offsets[n] for n in some]
            hots = [store.onehot(ax + 1 + dx, ay + 1 + dy, g) for dx, dy, g in spots]
            term = dot(weights, jnp.concatenate(hots, axis=1), NT)
            totals[ay] = totals[ay] + term if ay in totals else term

        staggered([(ay, some) for ay in range(z.nay) for some in grouped(z.split_offsets(ay)[1])], weigh_some, gather_some, LAG)
        return [
            jnp.concatenate(
                [totals[ay][k * slots:(k + 1) * slots].astype(bf) for k in range(rad)], axis=1
            ) for ay in range(z.nay)
        ]

    def adj_at(ax, ay):
        if 0 < ax < z.nax - 1 and z.inner(ay):
            return adj_own.at[(ax - 1) * by + ay - 1]
        return adj_table.at[ax * z.nay + ay]

    def adjoint_of(mixed, ax):
        group = [(ax, ay) for ay in range(z.nay)]
        messages = dot(jnp.concatenate(mixed, axis=0), table[...], NN)
        adjoints = []
        for i, spot in enumerate(group):
            message = MSG_SCALE * messages[i * slots:(i + 1) * slots]
            sigmoid = 1.0 / (1.0 + jnp.exp(-message))
            if z.cell(*spot) is not None:
                act_own[z.cell(*spot)] = (message * sigmoid).astype(bf)
            slope = sigmoid * (1.0 + message * (1.0 - sigmoid)) * readout[0:1]
            adjoints.append(jnp.where(store.anchor(*spot)[3] >= 0.0, slope, 0.0).astype(bf))
        turned = dot(jnp.concatenate(adjoints, axis=0), table[...], NT)
        for i, spot in enumerate(group):
            out = adj_at(*spot)
            for r, c in enumerate(z.rows):
                high, low = split(turned[slots * i + c.start:slots * i + c.stop])
                for k in range(rad):
                    at = slice((r * rad + k) * STEP, (r * rad + k + 1) * STEP)
                    out[at, 0:spec] = high[:, k * spec:(k + 1) * spec]
                    out[at, spec:] = low[:, k * spec:(k + 1) * spec]

    staggered([(ax,) for ax in range(z.nax)], message_at, adjoint_of, BEHIND)

    back[...] = jnp.zeros_like(back)

    work = []
    for ax in range(z.nax):
        for ay in range(z.nay):
            some = [n for n, (dx, dy, _) in enumerate(z.offsets) if z.cell(ax + dx, ay + dy) is not None]
            sums = None if z.cell(ax, ay) is None else [[None] * len(z.rows) for _ in range(3)]
            work.append((ax, ay, adj_at(ax, ay), some, sums))
    blocks(z, store, region, work, back)
    for ax, ay, _, _, sums in work:
        if sums is not None:
            for q in range(3):
                for r, c in enumerate(z.rows):
                    mine[z.cell(ax, ay), q, c, :] = sums[q][r]

    for ox in range(z.block[0]):
        for oy in range(by):
            for g in range(z.groups):
                start = slots if g == 0 else 0
                for q in range(3):
                    row = FORCE_SCALE * jnp.sum(back[(ox * by + oy) * z.groups + g, q], axis=0, keepdims=True)
                    other[g, ox, oy, :, q * slots:(q + 1) * slots] = row[:, start:start + slots]
                    if g == 0:
                        part[ox, oy, :, q * slots:(q + 1) * slots] = row[:, 0:slots]


def own_kernel(
    z, region, readout, emb_energy, onehot_near, anchors_near, kept_near,
    part, mine_part, adj_own, act_own, onehot_far, kept_own,
    energies, own, mine,
):
    slots = z.slots
    store = Store(z, onehot_near, onehot_far, anchors_near, None, kept_near, kept_own, None)
    cells = [(ox, oy) for ox in range(z.block[0]) for oy in range(z.block[1])]
    hots = jnp.concatenate([store.onehot(ox + HALO, oy + HALO, 0)[:, 0:slots] for ox, oy in cells], axis=1)
    acts = jnp.concatenate([act_own[o] for o in range(len(cells))], axis=0)
    energy = dot(thirds(emb_energy[...]), hots, NN) + dot(thirds(readout[...]), acts, NT)
    energy = jnp.sum(energy, axis=0, keepdims=True)
    for o, (ox, oy) in enumerate(cells):
        marked = region[ox + HALO, oy + HALO, 3:4, 0:slots]
        energies[ox, oy, :, :] = jnp.where(marked >= 0.0, energy[:, o * slots:(o + 1) * slots], 0.0)

    work = []
    for o, (ox, oy) in enumerate(cells):
        some = [n for n, (dx, dy, _) in enumerate(z.offsets) if z.cell(ox + 1 + dx, oy + 1 + dy) is None]
        sums = [[mine_part[o, q, c, :] for c in z.rows] for q in range(3)]
        work.append((ox + 1, oy + 1, adj_own.at[o], some, sums))
    blocks(z, store, region, work, None)
    for o, (_, _, _, _, sums) in enumerate(work):
        for q in range(3):
            for r, c in enumerate(z.rows):
                mine[o, q, c, :] = sums[q][r]

    high, low = split(mine[...].reshape(len(cells) * 3 * slots, LANES))
    ones = jnp.ones((8, 2 * LANES), jnp.bfloat16)
    rows = dot(ones, jnp.concatenate([high, low], axis=1), NT)[0:1]
    for o, (ox, oy) in enumerate(cells):
        for q in range(3):
            at = (o * 3 + q) * slots
            lanes = slice(q * slots, (q + 1) * slots)
            own[ox, oy, :, lanes] = part[ox, oy, :, lanes] - FORCE_SCALE * rows[:, at:at + slots]


VMEM = pl.BlockSpec(memory_space=pltpu.VMEM)
HBM = pl.BlockSpec(memory_space=pltpu.HBM)


def in_hbm(*arrays):
    return [pltpu.with_memory_space_constraint(array, pltpu.HBM) for array in arrays]


def pack(positions, species, counts):
    bx, by, _, slots = species.shape
    return pl.pallas_call(
        pack_kernel,
        out_shape=jax.ShapeDtypeStruct((bx, by, 4, slots), jnp.float32),
        in_specs=[HBM] * 3,
        out_specs=VMEM,
        scratch_shapes=[
            pltpu.SMEM(counts.shape, counts.dtype),
            pltpu.VMEM(positions.shape, positions.dtype),
            pltpu.VMEM(species.shape, species.dtype),
            pltpu.SemaphoreType.DMA((3,)),
        ],
        compiler_params=pltpu.CompilerParams(vmem_limit_bytes=1024 * 1024),
    )(*in_hbm(counts, positions, species))


def near_layer(z, near, embed, filters, w_up, w_energy):
    width = embed.shape[1]
    by = z.block[1]
    cells, most = z.nax * by, max(len(z.split_offsets(y + 1)[0]) for y in range(by))
    shapes = [
        ((z.rad * z.spec, width), jnp.bfloat16),
        ((8, width), jnp.float32),
        ((8, z.spec), jnp.float32),
        ((z.nx * by * z.groups, z.spec, LANES), jnp.bfloat16),
        ((cells, 4, z.slots, LANES), jnp.float32),
        ((cells, z.rad * z.slots, z.spec), jnp.float32),
        ((cells, most, 2, z.slots, LANES), jnp.float32),
    ]
    flops = 2 * cells * most * z.rad * z.slots * LANES * z.spec
    return pl.pallas_call(
        functools.partial(near_kernel, z),
        out_shape=[jax.ShapeDtypeStruct(*shape) for shape in shapes],
        in_specs=[VMEM] + [HBM] * 4,
        out_specs=[VMEM] * len(shapes),
        scratch_shapes=[
            pltpu.VMEM((z.spec, width), jnp.float32),
            pltpu.VMEM((4, LANES, LANES), jnp.float32),
            pltpu.VMEM(embed.shape, embed.dtype),
            pltpu.VMEM(filters.shape, filters.dtype),
            pltpu.VMEM(w_up.shape, w_up.dtype),
            pltpu.VMEM(w_energy.shape, w_energy.dtype),
            pltpu.SemaphoreType.DMA((4,)),
        ],
        compiler_params=pltpu.CompilerParams(vmem_limit_bytes=12 * 1024 * 1024),
        cost_estimate=pl.CostEstimate(flops=flops, bytes_accessed=1 << 20, transcendentals=0),
    )(near, *in_hbm(embed, filters, w_up, w_energy))


def call(kernel, z, shapes, scratch, limit, operands):
    return pl.pallas_call(
        functools.partial(kernel, z),
        out_shape=[jax.ShapeDtypeStruct(*shape) for shape in shapes],
        in_specs=[VMEM] * len(operands),
        out_specs=[VMEM] * len(shapes),
        scratch_shapes=[pltpu.VMEM(*shape) for shape in scratch],
        compiler_params=pltpu.CompilerParams(vmem_limit_bytes=limit),
    )(*operands)


def far_layer(z, region, near):
    table, readout, emb_energy, onehot, anchors, sums, kept = near
    width = table.shape[1]
    cells, ring = z.block[0] * z.block[1], z.nax * z.nay
    offsets, most = len(z.offsets), max(len(z.split_offsets(y + 1)[1]) for y in range(z.block[1]))
    pair = (2, z.slots, LANES)
    shapes = [
        ((z.groups,) + z.block + (1, 3 * z.slots), jnp.float32),
        (z.block + (1, 3 * z.slots), jnp.float32),
        ((cells, 3, z.slots, LANES), jnp.float32),
        ((cells, z.rad * z.slots, 2 * z.spec), jnp.bfloat16),
        ((cells, z.slots, width), jnp.bfloat16),
        ((z.nx * 2 * HALO * z.groups, z.spec, LANES), jnp.bfloat16),
        ((z.nax * z.block[1], most) + pair, jnp.float32),
    ]
    scratch = [
        ((z.nax * 2, 4, z.slots, LANES), jnp.float32),
        ((z.nax * 2, offsets) + pair, jnp.float32),
        ((4, LANES, LANES), jnp.float32),
        ((ring, z.rad * z.slots, 2 * z.spec), jnp.bfloat16),
        ((cells * z.groups, 3, 8, LANES), jnp.float32),
    ]
    operands = (region, table, readout, onehot, anchors, sums, kept)
    return call(far_kernel, z, shapes, scratch, FAR_VMEM, operands)


def own_layer(z, region, near, far):
    table, readout, emb_energy, onehot, anchors, sums, kept = near
    shapes = [
        (z.block + (1, z.slots), jnp.float32),
        (z.block + (1, 3 * z.slots), jnp.float32),
    ]
    scratch = [((z.block[0] * z.block[1], 3, z.slots, LANES), jnp.float32)]
    operands = (region, readout, emb_energy, onehot, anchors, kept) + tuple(far)
    return call(own_kernel, z, shapes, scratch, OWN_VMEM, operands)


def on_device(positions, species, counts, embed, filters, w_up, w_energy):
    bx, by = positions.shape[:2]
    slots = species.shape[-1]
    width = embed.shape[1]
    depth = lax.axis_size("gz")
    merged = depth * positions.shape[2] == 2
    spec = -(-embed.shape[0] // LANES) * LANES
    z = Cells((bx, by), merged, filters.shape[1] // width, spec, slots)
    block = pack(positions, species, counts.reshape(bx, by))
    upward = [(i, (i + 1) % depth) for i in range(depth)]
    downward = [(b, a) for a, b in upward]
    low = lax.ppermute(block, "gz", upward)
    if merged:
        block = jnp.concatenate([block, low], axis=3)
    else:
        high = lax.ppermute(block, "gz", downward)
        empty = jnp.full_like(block, -1.0)
        block = jnp.concatenate(
            [jnp.concatenate([block, low], axis=3), jnp.concatenate([high, empty], axis=3)], axis=2
        )
    block = exchange(block, "gx", 0, HALO)
    near = near_layer(z, block, embed, filters, w_up, w_energy.reshape(1, width))
    region = exchange(block, "gy", 1, HALO)
    other, *far = far_layer(z, region, near)
    energies, own = own_layer(z, region, near, far)

    forces = own + lax.ppermute(other[0], "gz", downward)
    if not merged:
        forces = forces + lax.ppermute(other[1], "gz", upward)
    return energies, forces


def solution(mesh):
    in_specs = (
        P("gx", "gy", "gz", None),
        P("gx", "gy", "gz", None),
        P("gx", "gy", "gz"),
        P(),
        P(),
        P(),
        P(),
    )
    out_specs = (P("gx", "gy", "gz", None), P("gx", "gy", "gz", None))
    return jax.shard_map(
        on_device, mesh=mesh, in_specs=in_specs, out_specs=out_specs, check_vma=False
    )
```
